128 devices in a mesh: seq: 64 (over z, y, x), head: 2 (over core), dp: 1.
Axes of the slice: x: 4, y: 4, z: 4, core: 2. Of those that a mesh axis runs over, the one named last changes fastest.
Arguments:
- tokens: bfloat16 [16384, 3072], P(('dp', 'seq'), 'head'), may hold values from -22 to 22
- clip_id: int32 [16384], P(('dp', 'seq')), may hold values from 0 to 2, never falling along the last dimension, each value on 1 to 10240 neighbouring positions
- w_qkv: bfloat16 [3, 3072, 1536], P(None, None, 'head'), may hold values from -0.109375 to 0.109375
- w_out: bfloat16 [1536, 3072], P('head'), may hold values from -0.15625 to 0.15625
Outputs:
- output_rows: bfloat16 [16384, 3072], P(('dp', 'seq'), 'head')
The draws below stay inside these ranges and needn't reach their ends.
Inputs may be any that keep to these rules, and one draw needn't show every extreme that they name: `clip_id`: clip numbers never fall along the rows; each clip holds 1 to 10240 rows and one holds exactly 10240.
All inputs are finite; a program needn't handle non-finite values.
Results may differ from the reference program's by a relative error of at most 0.015.
Values may be sent and summed in bfloat16 or wider, within the bound.
No kernel may reach another device: no remote copies, remote signals or barrier semaphores. Data moves between devices by JAX's collectives and lax.ppermute only.
A program may use at most 192 MiB of HBM per device.

```python
import math
import jax
import jax.numpy as jnp
import numpy as np
from jax import lax

D = 3072
HEAD_DIM = 128
HEADS = 12
TOK_SEQ = 256
CLIPS = 3
TOKENS = 16384
MAXCLIP = 10240


def draw_tokens(key, part):
    key = jax.random.fold_in(key, 11)
    first_key = jax.random.fold_in(key, 0)
    return jnp.clip(jax.random.normal(first_key, (TOKENS, D), jnp.float32), -6.0, 6.0).astype(jnp.bfloat16)


def level_of(own_key, shape, cuts, smallest, top_value):
    gain, own = 1.0, jax.random.fold_in(own_key, 6)
    for position, blocks in cuts:
        steps = jnp.exp(jax.random.uniform(jax.random.fold_in(own, position), (blocks,), jnp.float32, smallest / len(cuts), top_value / len(cuts)))
        gain = gain * jnp.repeat(steps, shape[position] // blocks).reshape([-1 if axis == position else 1 for axis in range(len(shape))])
    return gain


def split_up(amount, total, limit, lean):
    loads = [(1 << 20) // math.isqrt(grade ** lean) + 1 for grade in range(2, amount + 1)]
    surplus, holding = total - limit - (amount - 1), [1] * (amount - 1)
    while surplus > 0:
        free = [i for i in range(amount - 1) if holding[i] < limit]
        mass, left = sum([loads[i] for i in free]), surplus
        for i in free:
            more = min(limit - holding[i], max(1, left * loads[i] // mass), surplus)
            holding[i] = holding[i] + more
            surplus = surplus - more
    return np.array([limit] + holding)


def ragged(own_key, number_of, total, bound, skew):
    if number_of == 2:
        one = jax.random.randint(own_key, (), max(1, total - bound), min(bound, total - 1) + 1)
        return jnp.stack([one, total - one])
    sizes = jnp.asarray(split_up(number_of, total, bound, skew), jnp.int32)
    couples = (number_of - 1) // 2
    giver, taker = sizes[1:1 + 2 * couples:2], sizes[2:2 + 2 * couples:2]
    slack = jnp.minimum(giver - 1, bound - taker)
    passed = jax.random.randint(jax.random.fold_in(own_key, 1), (couples,), 0, 1 << 20) % (slack + 1)
    sizes = sizes.at[1:1 + 2 * couples:2].set(giver - passed).at[2:2 + 2 * couples:2].set(taker + passed)
    return sizes[jax.random.permutation(jax.random.fold_in(own_key, 2), number_of)]


def normal_values(key, dims, width, most, shards=(), held_as=jnp.bfloat16):
    drawn = jax.random.normal(key, dims, jnp.float32) * width
    if len(shards) > 0:
        drawn = level_of(key, dims, shards, -0.22, 0.18) * drawn
    return jnp.clip(drawn, min=-most, max=most).astype(held_as)


def setup_inputs(seed: int = 0, part: int = 0) -> dict:
    streams_of = jax.random.split(jax.random.key(seed), 5)
    part_keys = jax.random.split(jax.random.fold_in(streams_of[4], part), 5)
    tokens = draw_tokens(jax.random.fold_in(jax.random.fold_in(streams_of[4], part), 71), part)
    clip_id = jnp.searchsorted(jnp.cumsum(ragged(part_keys[1], CLIPS, TOKENS, MAXCLIP, 0)), jnp.arange(TOKENS), side="right").astype(jnp.int32)
    w_qkv = normal_values(streams_of[2], (3, D, HEADS * HEAD_DIM), D ** -0.5, 0.109375, ((2, 2),))
    w_out = normal_values(streams_of[3], (HEADS * HEAD_DIM, D), (HEADS * HEAD_DIM) ** -0.5, 0.15625, ((0, 2),))
    return {"tokens": tokens, "clip_id": clip_id, "w_qkv": w_qkv, "w_out": w_out}


def reference(tokens, clip_id, w_qkv, w_out):
    score_scale = 1.0 / math.sqrt(HEAD_DIM)
    projected = [jnp.dot(tokens, w_qkv[matrix_index], preferred_element_type=jnp.float32).astype(jnp.bfloat16) for matrix_index in range(3)]
    queries, keys, values = [matrix.reshape(TOKENS, HEADS, HEAD_DIM).transpose(1, 0, 2) for matrix in projected]
    block_count = TOKENS // TOK_SEQ

    def per_head(operands):
        head_queries, head_keys, head_values = operands
        query_blocks = head_queries.reshape(block_count, TOK_SEQ, HEAD_DIM)
        clip_blocks = clip_id.reshape(block_count, TOK_SEQ)

        def per_block(inputs):
            query_part, clip_part = inputs
            scores = jnp.dot(query_part, head_keys.T, preferred_element_type=jnp.float32) * score_scale
            allowed = clip_part[:, None] == clip_id[None, :]
            scores = jnp.where(allowed, scores, -1e+30)
            highest = lax.optimization_barrier(jnp.max(scores, axis=-1, keepdims=True))
            weights = jnp.where(allowed, jnp.exp(scores - highest), 0.0)
            totals = lax.optimization_barrier(jnp.sum(weights, axis=-1, keepdims=True))
            summed = jnp.dot(weights.astype(jnp.bfloat16), head_values, preferred_element_type=jnp.float32)
            return (summed / totals).astype(jnp.bfloat16)
        return lax.map(per_block, (query_blocks, clip_blocks)).reshape(TOKENS, HEAD_DIM)
    head_results = lax.map(per_head, (queries, keys, values))
    attended = head_results.transpose(1, 0, 2).reshape(TOKENS, HEADS * HEAD_DIM)
    return jnp.dot(attended, w_out, preferred_element_type=jnp.float32).astype(jnp.bfloat16)
```

```python
import functools
import math

import jax
import jax.numpy as jnp
from jax import lax
from jax.experimental import pallas as pl
from jax.experimental.pallas import tpu as pltpu
from jax.sharding import Mesh
from jax.sharding import PartitionSpec as P

HEAD_DIM = 128
CHUNK = 1024
SEG = 128
NEG = -1e30
FLOOR = -1e29


def attend_kernel(info, q_ref, kv_ref, o_ref, keys, vals, scores):
    b1, b2, zl, y, x, c = [info[n] for n in range(6)]

    for zz in range(4):
        for cc in range(2):
            slot = ((zz & 1) ^ zl) * 2 + ((zz >> 1) ^ cc)
            for yy in range(4):
                at = ((zz * 4 + yy) * 2 + cc) * SEG
                keys[at : at + SEG, :] = kv_ref[yy * 2 + cc, slot, 0]
                vals[at : at + SEG, :HEAD_DIM] = kv_ref[yy * 2 + cc, slot, 1]
    vals[:, HEAD_DIM:] = jnp.ones((4096, HEAD_DIM), jnp.bfloat16)

    def below(bound):
        return (bound // 1024) * 256 + jnp.clip(bound % 1024 - x * 256, 0, 256)

    n1, n2 = below(b1), below(b2)
    row = lax.broadcasted_iota(jnp.int32, (256, 1), 0)
    eye = (
        lax.broadcasted_iota(jnp.int32, (SEG, SEG), 0)
        == lax.broadcasted_iota(jnp.int32, (SEG, SEG), 1)
    ).astype(jnp.float32)

    def lower(pos):
        return jnp.where(pos >= b2, n2, jnp.where(pos >= b1, n1, 0))

    def upper(pos):
        return jnp.where(pos >= b2, 4096, jnp.where(pos >= b1, n2, n1))

    def tile(t, carry):
        zz, xp = t // 2, t % 2
        slot = ((zz & 1) ^ zl) * 2 + ((zz >> 1) ^ c)
        q = jnp.concatenate([q_ref[2 * xp, slot], q_ref[2 * xp + 1, slot]], axis=0)
        first = zz * 4096 + y * 1024 + xp * 512 + c * 128
        last = first + 256 + 127
        pos = first + row + jnp.where(row >= SEG, SEG, 0)
        low_row, high_row = lower(pos), upper(pos)
        low_all, high_all = lower(first), upper(last)
        low_in, high_in = lower(last), upper(first)
        start = (low_all // 256) * 256
        count = (high_all - start + CHUNK - 1) // CHUNK
        start = pl.multiple_of(jnp.minimum(start, 4096 - count * CHUNK), 256)

        def first_pass(i, top):
            at = pl.multiple_of(start + i * CHUNK, 256)
            s = lax.dot_general(
                q, keys[pl.ds(at, CHUNK), :], (((1,), (1,)), ((), ())), preferred_element_type=jnp.float32
            )

            def masked():
                index = at + lax.broadcasted_iota(jnp.int32, (256, CHUNK), 1)
                return jnp.where((index >= low_row) & (index < high_row), s, NEG)

            s = lax.cond((at >= low_in) & (at + CHUNK <= high_in), lambda: s, masked)
            scores[i] = s
            for n in range(CHUNK // 128):
                top = jnp.maximum(top, s[:, n * 128 : (n + 1) * 128])
            return top

        top = lax.fori_loop(0, count, first_pass, jnp.full((256, 128), NEG, jnp.float32))
        top = jnp.maximum(jnp.max(top, axis=1, keepdims=True), FLOOR)

        def second_pass(i, acc):
            at = pl.multiple_of(start + i * CHUNK, 256)
            weights = jnp.exp(scores[i] - top).astype(jnp.bfloat16)
            return acc + jnp.dot(weights, vals[pl.ds(at, CHUNK), :], preferred_element_type=jnp.float32)

        acc = lax.fori_loop(0, count, second_pass, jnp.zeros((256, 256), jnp.float32))
        total = jnp.maximum(acc[:, HEAD_DIM:], 1e-30)
        out = (acc[:, :HEAD_DIM] / total).astype(jnp.bfloat16)
        level = top + jnp.log(total)
        for half in range(2):
            rel = (2 * xp + half - x + 4) % 4
            o_ref[rel, slot] = out[half * SEG : (half + 1) * SEG]
            line = jnp.sum(level[half * SEG : (half + 1) * SEG] * eye, axis=0, keepdims=True)
            high = line.astype(jnp.bfloat16).astype(jnp.float32)
            middle = (line - high).astype(jnp.bfloat16).astype(jnp.float32)
            rest = line - high - middle
            sub = lax.broadcasted_iota(jnp.int32, (16, 128), 0)
            parts = jnp.where(sub == 0, high, jnp.where(sub == 1, middle, jnp.where(sub == 2, rest, 0.0)))
            o_ref[rel, 4, pl.ds(pl.multiple_of(slot * 16, 16), 16), :] = parts.astype(jnp.bfloat16)
        return carry

    lax.fori_loop(0, 8, tile, 0)


def attend(info, q, kv):
    return pl.pallas_call(
        attend_kernel,
        out_shape=jax.ShapeDtypeStruct((4, 5, SEG, HEAD_DIM), jnp.bfloat16),
        in_specs=[
            pl.BlockSpec(memory_space=pltpu.SMEM),
            pl.BlockSpec(memory_space=pltpu.VMEM),
            pl.BlockSpec(memory_space=pltpu.VMEM),
        ],
        out_specs=pl.BlockSpec(memory_space=pltpu.VMEM),
        scratch_shapes=[
            pltpu.VMEM((4096, HEAD_DIM), jnp.bfloat16),
            pltpu.VMEM((4096, 2 * HEAD_DIM), jnp.bfloat16),
            pltpu.VMEM((4096 // CHUNK, 256, CHUNK), jnp.float32),
        ],
        compiler_params=pltpu.CompilerParams(vmem_limit_bytes=40 << 20),
        cost_estimate=pl.CostEstimate(
            flops=2 * 2 * 2048 * 4096 * 128 * 2, bytes_accessed=4 << 20, transcendentals=2048 * 4096
        ),
    )(info, q, kv)


def combine_kernel(*refs):
    out_ref = refs[-1]
    eye = (
        lax.broadcasted_iota(jnp.int32, (SEG, SEG), 0)
        == lax.broadcasted_iota(jnp.int32, (SEG, SEG), 1)
    ).astype(jnp.float32)
    for head in range(3):
        parts = refs[4 * head : 4 * head + 4]
        for slot in range(4):
            levels = []
            for part in parts:
                lines = part[4, slot * 16 : (slot + 1) * 16, :].astype(jnp.float32)
                levels.append(jnp.sum(lines, axis=0, keepdims=True))
            top = functools.reduce(jnp.maximum, levels)
            shares = [jnp.exp(level - top) for level in levels]
            total = functools.reduce(jnp.add, shares)
            spread = jnp.concatenate([eye * (share / total) for share in shares], axis=1)
            stacked = jnp.concatenate([part[slot] for part in parts], axis=0)
            mixed = jnp.dot(spread.astype(jnp.bfloat16), stacked, preferred_element_type=jnp.float32)
            out_ref[slot, :, head * HEAD_DIM : (head + 1) * HEAD_DIM] = mixed.astype(jnp.bfloat16)


def combine(blocks):
    return pl.pallas_call(
        combine_kernel,
        out_shape=jax.ShapeDtypeStruct((4, SEG, 3 * HEAD_DIM), jnp.bfloat16),
        in_specs=[pl.BlockSpec(memory_space=pltpu.VMEM)] * len(blocks),
        out_specs=pl.BlockSpec(memory_space=pltpu.VMEM),
        compiler_params=pltpu.CompilerParams(vmem_limit_bytes=32 << 20),
    )(*blocks)


SLOTS = [(a, b) for a in range(2) for b in range(2)]


def spread_pairs(a, b):
    pairs = []
    for z in range(4):
        for c in range(2):
            target = (2 * c + ((z % 2) ^ a)) * 2 + ((z // 2) ^ b)
            pairs.append((z * 2 + c, target))
    return pairs


def body(tokens, clip_id, w_qkv, w_out):
    z, y, x, c = [lax.axis_index(name) for name in ("z", "y", "x", "core")]
    zl, zh = z % 2, z // 2
    swap = [(0, 1), (1, 0)]

    counts = jnp.stack([jnp.sum(clip_id < 1), jnp.sum(clip_id < 2)]).astype(jnp.int32)
    bounds = lax.psum(counts, ("z", "y", "x"))
    info = jnp.concatenate([bounds, jnp.stack([zl, y, x, c]).astype(jnp.int32)])

    other = lax.ppermute(tokens, "core", swap)
    both = jnp.where(c == 0, jnp.concatenate([tokens, other], 1), jnp.concatenate([other, tokens], 1))
    stacked = jnp.einsum("td,sdc->stc", both, w_qkv, preferred_element_type=jnp.float32)
    scale = jnp.array([1.0 / math.sqrt(HEAD_DIM), 1.0, 1.0], jnp.float32)[:, None, None]
    stacked = (stacked * scale).astype(jnp.bfloat16)

    arrived = []
    for a, b in SLOTS:
        block = lax.dynamic_slice(stacked, (0, (zh ^ b) * SEG, (zl ^ a) * 384), (3, SEG, 384))
        arrived.append(lax.ppermute(block, ("z", "core"), spread_pairs(a, b)))

    results = []
    for head in range(3):
        cols = slice(head * HEAD_DIM, (head + 1) * HEAD_DIM)
        own_kv = jnp.stack([block[1:, :, cols] for block in arrived])
        own_q = jnp.stack([block[0, :, cols] for block in arrived])
        kv = lax.all_gather(own_kv, ("y", "core"), axis=0)
        q = lax.all_gather(own_q, "x", axis=0)
        out = attend(info, q, kv)
        results.append(out[0])
        for step in (1, 2, 3):
            results.append(lax.ppermute(out[step], "x", [(n, (n + step) % 4) for n in range(4)]))
    mixed = combine(results)

    back = []
    for index, (a, b) in enumerate(SLOTS):
        pairs = [(target, source) for source, target in spread_pairs(a, b)]
        back.append(lax.ppermute(mixed[index], ("z", "core"), pairs))
    rows = []
    for half in range(2):
        by_a = [jnp.where(zh == half, back[2 * a], back[2 * a + 1]) for a in range(2)]
        rows.append(
            jnp.concatenate([jnp.where(zl == 0, by_a[0], by_a[1]), jnp.where(zl == 0, by_a[1], by_a[0])], 1)
        )
    attended = jnp.concatenate(rows, axis=0)
    half_cols = w_out.shape[1] // 2
    w_there = lax.dynamic_slice(w_out, (0, (1 - c) * half_cols), (w_out.shape[0], half_cols))
    w_here = lax.dynamic_slice(w_out, (0, c * half_cols), (w_out.shape[0], half_cols))
    there = jnp.dot(attended, w_there, preferred_element_type=jnp.float32).astype(jnp.bfloat16)
    received = lax.ppermute(there, "core", swap)
    here = jnp.dot(attended, w_here, preferred_element_type=jnp.float32)
    return (here + received.astype(jnp.float32)).astype(jnp.bfloat16)


def solution(mesh):
    fine = Mesh(mesh.devices.reshape(4, 4, 4, 2), ("z", "y", "x", "core"))
    seq = ("z", "y", "x")
    in_specs = (P(seq, "core"), P(seq), P(None, None, "core"), P("core", None))
    return jax.shard_map(body, mesh=fine, in_specs=in_specs, out_specs=P(seq, "core"), check_vma=False)
```

```python
import functools
import math

import jax
import jax.numpy as jnp
from jax import lax
from jax.experimental import pallas as pl
from jax.experimental.pallas import tpu as pltpu
from jax.sharding import Mesh
from jax.sharding import PartitionSpec as P

HEAD_DIM = 128
SEG = 128
TILE = 512
KEYS = 4096
NEG = -1e30
FLOOR = -1e29
WIDTHS = (768, 1536, 2048, 2688, 3328, 4096)
SLOTS = [(a, b) for a in range(2) for b in range(2)]
VMEM = pl.BlockSpec(memory_space=pltpu.VMEM)
SMEM = pl.BlockSpec(memory_space=pltpu.SMEM)


def prepare_kernel(*refs):
    blocks, (q_ref, *kv_refs) = refs[:4], refs[4:]
    for slot, block in enumerate(blocks):
        q_ref[slot * SEG : (slot + 1) * SEG, :] = block[:SEG, :]
        for head, kv_ref in enumerate(kv_refs):
            cols = slice(head * HEAD_DIM, (head + 1) * HEAD_DIM)
            kv_ref[slot * 2 * SEG : (slot + 1) * 2 * SEG, :] = block[SEG : 3 * SEG, cols]
    sub = lax.broadcasted_iota(jnp.int32, (16, 3 * HEAD_DIM), 0)
    counts = jnp.zeros((16, 3 * HEAD_DIM), jnp.float32)
    for slot, block in enumerate(blocks):
        counts = jnp.where(sub == slot, block[3 * SEG : 3 * SEG + 1, :].astype(jnp.float32), counts)
    q_ref[4 * SEG :, :] = counts.astype(jnp.bfloat16)
    for kv_ref in kv_refs:
        kv_ref[8 * SEG :, :] = counts[:, :HEAD_DIM].astype(jnp.bfloat16)


def prepare(blocks):
    shapes = [(4 * SEG + 16, 3 * HEAD_DIM)] + [(8 * SEG + 16, HEAD_DIM)] * 3
    return pl.pallas_call(
        prepare_kernel,
        out_shape=[jax.ShapeDtypeStruct(shape, jnp.bfloat16) for shape in shapes],
        in_specs=[VMEM] * 4,
        out_specs=[VMEM] * 4,
        compiler_params=pltpu.CompilerParams(vmem_limit_bytes=32 << 20),
    )(*blocks)


def attend_kernel(head, info, *refs):
    q_refs, kv_refs, o_refs = refs[:4], refs[4:12], refs[12:16]
    queries, keys, vals, scores, tops, sums, flat = refs[16:]
    zl, y, x, c = [info[n] for n in range(4)]
    lane = lax.broadcasted_iota(jnp.int32, (SEG, HEAD_DIM), 1)
    row = lax.broadcasted_iota(jnp.int32, (SEG, HEAD_DIM), 0)

    def bounds(lines):
        found = sum(line.astype(jnp.float32) for line in lines)
        return [
            jnp.sum(jnp.where(lane[:16] == n, found, 0.0), keepdims=True)[0, 0].astype(jnp.int32)
            for n in range(2)
        ]

    n1, n2 = bounds([ref[8 * SEG :, :] for ref in kv_refs])
    m1, m2 = bounds([ref[4 * SEG :, :HEAD_DIM] for ref in q_refs])

    def clip_of(index, first, second):
        return (index >= first).astype(jnp.int32) + (index >= second).astype(jnp.int32)

    for n in range(KEYS // SEG):
        own = clip_of(row + n * SEG, n1, n2) == lane
        keys[n * SEG : (n + 1) * SEG, HEAD_DIM:] = own.astype(jnp.float32).astype(jnp.bfloat16)
    for n in range(2048 // SEG):
        differs = (clip_of(row + n * SEG, m1, m2) != lane) & (lane < 3)
        queries[n * SEG : (n + 1) * SEG, HEAD_DIM:] = jnp.where(differs, NEG, 0.0).astype(jnp.bfloat16)
    vals[:, HEAD_DIM:] = jnp.ones((KEYS, HEAD_DIM), jnp.bfloat16)
    for slot, (a, b) in enumerate(SLOTS):
        for step in range(4):
            zz = 2 * (c ^ b) + (zl ^ a)
            at = pl.multiple_of((zz * 4 + ((x - step) & 3)) * SEG, SEG)
            cols = slice(head * HEAD_DIM, (head + 1) * HEAD_DIM)
            queries[pl.ds(at, SEG), :HEAD_DIM] = q_refs[step][slot * SEG : (slot + 1) * SEG, cols]
            for far in range(2):
                cc = c ^ far
                zz = 2 * (cc ^ b) + (zl ^ a)
                at = pl.multiple_of(((zz * 4 + ((y - step) & 3)) * 2 + cc) * SEG, SEG)
                block = kv_refs[far * 4 + step]
                keys[pl.ds(at, SEG), :HEAD_DIM] = block[slot * 2 * SEG : slot * 2 * SEG + SEG, :]
                vals[pl.ds(at, SEG), :HEAD_DIM] = block[slot * 2 * SEG + SEG : (slot + 1) * 2 * SEG, :]

    eye = (lane == row).astype(jnp.float32)

    def tile(zz, carry):
        first, last = zz * TILE, zz * TILE + TILE - 1
        low = jnp.where(first >= m2, n2, jnp.where(first >= m1, n1, 0))
        high = jnp.where(last >= m2, KEYS, jnp.where(last >= m1, n2, n1))
        low = (low // SEG) * SEG
        need = high - low
        rows = pl.ds(pl.multiple_of(first, TILE), TILE)
        tops[...] = jnp.full((TILE, HEAD_DIM), NEG, jnp.float32)
        sums[...] = jnp.zeros((TILE, 2 * HEAD_DIM), jnp.float32)

        def runs(k):
            under = WIDTHS[k - 1] if k else 0
            return ((need > under) & (need <= WIDTHS[k])).astype(jnp.int32)

        for k, width in enumerate(WIDTHS):
            at = pl.multiple_of(jnp.minimum(low, KEYS - width), SEG)

            def first_pass(i, carry, width=width, at=at):
                s = lax.dot_general(
                    queries[rows, :],
                    keys[pl.ds(at, width), :],
                    (((1,), (1,)), ((), ())),
                    preferred_element_type=jnp.float32,
                )
                scores[:, :width] = s
                top = s[:, :128]
                for n in range(1, width // 128):
                    top = jnp.maximum(top, s[:, n * 128 : (n + 1) * 128])
                tops[...] = top
                return carry

            lax.fori_loop(0, runs(k), first_pass, 0)

        top = jnp.maximum(jnp.max(tops[...], axis=1, keepdims=True), FLOOR)

        for k, width in enumerate(WIDTHS):
            at = pl.multiple_of(jnp.minimum(low, KEYS - width), SEG)

            def second_pass(i, carry, width=width, at=at):
                weights = jnp.exp(scores[:, :width] - top).astype(jnp.bfloat16)
                sums[...] = jnp.dot(weights, vals[pl.ds(at, width), :], preferred_element_type=jnp.float32)
                return carry

            lax.fori_loop(0, runs(k), second_pass, 0)

        total = jnp.maximum(sums[:, HEAD_DIM:], 1e-30)
        flat[...] = (sums[:, :HEAD_DIM] / total).astype(jnp.bfloat16)
        tops[...] = top + jnp.log(total)
        slot = ((zz & 1) ^ zl) * 2 + ((zz >> 1) ^ c)
        for step in range(4):
            at = pl.multiple_of(((x + step) & 3) * SEG, SEG)
            o_refs[step][pl.ds(pl.multiple_of(slot * SEG, SEG), SEG), :] = flat[pl.ds(at, SEG), :]
            line = jnp.sum(tops[pl.ds(at, SEG), :] * eye, axis=0, keepdims=True)
            big = line.astype(jnp.bfloat16).astype(jnp.float32)
            middle = (line - big).astype(jnp.bfloat16).astype(jnp.float32)
            rest = line - big - middle
            sub = lax.broadcasted_iota(jnp.int32, (16, 128), 0)
            parts = jnp.where(sub == 0, big, jnp.where(sub == 1, middle, jnp.where(sub == 2, rest, 0.0)))
            o_refs[step][pl.ds(pl.multiple_of(4 * SEG + slot * 16, 16), 16), :] = parts.astype(jnp.bfloat16)
        return carry

    lax.fori_loop(0, 4, tile, 0)


def attend(head, info, queries, pairs):
    return pl.pallas_call(
        functools.partial(attend_kernel, head),
        out_shape=[jax.ShapeDtypeStruct((4 * SEG + 64, HEAD_DIM), jnp.bfloat16)] * 4,
        in_specs=[SMEM] + [VMEM] * 12,
        out_specs=[VMEM] * 4,
        scratch_shapes=[
            pltpu.VMEM((2048, 2 * HEAD_DIM), jnp.bfloat16),
            pltpu.VMEM((KEYS, 2 * HEAD_DIM), jnp.bfloat16),
            pltpu.VMEM((KEYS, 2 * HEAD_DIM), jnp.bfloat16),
            pltpu.VMEM((TILE, KEYS), jnp.float32),
            pltpu.VMEM((TILE, HEAD_DIM), jnp.float32),
            pltpu.VMEM((TILE, 2 * HEAD_DIM), jnp.float32),
            pltpu.VMEM((TILE, HEAD_DIM), jnp.bfloat16),
        ],
        compiler_params=pltpu.CompilerParams(vmem_limit_bytes=48 << 20),
        cost_estimate=pl.CostEstimate(
            flops=2 * 2 * 2048 * 4096 * 128, bytes_accessed=4 << 20, transcendentals=2048 * 4096
        ),
    )(info, *queries, *pairs)


def combine_kernel(*refs):
    out_ref = refs[-1]
    eye = (
        lax.broadcasted_iota(jnp.int32, (SEG, SEG), 0)
        == lax.broadcasted_iota(jnp.int32, (SEG, SEG), 1)
    ).astype(jnp.float32)
    for head in range(3):
        parts = refs[4 * head : 4 * head + 4]
        for slot in range(4):
            levels = []
            for part in parts:
                lines = part[4 * SEG + slot * 16 : 4 * SEG + (slot + 1) * 16, :].astype(jnp.float32)
                levels.append(jnp.sum(lines, axis=0, keepdims=True))
            top = functools.reduce(jnp.maximum, levels)
            shares = [jnp.exp(level - top) for level in levels]
            total = functools.reduce(jnp.add, shares)
            spread = jnp.concatenate([eye * (share / total) for share in shares], axis=1)
            stacked = jnp.concatenate([part[slot * SEG : (slot + 1) * SEG, :] for part in parts], axis=0)
            mixed = jnp.dot(spread.astype(jnp.bfloat16), stacked, preferred_element_type=jnp.float32)
            out_ref[slot, :, head * HEAD_DIM : (head + 1) * HEAD_DIM] = mixed.astype(jnp.bfloat16)


def combine(blocks):
    return pl.pallas_call(
        combine_kernel,
        out_shape=jax.ShapeDtypeStruct((4, SEG, 3 * HEAD_DIM), jnp.bfloat16),
        in_specs=[VMEM] * len(blocks),
        out_specs=VMEM,
        compiler_params=pltpu.CompilerParams(vmem_limit_bytes=32 << 20),
    )(*blocks)


def spread_pairs(a, b):
    pairs = []
    for z in range(4):
        for c in range(2):
            target = (2 * c + ((z % 2) ^ a)) * 2 + ((z // 2) ^ b)
            pairs.append((z * 2 + c, target))
    return pairs


def turn(step):
    return [(n, (n + step) % 4) for n in range(4)]


def body(tokens, clip_id, w_qkv, w_out):
    z, y, x, c = [lax.axis_index(name) for name in ("z", "y", "x", "core")]
    zl, zh = z % 2, z // 2
    swap = [(0, 1), (1, 0)]

    halves = clip_id.reshape(2, SEG)
    counts = jnp.stack([jnp.sum(halves < 1, axis=1), jnp.sum(halves < 2, axis=1)], axis=1)
    header = jnp.pad(counts.astype(jnp.bfloat16)[:, None, :], ((0, 0), (0, 15), (0, 382)))

    other = lax.ppermute(tokens, "core", swap)
    both = jnp.where(c == 0, jnp.concatenate([tokens, other], 1), jnp.concatenate([other, tokens], 1))
    stacked = jnp.einsum("td,sdc->stc", both, w_qkv, preferred_element_type=jnp.float32)
    scale = jnp.array([1.0 / math.sqrt(HEAD_DIM), 1.0, 1.0], jnp.float32)[:, None, None]
    stacked = (stacked * scale).astype(jnp.bfloat16)

    arrived = []
    for a, b in SLOTS:
        block = lax.dynamic_slice(stacked, (0, (zh ^ b) * SEG, (zl ^ a) * 384), (3, SEG, 384))
        head_rows = lax.dynamic_slice(header, (zh ^ b, 0, 0), (1, 16, 384))
        block = jnp.concatenate([block.reshape(3 * SEG, 384), head_rows[0]], axis=0)
        arrived.append(lax.ppermute(block, ("z", "core"), spread_pairs(a, b)))

    own_q, *own_kv = prepare(arrived)
    queries = [own_q] + [lax.ppermute(own_q, "x", turn(step)) for step in (1, 2, 3)]
    pairs = []
    for head in range(3):
        near = [own_kv[head]] + [lax.ppermute(own_kv[head], "y", turn(step)) for step in (1, 2, 3)]
        pairs.append(near + [lax.ppermute(block, "core", swap) for block in near])
    info = jnp.stack([zl, y, x, c]).astype(jnp.int32)

    results = []
    for head in range(3):
        out = attend(head, info, queries, pairs[head])
        results.append(out[0])
        for step in (1, 2, 3):
            results.append(lax.ppermute(out[step], "x", turn(step)))
    mixed = combine(results)

    back = []
    for index, (a, b) in enumerate(SLOTS):
        returns = [(target, source) for source, target in spread_pairs(a, b)]
        back.append(lax.ppermute(mixed[index], ("z", "core"), returns))
    rows = []
    for half in range(2):
        by_a = [jnp.where(zh == half, back[2 * a], back[2 * a + 1]) for a in range(2)]
        rows.append(
            jnp.concatenate([jnp.where(zl == 0, by_a[0], by_a[1]), jnp.where(zl == 0, by_a[1], by_a[0])], 1)
        )
    attended = jnp.concatenate(rows, axis=0)
    half_cols = w_out.shape[1] // 2
    w_there = lax.dynamic_slice(w_out, (0, (1 - c) * half_cols), (w_out.shape[0], half_cols))
    w_here = lax.dynamic_slice(w_out, (0, c * half_cols), (w_out.shape[0], half_cols))
    there = jnp.dot(attended, w_there, preferred_element_type=jnp.float32).astype(jnp.bfloat16)
    received = lax.ppermute(there, "core", swap)
    here = jnp.dot(attended, w_here, preferred_element_type=jnp.float32)
    return (here + received.astype(jnp.float32)).astype(jnp.bfloat16)


def solution(mesh):
    fine = Mesh(mesh.devices.reshape(4, 4, 4, 2), ("z", "y", "x", "core"))
    seq = ("z", "y", "x")
    in_specs = (P(seq, "core"), P(seq), P(None, None, "core"), P("core", None))
    return jax.shard_map(body, mesh=fine, in_specs=in_specs, out_specs=P(seq, "core"), check_vma=False)
```

```python
import functools
import math

import jax
import jax.numpy as jnp
from jax import lax
from jax.experimental import pallas as pl
from jax.experimental.pallas import tpu as pltpu
from jax.sharding import Mesh
from jax.sharding import PartitionSpec as P

HEAD_DIM = 128
SEG = 128
TILE = 512
KEYS = 4096
NEG = -1e30
FLOOR = -1e29
WIDTHS = (768, 1536, 2048, 2688, 3328, 4096)
SLOTS = [(a, b) for a in range(2) for b in range(2)]
VMEM = pl.BlockSpec(memory_space=pltpu.VMEM)
SMEM = pl.BlockSpec(memory_space=pltpu.SMEM)


def slot_counts(blocks):
    sub = lax.broadcasted_iota(jnp.int32, (16, HEAD_DIM), 0)
    counts = jnp.zeros((16, HEAD_DIM), jnp.float32)
    for slot, block in enumerate(blocks):
        line = block[3 * SEG : 3 * SEG + 1, :HEAD_DIM].astype(jnp.float32)
        counts = jnp.where(sub == slot, line, counts)
    return counts.astype(jnp.bfloat16)


def queries_kernel(heads, *refs):
    blocks, q_ref = refs[:4], refs[-1]
    cols = slice(heads[0] * HEAD_DIM, (heads[-1] + 1) * HEAD_DIM)
    for slot, block in enumerate(blocks):
        q_ref[slot * SEG : (slot + 1) * SEG, :] = block[:SEG, cols]
    counts = slot_counts(blocks)
    for n in range(len(heads)):
        q_ref[4 * SEG :, n * HEAD_DIM : (n + 1) * HEAD_DIM] = counts


def pairs_kernel(heads, *refs):
    blocks, kv_ref = refs[:4], refs[-1]
    cols = slice(heads[0] * HEAD_DIM, (heads[-1] + 1) * HEAD_DIM)
    for slot, block in enumerate(blocks):
        kv_ref[slot * 2 * SEG : (slot + 1) * 2 * SEG, :] = block[SEG : 3 * SEG, cols]
    counts = slot_counts(blocks)
    for n in range(len(heads)):
        kv_ref[8 * SEG :, n * HEAD_DIM : (n + 1) * HEAD_DIM] = counts


def merge_kernel(place, info, *refs):
    blocks, out_ref = refs[:4], refs[-1]
    zl, y, x, c = [info[n] for n in range(4)]
    cols = slice(place * HEAD_DIM, (place + 1) * HEAD_DIM)
    for step, block in enumerate(blocks):
        for slot, (a, b) in enumerate(SLOTS):
            zz = 2 * (c ^ b) + (zl ^ a)
            at = pl.multiple_of((zz * 4 + ((y - step) & 3)) * SEG, SEG)
            out_ref[pl.ds(at, SEG), :] = block[slot * 2 * SEG : slot * 2 * SEG + SEG, cols]
            out_ref[pl.ds(2048 + at, SEG), :] = block[slot * 2 * SEG + SEG : (slot + 1) * 2 * SEG, cols]
        out_ref[4096 + 16 * step : 4096 + 16 * (step + 1), :] = block[8 * SEG :, cols]


def small_call(kernel, rows, cols, operands, after=(), info=None):
    lead = [] if info is None else [info]
    return pl.pallas_call(
        kernel,
        out_shape=jax.ShapeDtypeStruct((rows, cols), jnp.bfloat16),
        in_specs=[SMEM] * len(lead) + [VMEM] * len(operands) + [pl.BlockSpec(memory_space=pl.ANY)] * len(after),
        out_specs=VMEM,
        compiler_params=pltpu.CompilerParams(vmem_limit_bytes=32 << 20),
    )(*lead, *operands, *after)


def attend_kernel(head, info, *refs):
    q_refs, (near, far), refs = refs[:4], refs[4:6], refs[6:]
    before, refs = (refs[:4], refs[4:]) if head == 1 else ((), refs)
    o_refs, (queries, keys, vals, scores, tops, sums, flat) = refs[:4], refs[4:]
    base = 0
    for old, o_ref in zip(before, o_refs):
        base = old.shape[0]
        o_ref[:base, :] = old[...]
    zl, y, x, c = [info[n] for n in range(4)]
    lane = lax.broadcasted_iota(jnp.int32, (SEG, HEAD_DIM), 1)
    row = lax.broadcasted_iota(jnp.int32, (SEG, HEAD_DIM), 0)

    def bounds(lines):
        found = sum(line.astype(jnp.float32) for line in lines)
        return [
            jnp.sum(jnp.where(lane[:16] == n, found, 0.0), keepdims=True)[0, 0].astype(jnp.int32)
            for n in range(2)
        ]

    n1, n2 = bounds([ref[KEYS + 16 * n : KEYS + 16 * (n + 1), :] for ref in (near, far) for n in range(4)])
    m1, m2 = bounds([ref[4 * SEG :, :HEAD_DIM] for ref in q_refs])

    def clip_of(index, first, second):
        return (index >= first).astype(jnp.int32) + (index >= second).astype(jnp.int32)

    for n in range(KEYS // SEG):
        own = clip_of(row + n * SEG, n1, n2) == lane
        keys[n * SEG : (n + 1) * SEG, HEAD_DIM:] = own.astype(jnp.float32).astype(jnp.bfloat16)
    for n in range(2048 // SEG):
        differs = (clip_of(row + n * SEG, m1, m2) != lane) & (lane < 3)
        queries[n * SEG : (n + 1) * SEG, HEAD_DIM:] = jnp.where(differs, NEG, 0.0).astype(jnp.bfloat16)
    vals[:, HEAD_DIM:] = jnp.ones((KEYS, HEAD_DIM), jnp.bfloat16)
    for slot, (a, b) in enumerate(SLOTS):
        for step in range(4):
            zz = 2 * (c ^ b) + (zl ^ a)
            at = pl.multiple_of((zz * 4 + ((x - step) & 3)) * SEG, SEG)
            place = head - 1 if step == 2 and head else head
            cols = slice(place * HEAD_DIM, (place + 1) * HEAD_DIM)
            queries[pl.ds(at, SEG), :HEAD_DIM] = q_refs[step][slot * SEG : (slot + 1) * SEG, cols]
    for n in range(16):
        for cc, ref in ((c, near), (1 - c, far)):
            at = pl.multiple_of((2 * n + cc) * SEG, SEG)
            keys[pl.ds(at, SEG), :HEAD_DIM] = ref[n * SEG : (n + 1) * SEG, :]
            vals[pl.ds(at, SEG), :HEAD_DIM] = ref[2048 + n * SEG : 2048 + (n + 1) * SEG, :]

    eye = (lane == row).astype(jnp.float32)

    def tile(zz, carry):
        first, last = zz * TILE, zz * TILE + TILE - 1
        low = jnp.where(first >= m2, n2, jnp.where(first >= m1, n1, 0))
        high = jnp.where(last >= m2, KEYS, jnp.where(last >= m1, n2, n1))
        low = (low // SEG) * SEG
        need = high - low
        rows = pl.ds(pl.multiple_of(first, TILE), TILE)
        tops[...] = jnp.full((TILE, HEAD_DIM), NEG, jnp.float32)
        sums[...] = jnp.zeros((TILE, 2 * HEAD_DIM), jnp.float32)

        def runs(k):
            under = WIDTHS[k - 1] if k else 0
            return ((need > under) & (need <= WIDTHS[k])).astype(jnp.int32)

        for k, width in enumerate(WIDTHS):
            at = pl.multiple_of(jnp.minimum(low, KEYS - width), SEG)

            def first_pass(i, carry, width=width, at=at):
                s = lax.dot_general(
                    queries[rows, :],
                    keys[pl.ds(at, width), :],
                    (((1,), (1,)), ((), ())),
                    preferred_element_type=jnp.float32,
                )
                scores[:, :width] = s
                top = s[:, :128]
                for n in range(1, width // 128):
                    top = jnp.maximum(top, s[:, n * 128 : (n + 1) * 128])
                tops[...] = top
                return carry

            lax.fori_loop(0, runs(k), first_pass, 0)

        top = jnp.maximum(jnp.max(tops[...], axis=1, keepdims=True), FLOOR)

        for k, width in enumerate(WIDTHS):
            at = pl.multiple_of(jnp.minimum(low, KEYS - width), SEG)

            def second_pass(i, carry, width=width, at=at):
                weights = jnp.exp(scores[:, :width] - top).astype(jnp.bfloat16)
                sums[...] = jnp.dot(weights, vals[pl.ds(at, width), :], preferred_element_type=jnp.float32)
                return carry

            lax.fori_loop(0, runs(k), second_pass, 0)

        total = jnp.maximum(sums[:, HEAD_DIM:], 1e-30)
        flat[...] = (sums[:, :HEAD_DIM] / total).astype(jnp.bfloat16)
        tops[...] = top + jnp.log(total)
        slot = ((zz & 1) ^ zl) * 2 + ((zz >> 1) ^ c)
        for step in range(4):
            at = pl.multiple_of(((x + step) & 3) * SEG, SEG)
            o_refs[step][pl.ds(pl.multiple_of(base + slot * SEG, 64), SEG), :] = flat[pl.ds(at, SEG), :]
            line = jnp.sum(tops[pl.ds(at, SEG), :] * eye, axis=0, keepdims=True)
            big = line.astype(jnp.bfloat16).astype(jnp.float32)
            middle = (line - big).astype(jnp.bfloat16).astype(jnp.float32)
            rest = line - big - middle
            sub = lax.broadcasted_iota(jnp.int32, (16, 128), 0)
            parts = jnp.where(sub == 0, big, jnp.where(sub == 1, middle, jnp.where(sub == 2, rest, 0.0)))
            o_refs[step][pl.ds(pl.multiple_of(base + 4 * SEG + slot * 16, 16), 16), :] = parts.astype(jnp.bfloat16)
        return carry

    lax.fori_loop(0, 4, tile, 0)


def attend(head, info, queries, near, far, before=()):
    return pl.pallas_call(
        functools.partial(attend_kernel, head),
        out_shape=[jax.ShapeDtypeStruct(((2 if before else 1) * (4 * SEG + 64), HEAD_DIM), jnp.bfloat16)] * 4,
        in_specs=[SMEM] + [VMEM] * (6 + len(before)),
        out_specs=[VMEM] * 4,
        scratch_shapes=[
            pltpu.VMEM((2048, 2 * HEAD_DIM), jnp.bfloat16),
            pltpu.VMEM((KEYS, 2 * HEAD_DIM), jnp.bfloat16),
            pltpu.VMEM((KEYS, 2 * HEAD_DIM), jnp.bfloat16),
            pltpu.VMEM((TILE, KEYS), jnp.float32),
            pltpu.VMEM((TILE, HEAD_DIM), jnp.float32),
            pltpu.VMEM((TILE, 2 * HEAD_DIM), jnp.float32),
            pltpu.VMEM((TILE, HEAD_DIM), jnp.bfloat16),
        ],
        compiler_params=pltpu.CompilerParams(vmem_limit_bytes=48 << 20),
        cost_estimate=pl.CostEstimate(
            flops=2 * 2 * 2048 * 4096 * 128, bytes_accessed=4 << 20, transcendentals=2048 * 4096
        ),
    )(info, *queries, near, far, *before)


def combine_kernel(*refs):
    out_ref = refs[-1]
    eye = (
        lax.broadcasted_iota(jnp.int32, (SEG, SEG), 0)
        == lax.broadcasted_iota(jnp.int32, (SEG, SEG), 1)
    ).astype(jnp.float32)
    for head in range(3):
        parts = refs[:4] if head < 2 else refs[4:8]
        base = 4 * SEG + 64 if head == 1 else 0
        for slot in range(4):
            levels = []
            for part in parts:
                at = base + 4 * SEG + slot * 16
                lines = part[at : at + 16, :].astype(jnp.float32)
                levels.append(jnp.sum(lines, axis=0, keepdims=True))
            top = functools.reduce(jnp.maximum, levels)
            shares = [jnp.exp(level - top) for level in levels]
            total = functools.reduce(jnp.add, shares)
            spread = jnp.concatenate([eye * (share / total) for share in shares], axis=1)
            at = base + slot * SEG
            stacked = jnp.concatenate([part[at : at + SEG, :] for part in parts], axis=0)
            mixed = jnp.dot(spread.astype(jnp.bfloat16), stacked, preferred_element_type=jnp.float32)
            out_ref[slot, :, head * HEAD_DIM : (head + 1) * HEAD_DIM] = mixed.astype(jnp.bfloat16)


def combine(blocks):
    return pl.pallas_call(
        combine_kernel,
        out_shape=jax.ShapeDtypeStruct((4, SEG, 3 * HEAD_DIM), jnp.bfloat16),
        in_specs=[VMEM] * len(blocks),
        out_specs=VMEM,
        compiler_params=pltpu.CompilerParams(vmem_limit_bytes=32 << 20),
    )(*blocks)


def spread_pairs(a, b):
    pairs = []
    for z in range(4):
        for c in range(2):
            target = (2 * c + ((z % 2) ^ a)) * 2 + ((z // 2) ^ b)
            pairs.append((z * 2 + c, target))
    return pairs


def turn(step):
    return [(n, (n + step) % 4) for n in range(4)]


def body(tokens, clip_id, w_qkv, w_out):
    z, y, x, c = [lax.axis_index(name) for name in ("z", "y", "x", "core")]
    zl, zh = z % 2, z // 2
    swap = [(0, 1), (1, 0)]

    halves = clip_id.reshape(2, SEG)
    counts = jnp.stack([jnp.sum(halves < 1, axis=1), jnp.sum(halves < 2, axis=1)], axis=1)
    header = jnp.pad(counts.astype(jnp.bfloat16)[:, None, :], ((0, 0), (0, 15), (0, 382)))

    other = lax.ppermute(tokens, "core", swap)
    both = jnp.where(c == 0, jnp.concatenate([tokens, other], 1), jnp.concatenate([other, tokens], 1))
    stacked = jnp.einsum("td,sdc->stc", both, w_qkv, preferred_element_type=jnp.float32)
    scale = jnp.array([1.0 / math.sqrt(HEAD_DIM), 1.0, 1.0], jnp.float32)[:, None, None]
    stacked = (stacked * scale).astype(jnp.bfloat16)

    arrived = []
    for a, b in SLOTS:
        block = lax.dynamic_slice(stacked, (0, (zh ^ b) * SEG, (zl ^ a) * 384), (3, SEG, 384))
        head_rows = lax.dynamic_slice(header, (zh ^ b, 0, 0), (1, 16, 384))
        block = jnp.concatenate([block.reshape(3 * SEG, 384), head_rows[0]], axis=0)
        arrived.append(lax.ppermute(block, ("z", "core"), spread_pairs(a, b)))

    info = jnp.stack([zl, y, x, c]).astype(jnp.int32)

    def pair_blocks(heads, after):
        kernel = functools.partial(pairs_kernel, heads)
        own = small_call(kernel, 8 * SEG + 16, len(heads) * HEAD_DIM, arrived, after)
        return [own] + [lax.ppermute(own, "y", turn(step)) for step in (1, 2, 3)]

    def merged(blocks, place, after):
        near = small_call(functools.partial(merge_kernel, place), KEYS + 64, HEAD_DIM, blocks, after, info)
        return near, lax.ppermute(near, "core", swap)

    def query_block(heads, after):
        kernel = functools.partial(queries_kernel, heads)
        return small_call(kernel, 4 * SEG + 16, len(heads) * HEAD_DIM, arrived, after)

    own_q = query_block((0, 1, 2), ())
    beside = [lax.ppermute(own_q, "x", turn(step)) for step in (1, 3)]
    first = pair_blocks((0,), (own_q,))
    across = lax.ppermute(query_block((0,), first[1:]), "x", turn(2))
    second = pair_blocks((1, 2), (*first[1:], *beside))
    part = attend(0, info, [own_q, beside[0], across, beside[1]], *merged(first, 0, beside))
    across = lax.ppermute(query_block((1, 2), (*first[1:], *beside)), "x", turn(2))
    queries = [own_q, beside[0], across, beside[1]]
    pairs = [merged(second, place, part[:1]) for place in range(2)]
    part = attend(1, info, queries, *pairs[0], part)
    last = attend(2, info, queries, *pairs[1])
    results = []
    for blocks in (part, last):
        results.append(blocks[0])
        for step in (1, 2, 3):
            results.append(lax.ppermute(blocks[step], "x", turn(step)))
    mixed = combine(results)

    back = []
    for index, (a, b) in enumerate(SLOTS):
        returns = [(target, source) for source, target in spread_pairs(a, b)]
        back.append(lax.ppermute(mixed[index], ("z", "core"), returns))
    rows = []
    for half in range(2):
        by_a = [jnp.where(zh == half, back[2 * a], back[2 * a + 1]) for a in range(2)]
        rows.append(
            jnp.concatenate([jnp.where(zl == 0, by_a[0], by_a[1]), jnp.where(zl == 0, by_a[1], by_a[0])], 1)
        )
    attended = jnp.concatenate(rows, axis=0)
    half_cols = w_out.shape[1] // 2
    w_there = lax.dynamic_slice(w_out, (0, (1 - c) * half_cols), (w_out.shape[0], half_cols))
    w_here = lax.dynamic_slice(w_out, (0, c * half_cols), (w_out.shape[0], half_cols))
    there = jnp.dot(attended, w_there, preferred_element_type=jnp.float32).astype(jnp.bfloat16)
    received = lax.ppermute(there, "core", swap)
    here = jnp.dot(attended, w_here, preferred_element_type=jnp.float32)
    return (here + received.astype(jnp.float32)).astype(jnp.bfloat16)


def solution(mesh):
    fine = Mesh(mesh.devices.reshape(4, 4, 4, 2), ("z", "y", "x", "core"))
    seq = ("z", "y", "x")
    in_specs = (P(seq, "core"), P(seq), P(None, None, "core"), P("core", None))
    return jax.shard_map(body, mesh=fine, in_specs=in_specs, out_specs=P(seq, "core"), check_vma=False)
```

```python
import functools
import math

import jax
import jax.numpy as jnp
from jax import lax
from jax.experimental import pallas as pl
from jax.experimental.pallas import tpu as pltpu
from jax.sharding import Mesh
from jax.sharding import PartitionSpec as P

HEAD_DIM = 128
SEG = 128
TILE = 512
KEYS = 4096
NEG = -1e30
FLOOR = -1e29
WIDTHS = (768, 1536, 2048, 2688, 3328, 4096)
SLOTS = [(a, b) for a in range(2) for b in range(2)]
VMEM = pl.BlockSpec(memory_space=pltpu.VMEM)
SMEM = pl.BlockSpec(memory_space=pltpu.SMEM)


def project(width, place_of, own, other, w_qkv, header, info, after=()):
    def kernel(info_ref, own_ref, other_ref, w_ref, header_ref, *refs):
        out_refs = refs[-2:]
        c = info_ref[3]
        s, a = pl.program_id(0), pl.program_id(1)
        depth = own_ref.shape[1]
        here = pl.multiple_of(c * depth, depth)
        there = pl.multiple_of((1 - c) * depth, depth)
        total = jnp.dot(own_ref[...], w_ref[0, pl.ds(here, depth), :], preferred_element_type=jnp.float32)
        total += jnp.dot(other_ref[...], w_ref[0, pl.ds(there, depth), :], preferred_element_type=jnp.float32)
        result = (total * jnp.where(s == 0, 1.0 / math.sqrt(HEAD_DIM), 1.0)).astype(jnp.bfloat16)
        for which in range(2):

            @pl.when(a == which)
            def _():
                out_refs[which][pl.ds(pl.multiple_of(s * 256, 256), 256), :] = result
                for n in range(width // HEAD_DIM):
                    out_refs[which][768:, n * HEAD_DIM : (n + 1) * HEAD_DIM] = header_ref[...]

    whole = lambda s, a, info_ref: (0, 0)
    grid_spec = pltpu.PrefetchScalarGridSpec(
        num_scalar_prefetch=1,
        grid=(3, 2),
        in_specs=[
            pl.BlockSpec(own.shape, whole),
            pl.BlockSpec(own.shape, whole),
            pl.BlockSpec(
                (1, w_qkv.shape[1], width), lambda s, a, info_ref: (s, 0, place_of(a ^ info_ref[0]))
            ),
            pl.BlockSpec(header.shape, whole),
        ]
        + [pl.BlockSpec(memory_space=pl.ANY)] * len(after),
        out_specs=[pl.BlockSpec((784, width), whole)] * 2,
    )
    return pl.pallas_call(
        kernel,
        grid_spec=grid_spec,
        out_shape=[jax.ShapeDtypeStruct((784, width), jnp.bfloat16)] * 2,
        compiler_params=pltpu.CompilerParams(vmem_limit_bytes=40 << 20),
        cost_estimate=pl.CostEstimate(
            flops=2 * 6 * 256 * 3072 * width, bytes_accessed=2 * 6 * 3072 * width, transcendentals=0
        ),
    )(info, own, other, w_qkv, header, *after)


def pass_kernel(*refs):
    for block, out_ref in zip(refs[:2], refs[-2:]):
        out_ref[...] = block[...]


def split_kernel(info, *refs):
    blocks, out_refs = refs[:2], refs[-2:]
    c = info[3]
    cols = out_refs[0].shape[1]
    sub = lax.broadcasted_iota(jnp.int32, (16, cols), 0)
    for out_ref, half in zip(out_refs, (c, 1 - c)):
        counts = jnp.zeros((16, cols), jnp.float32)
        for a, block in enumerate(blocks):
            out_ref[a * SEG : (a + 1) * SEG, :] = block[pl.ds(pl.multiple_of(half * SEG, SEG), SEG), :]
            lines = block[768:, :].astype(jnp.float32)
            line = jnp.sum(jnp.where(sub == half, lines, 0.0), axis=0, keepdims=True)
            counts = jnp.where(sub == a, line, counts)
        out_ref[2 * SEG :, :] = counts.astype(jnp.bfloat16)


def queries_kernel(*refs):
    (kept, came), q_ref = refs[:2], refs[-1]
    for slot, (a, b) in enumerate(SLOTS):
        q_ref[slot * SEG : (slot + 1) * SEG, :] = (kept, came)[b][a * SEG : (a + 1) * SEG, :]
    counts = kept[2 * SEG :, :].astype(jnp.float32) + came[2 * SEG :, :].astype(jnp.float32)
    q_ref[4 * SEG :, :] = counts.astype(jnp.bfloat16)


def pairs_kernel(place, *refs):
    blocks, kv_ref = refs[:2], refs[-1]
    cols = slice(place * HEAD_DIM, (place + 1) * HEAD_DIM)
    for a, block in enumerate(blocks):
        kv_ref[a * 512 : (a + 1) * 512, :] = block[256:768, cols]
        kv_ref[1024 + 16 * a : 1024 + 16 * (a + 1), :] = block[768:, cols]


def merge_kernel(info, *refs):
    blocks, out_ref = refs[:4], refs[-1]
    zl, y = info[0], info[1]
    for step, block in enumerate(blocks):
        for a in range(2):
            at = pl.multiple_of(((zl ^ a) * 4 + ((y - step) & 3)) * 256, 256)
            out_ref[pl.ds(at, 256), :] = block[a * 512 : a * 512 + 256, :]
            out_ref[pl.ds(2048 + at, 256), :] = block[a * 512 + 256 : a * 512 + 512, :]
        out_ref[4096 + 32 * step : 4096 + 32 * (step + 1), :] = block[1024:, :]


def small_call(kernel, rows, cols, operands, after=(), info=None, outs=1):
    lead = [] if info is None else [info]
    return pl.pallas_call(
        kernel,
        out_shape=[jax.ShapeDtypeStruct((rows, cols), jnp.bfloat16)] * outs,
        in_specs=[SMEM] * len(lead) + [VMEM] * len(operands) + [pl.BlockSpec(memory_space=pl.ANY)] * len(after),
        out_specs=[VMEM] * outs,
        compiler_params=pltpu.CompilerParams(vmem_limit_bytes=32 << 20),
    )(*lead, *operands, *after)


def attend_kernel(head, info, *refs):
    q_refs, (near, far), refs = refs[:4], refs[4:6], refs[6:]
    before, refs = (refs[:4], refs[4:]) if head == 1 else ((), refs[-11:])
    o_refs, (queries, keys, vals, scores, tops, sums, flat) = refs[:4], refs[4:]
    base = 0
    for old, o_ref in zip(before, o_refs):
        base = old.shape[0]
        o_ref[:base, :] = old[...]
    zl, y, x, c = [info[n] for n in range(4)]
    lane = lax.broadcasted_iota(jnp.int32, (SEG, HEAD_DIM), 1)
    row = lax.broadcasted_iota(jnp.int32, (SEG, HEAD_DIM), 0)

    def bounds(lines):
        found = sum(line.astype(jnp.float32) for line in lines)
        return [
            jnp.sum(jnp.where(lane[:16] == n, found, 0.0), keepdims=True)[0, 0].astype(jnp.int32)
            for n in range(2)
        ]

    n1, n2 = bounds([ref[KEYS + 16 * n : KEYS + 16 * (n + 1), :] for ref in (near, far) for n in range(8)])
    m1, m2 = bounds([ref[4 * SEG :, :HEAD_DIM] for ref in q_refs])

    def clip_of(index, first, second):
        return (index >= first).astype(jnp.int32) + (index >= second).astype(jnp.int32)

    for n in range(KEYS // SEG):
        own = clip_of(row + n * SEG, n1, n2) == lane
        keys[n * SEG : (n + 1) * SEG, HEAD_DIM:] = own.astype(jnp.float32).astype(jnp.bfloat16)
    for n in range(2048 // SEG):
        differs = (clip_of(row + n * SEG, m1, m2) != lane) & (lane < 3)
        queries[n * SEG : (n + 1) * SEG, HEAD_DIM:] = jnp.where(differs, NEG, 0.0).astype(jnp.bfloat16)
    vals[:, HEAD_DIM:] = jnp.ones((KEYS, HEAD_DIM), jnp.bfloat16)
    for slot, (a, b) in enumerate(SLOTS):
        for step in range(4):
            zz = 2 * (c ^ b) + (zl ^ a)
            at = pl.multiple_of((zz * 4 + ((x - step) & 3)) * SEG, SEG)
            place = max(head - 1, 0)
            cols = slice(place * HEAD_DIM, (place + 1) * HEAD_DIM)
            queries[pl.ds(at, SEG), :HEAD_DIM] = q_refs[step][slot * SEG : (slot + 1) * SEG, cols]
    for cc, ref in ((c, near), (1 - c, far)):
        at = pl.ds(pl.multiple_of(cc * 2048, 2048), 2048)
        keys[at, :HEAD_DIM] = ref[:2048, :]
        vals[at, :HEAD_DIM] = ref[2048:4096, :]

    eye = (lane == row).astype(jnp.float32)

    def tile(zz, carry):
        first, last = zz * TILE, zz * TILE + TILE - 1
        low = jnp.where(first >= m2, n2, jnp.where(first >= m1, n1, 0))
        high = jnp.where(last >= m2, KEYS, jnp.where(last >= m1, n2, n1))
        low = (low // SEG) * SEG
        need = high - low
        rows = pl.ds(pl.multiple_of(first, TILE), TILE)
        tops[...] = jnp.full((TILE, HEAD_DIM), NEG, jnp.float32)
        sums[...] = jnp.zeros((TILE, 2 * HEAD_DIM), jnp.float32)

        def runs(k):
            under = WIDTHS[k - 1] if k else 0
            return ((need > under) & (need <= WIDTHS[k])).astype(jnp.int32)

        for k, width in enumerate(WIDTHS):
            at = pl.multiple_of(jnp.minimum(low, KEYS - width), SEG)

            def first_pass(i, carry, width=width, at=at):
                s = lax.dot_general(
                    queries[rows, :],
                    keys[pl.ds(at, width), :],
                    (((1,), (1,)), ((), ())),
                    preferred_element_type=jnp.float32,
                )
                scores[:, :width] = s
                top = s[:, :128]
                for n in range(1, width // 128):
                    top = jnp.maximum(top, s[:, n * 128 : (n + 1) * 128])
                tops[...] = top
                return carry

            lax.fori_loop(0, runs(k), first_pass, 0)

        top = jnp.maximum(jnp.max(tops[...], axis=1, keepdims=True), FLOOR)

        for k, width in enumerate(WIDTHS):
            at = pl.multiple_of(jnp.minimum(low, KEYS - width), SEG)

            def second_pass(i, carry, width=width, at=at):
                weights = jnp.exp(scores[:, :width] - top).astype(jnp.bfloat16)
                sums[...] = jnp.dot(weights, vals[pl.ds(at, width), :], preferred_element_type=jnp.float32)
                return carry

            lax.fori_loop(0, runs(k), second_pass, 0)

        total = jnp.maximum(sums[:, HEAD_DIM:], 1e-30)
        flat[...] = (sums[:, :HEAD_DIM] / total).astype(jnp.bfloat16)
        tops[...] = top + jnp.log(total)
        slot = ((zz & 1) ^ zl) * 2 + ((zz >> 1) ^ c)
        for step in range(4):
            at = pl.multiple_of(((x + step) & 3) * SEG, SEG)
            o_refs[step][pl.ds(pl.multiple_of(base + slot * SEG, 64), SEG), :] = flat[pl.ds(at, SEG), :]
            line = jnp.sum(tops[pl.ds(at, SEG), :] * eye, axis=0, keepdims=True)
            big = line.astype(jnp.bfloat16).astype(jnp.float32)
            middle = (line - big).astype(jnp.bfloat16).astype(jnp.float32)
            rest = line - big - middle
            sub = lax.broadcasted_iota(jnp.int32, (16, 128), 0)
            parts = jnp.where(sub == 0, big, jnp.where(sub == 1, middle, jnp.where(sub == 2, rest, 0.0)))
            o_refs[step][pl.ds(pl.multiple_of(base + 4 * SEG + slot * 16, 16), 16), :] = parts.astype(jnp.bfloat16)
        return carry

    lax.fori_loop(0, 4, tile, 0)


def attend(head, info, queries, near, far, before=(), after=()):
    return pl.pallas_call(
        functools.partial(attend_kernel, head),
        out_shape=[jax.ShapeDtypeStruct(((2 if before else 1) * (4 * SEG + 64), HEAD_DIM), jnp.bfloat16)] * 4,
        in_specs=[SMEM] + [VMEM] * (6 + len(before)) + [pl.BlockSpec(memory_space=pl.ANY)] * len(after),
        out_specs=[VMEM] * 4,
        scratch_shapes=[
            pltpu.VMEM((2048, 2 * HEAD_DIM), jnp.bfloat16),
            pltpu.VMEM((KEYS, 2 * HEAD_DIM), jnp.bfloat16),
            pltpu.VMEM((KEYS, 2 * HEAD_DIM), jnp.bfloat16),
            pltpu.VMEM((TILE, KEYS), jnp.float32),
            pltpu.VMEM((TILE, HEAD_DIM), jnp.float32),
            pltpu.VMEM((TILE, 2 * HEAD_DIM), jnp.float32),
            pltpu.VMEM((TILE, HEAD_DIM), jnp.bfloat16),
        ],
        compiler_params=pltpu.CompilerParams(vmem_limit_bytes=48 << 20),
        cost_estimate=pl.CostEstimate(
            flops=2 * 2 * 2048 * 4096 * 128, bytes_accessed=4 << 20, transcendentals=2048 * 4096
        ),
    )(info, *queries, near, far, *before, *after)


def combine_kernel(*refs):
    out_ref = refs[-1]
    eye = (
        lax.broadcasted_iota(jnp.int32, (SEG, SEG), 0)
        == lax.broadcasted_iota(jnp.int32, (SEG, SEG), 1)
    ).astype(jnp.float32)
    for head in range(3):
        parts = refs[:4] if head < 2 else refs[4:8]
        base = 4 * SEG + 64 if head == 1 else 0
        for slot in range(4):
            levels = []
            for part in parts:
                at = base + 4 * SEG + slot * 16
                lines = part[at : at + 16, :].astype(jnp.float32)
                levels.append(jnp.sum(lines, axis=0, keepdims=True))
            top = functools.reduce(jnp.maximum, levels)
            shares = [jnp.exp(level - top) for level in levels]
            total = functools.reduce(jnp.add, shares)
            spread = jnp.concatenate([eye * (share / total) for share in shares], axis=1)
            at = base + slot * SEG
            stacked = jnp.concatenate([part[at : at + SEG, :] for part in parts], axis=0)
            mixed = jnp.dot(spread.astype(jnp.bfloat16), stacked, preferred_element_type=jnp.float32)
            out_ref[slot, :, head * HEAD_DIM : (head + 1) * HEAD_DIM] = mixed.astype(jnp.bfloat16)


def combine(blocks):
    return pl.pallas_call(
        combine_kernel,
        out_shape=jax.ShapeDtypeStruct((4, SEG, 3 * HEAD_DIM), jnp.bfloat16),
        in_specs=[VMEM] * len(blocks),
        out_specs=VMEM,
        compiler_params=pltpu.CompilerParams(vmem_limit_bytes=32 << 20),
    )(*blocks)


def spread_pairs(a, b):
    pairs = []
    for z in range(4):
        for c in range(2):
            target = (2 * c + ((z % 2) ^ a)) * 2 + ((z // 2) ^ b)
            pairs.append((z * 2 + c, target))
    return pairs


def turn(step):
    return [(n, (n + step) % 4) for n in range(4)]


def body(tokens, clip_id, w_qkv, w_out):
    z, y, x, c = [lax.axis_index(name) for name in ("z", "y", "x", "core")]
    zl, zh = z % 2, z // 2
    swap = [(0, 1), (1, 0)]
    info = jnp.stack([zl, y, x, c, zh]).astype(jnp.int32)

    halves = clip_id.reshape(2, SEG)
    counts = jnp.stack([jnp.sum(halves < 1, axis=1), jnp.sum(halves < 2, axis=1)], axis=1)
    header = jnp.pad(counts.astype(jnp.bfloat16), ((0, 14), (0, HEAD_DIM - 2)))

    other = lax.ppermute(tokens, "core", swap)
    shared = (tokens, other, w_qkv, header, info)

    def to_group(blocks):
        return [lax.ppermute(block, ("z", "core"), spread_pairs(a, 0)) for a, block in enumerate(blocks)]

    made = project(HEAD_DIM, lambda i: 2 + i, *shared)
    first_in = to_group(made)
    def key_blocks(arrived, place, after=()):
        [own] = small_call(functools.partial(pairs_kernel, place), 1056, HEAD_DIM, arrived, after)
        return [own] + [lax.ppermute(own, "y", turn(step)) for step in (1, 2, 3)]

    def merged(blocks, after=()):
        [near] = small_call(merge_kernel, KEYS + 128, HEAD_DIM, blocks, after, info)
        return near, lax.ppermute(near, "core", swap)

    def split(arrived, after=()):
        return small_call(split_kernel, 2 * SEG + 16, arrived[0].shape[1], arrived, after, info, 2)

    def query_blocks(keep, give, after=()):
        came = lax.ppermute(give, "core", swap)
        [own] = small_call(queries_kernel, 4 * SEG + 16, keep.shape[1], [keep, came], after)
        return [own] + [lax.ppermute(own, "x", turn(step)) for step in (1, 2, 3)]

    made_too = project(2 * HEAD_DIM, lambda i: 2 * i, *shared, made[:1])
    shares = split(first_in, made_too[:1])
    kv = key_blocks(first_in, 0, shares[:1])
    q_first = query_blocks(*shares, kv[:1])
    second_in = to_group(small_call(pass_kernel, 784, 2 * HEAD_DIM, made_too, (*first_in, kv[0]), outs=2))
    shares = split(second_in)
    kv_next = key_blocks(second_in, 0, kv[1:])
    q_second = query_blocks(*shares, (*q_first[1:], kv_next[0]))
    part = attend(0, info, q_first, *merged(kv, (*q_first[1:], shares[0])), after=q_second[1:])
    kv_last = key_blocks(second_in, 1, (*kv_next[1:], part[0]))
    part = attend(1, info, q_second, *merged(kv_next, part[:1]), part)
    last = attend(2, info, q_second, *merged(kv_last, part[:1]))
    results = []
    for blocks in (part, last):
        results.append(blocks[0])
        for step in (1, 2, 3):
            results.append(lax.ppermute(blocks[step], "x", turn(step)))
    mixed = combine(results)

    back = []
    for index, (a, b) in enumerate(SLOTS):
        returns = [(target, source) for source, target in spread_pairs(a, b)]
        back.append(lax.ppermute(mixed[index], ("z", "core"), returns))
    rows = []
    for half in range(2):
        by_a = [jnp.where(zh == half, back[2 * a], back[2 * a + 1]) for a in range(2)]
        groups = [jnp.where(zl == 0, by_a[0], by_a[1]), jnp.where(zl == 0, by_a[1], by_a[0])]
        rows.append(jnp.concatenate([groups[0][:, HEAD_DIM:], groups[0][:, :HEAD_DIM], groups[1]], 1))
    attended = jnp.concatenate(rows, axis=0)
    half_cols = w_out.shape[1] // 2
    w_there = lax.dynamic_slice(w_out, (0, (1 - c) * half_cols), (w_out.shape[0], half_cols))
    w_here = lax.dynamic_slice(w_out, (0, c * half_cols), (w_out.shape[0], half_cols))
    there = jnp.dot(attended, w_there, preferred_element_type=jnp.float32).astype(jnp.bfloat16)
    received = lax.ppermute(there, "core", swap)
    here = jnp.dot(attended, w_here, preferred_element_type=jnp.float32)
    return (here + received.astype(jnp.float32)).astype(jnp.bfloat16)


def solution(mesh):
    fine = Mesh(mesh.devices.reshape(4, 4, 4, 2), ("z", "y", "x", "core"))
    seq = ("z", "y", "x")
    in_specs = (P(seq, "core"), P(seq), P(None, None, "core"), P("core", None))
    return jax.shard_map(body, mesh=fine, in_specs=in_specs, out_specs=P(seq, "core"), check_vma=False)
```

```python
import functools
import math

import jax
import jax.numpy as jnp
from jax import lax
from jax.experimental import pallas as pl
from jax.experimental.pallas import tpu as pltpu
from jax.sharding import Mesh
from jax.sharding import PartitionSpec as P

HEAD_DIM = 128
SEG = 128
TILE = 512
KEYS = 4096
NEG = -1e30
FLOOR = -1e29
WIDTHS = (768, 1536, 2048, 2688, 3328, 4096)
SLOTS = [(a, b) for a in range(2) for b in range(2)]
VMEM = pl.BlockSpec(memory_space=pltpu.VMEM)
SMEM = pl.BlockSpec(memory_space=pltpu.SMEM)


def send_queries_kernel(info, q_ref, header, *out_refs):
    zl, zh = info[0], info[4]
    for slot, (a, b) in enumerate(SLOTS):
        half = zh ^ b
        rows = pl.ds(pl.multiple_of(half * SEG, SEG), SEG)
        for group in range(2):

            @pl.when((zl ^ a) == group)
            def _():
                out_refs[slot][:SEG, :] = q_ref[rows, group * 384 : (group + 1) * 384]

        for n in range(3):
            out_refs[slot][SEG:, n * HEAD_DIM : (n + 1) * HEAD_DIM] = header[half]


def send_pairs_kernel(info, kv_ref, header, *refs):
    out_refs, zl = refs[-2:], info[0]
    for a, out_ref in enumerate(out_refs):
        for group in range(2):

            @pl.when((zl ^ a) == group)
            def _():
                for n in range(2):
                    out_ref[n * 256 : (n + 1) * 256, :] = kv_ref[n, :, group * 384 : (group + 1) * 384]

        for n in range(3):
            out_ref[512:, n * HEAD_DIM : (n + 1) * HEAD_DIM] = header[2]


def queries_kernel(*refs):
    blocks, q_ref = refs[:4], refs[-1]
    counts = jnp.zeros((16, 3 * HEAD_DIM), jnp.float32)
    sub = lax.broadcasted_iota(jnp.int32, counts.shape, 0)
    for slot, block in enumerate(blocks):
        q_ref[slot * SEG : (slot + 1) * SEG, :] = block[:SEG, :]
        counts = jnp.where(sub == slot, block[SEG : SEG + 1, :].astype(jnp.float32), counts)
    q_ref[4 * SEG :, :] = counts.astype(jnp.bfloat16)


def pairs_kernel(place, *refs):
    blocks, kv_ref = refs[:2], refs[-1]
    cols = slice(place * HEAD_DIM, (place + 1) * HEAD_DIM)
    for a, block in enumerate(blocks):
        kv_ref[a * 512 : (a + 1) * 512, :] = block[:512, cols]
        kv_ref[1024 + 16 * a : 1024 + 16 * (a + 1), :] = block[512:, cols]


def merge_kernel(info, *refs):
    blocks, out_ref = refs[:4], refs[-1]
    zl, y = info[0], info[1]
    for step, block in enumerate(blocks):
        for a in range(2):
            at = pl.multiple_of(((zl ^ a) * 4 + ((y - step) & 3)) * 256, 256)
            out_ref[pl.ds(at, 256), :] = block[a * 512 : a * 512 + 256, :]
            out_ref[pl.ds(2048 + at, 256), :] = block[a * 512 + 256 : a * 512 + 512, :]
        out_ref[4096 + 32 * step : 4096 + 32 * (step + 1), :] = block[1024:, :]


def small_call(kernel, rows, cols, operands, after=(), info=None, outs=1):
    lead = [] if info is None else [info]
    return pl.pallas_call(
        kernel,
        out_shape=[jax.ShapeDtypeStruct((rows, cols), jnp.bfloat16)] * outs,
        in_specs=[SMEM] * len(lead) + [VMEM] * len(operands) + [pl.BlockSpec(memory_space=pl.ANY)] * len(after),
        out_specs=[VMEM] * outs,
        compiler_params=pltpu.CompilerParams(vmem_limit_bytes=32 << 20),
    )(*lead, *operands, *after)


def attend_kernel(head, info, *refs):
    q_refs, (near, far), refs = refs[:4], refs[4:6], refs[6:]
    before, refs = (refs[:4], refs[4:]) if head == 1 else ((), refs[-11:])
    o_refs, (queries, keys, vals, scores, tops, sums, flat) = refs[:4], refs[4:]
    base = 0
    for old, o_ref in zip(before, o_refs):
        base = old.shape[0]
        o_ref[:base, :] = old[...]
    zl, y, x, c = [info[n] for n in range(4)]
    lane = lax.broadcasted_iota(jnp.int32, (SEG, HEAD_DIM), 1)
    row = lax.broadcasted_iota(jnp.int32, (SEG, HEAD_DIM), 0)

    def bounds(lines):
        found = sum(line.astype(jnp.float32) for line in lines)
        return [
            jnp.sum(jnp.where(lane[:16] == n, found, 0.0), keepdims=True)[0, 0].astype(jnp.int32)
            for n in range(2)
        ]

    n1, n2 = bounds([ref[KEYS + 16 * n : KEYS + 16 * (n + 1), :] for ref in (near, far) for n in range(8)])
    m1, m2 = bounds([ref[4 * SEG :, :HEAD_DIM] for ref in q_refs])

    def clip_of(index, first, second):
        return (index >= first).astype(jnp.int32) + (index >= second).astype(jnp.int32)

    for n in range(KEYS // SEG):
        own = clip_of(row + n * SEG, n1, n2) == lane
        keys[n * SEG : (n + 1) * SEG, HEAD_DIM:] = own.astype(jnp.float32).astype(jnp.bfloat16)
    for n in range(2048 // SEG):
        differs = (clip_of(row + n * SEG, m1, m2) != lane) & (lane < 3)
        queries[n * SEG : (n + 1) * SEG, HEAD_DIM:] = jnp.where(differs, NEG, 0.0).astype(jnp.bfloat16)
    vals[:, HEAD_DIM:] = jnp.ones((KEYS, HEAD_DIM), jnp.bfloat16)
    for slot, (a, b) in enumerate(SLOTS):
        for step in range(4):
            zz = 2 * (c ^ b) + (zl ^ a)
            at = pl.multiple_of((zz * 4 + ((x - step) & 3)) * SEG, SEG)
            cols = slice(head * HEAD_DIM, (head + 1) * HEAD_DIM)
            queries[pl.ds(at, SEG), :HEAD_DIM] = q_refs[step][slot * SEG : (slot + 1) * SEG, cols]
    for cc, ref in ((c, near), (1 - c, far)):
        at = pl.ds(pl.multiple_of(cc * 2048, 2048), 2048)
        keys[at, :HEAD_DIM] = ref[:2048, :]
        vals[at, :HEAD_DIM] = ref[2048:4096, :]

    eye = (lane == row).astype(jnp.float32)

    def tile(zz, carry):
        first, last = zz * TILE, zz * TILE + TILE - 1
        low = jnp.where(first >= m2, n2, jnp.where(first >= m1, n1, 0))
        high = jnp.where(last >= m2, KEYS, jnp.where(last >= m1, n2, n1))
        low = (low // SEG) * SEG
        need = high - low
        rows = pl.ds(pl.multiple_of(first, TILE), TILE)
        tops[...] = jnp.full((TILE, HEAD_DIM), NEG, jnp.float32)
        sums[...] = jnp.zeros((TILE, 2 * HEAD_DIM), jnp.float32)

        def runs(k):
            under = WIDTHS[k - 1] if k else 0
            return ((need > under) & (need <= WIDTHS[k])).astype(jnp.int32)

        for k, width in enumerate(WIDTHS):
            at = pl.multiple_of(jnp.minimum(low, KEYS - width), SEG)

            def first_pass(i, carry, width=width, at=at):
                s = lax.dot_general(
                    queries[rows, :],
                    keys[pl.ds(at, width), :],
                    (((1,), (1,)), ((), ())),
                    preferred_element_type=jnp.float32,
                )
                scores[:, :width] = s
                top = s[:, :128]
                for n in range(1, width // 128):
                    top = jnp.maximum(top, s[:, n * 128 : (n + 1) * 128])
                tops[...] = top
                return carry

            lax.fori_loop(0, runs(k), first_pass, 0)

        top = jnp.maximum(jnp.max(tops[...], axis=1, keepdims=True), FLOOR)

        for k, width in enumerate(WIDTHS):
            at = pl.multiple_of(jnp.minimum(low, KEYS - width), SEG)

            def second_pass(i, carry, width=width, at=at):
                weights = jnp.exp(scores[:, :width] - top).astype(jnp.bfloat16)
                sums[...] = jnp.dot(weights, vals[pl.ds(at, width), :], preferred_element_type=jnp.float32)
                return carry

            lax.fori_loop(0, runs(k), second_pass, 0)

        total = jnp.maximum(sums[:, HEAD_DIM:], 1e-30)
        flat[...] = (sums[:, :HEAD_DIM] / total).astype(jnp.bfloat16)
        tops[...] = top + jnp.log(total)
        slot = ((zz & 1) ^ zl) * 2 + ((zz >> 1) ^ c)
        for step in range(4):
            at = pl.multiple_of(((x + step) & 3) * SEG, SEG)
            o_refs[step][pl.ds(pl.multiple_of(base + slot * SEG, 64), SEG), :] = flat[pl.ds(at, SEG), :]
            line = jnp.sum(tops[pl.ds(at, SEG), :] * eye, axis=0, keepdims=True)
            big = line.astype(jnp.bfloat16).astype(jnp.float32)
            middle = (line - big).astype(jnp.bfloat16).astype(jnp.float32)
            rest = line - big - middle
            sub = lax.broadcasted_iota(jnp.int32, (16, 128), 0)
            parts = jnp.where(sub == 0, big, jnp.where(sub == 1, middle, jnp.where(sub == 2, rest, 0.0)))
            o_refs[step][pl.ds(pl.multiple_of(base + 4 * SEG + slot * 16, 16), 16), :] = parts.astype(jnp.bfloat16)
        return carry

    lax.fori_loop(0, 4, tile, 0)


def attend(head, info, queries, near, far, before=(), after=()):
    return pl.pallas_call(
        functools.partial(attend_kernel, head),
        out_shape=[jax.ShapeDtypeStruct(((2 if before else 1) * (4 * SEG + 64), HEAD_DIM), jnp.bfloat16)] * 4,
        in_specs=[SMEM] + [VMEM] * (6 + len(before)) + [pl.BlockSpec(memory_space=pl.ANY)] * len(after),
        out_specs=[VMEM] * 4,
        scratch_shapes=[
            pltpu.VMEM((2048, 2 * HEAD_DIM), jnp.bfloat16),
            pltpu.VMEM((KEYS, 2 * HEAD_DIM), jnp.bfloat16),
            pltpu.VMEM((KEYS, 2 * HEAD_DIM), jnp.bfloat16),
            pltpu.VMEM((TILE, KEYS), jnp.float32),
            pltpu.VMEM((TILE, HEAD_DIM), jnp.float32),
            pltpu.VMEM((TILE, 2 * HEAD_DIM), jnp.float32),
            pltpu.VMEM((TILE, HEAD_DIM), jnp.bfloat16),
        ],
        compiler_params=pltpu.CompilerParams(vmem_limit_bytes=48 << 20),
        cost_estimate=pl.CostEstimate(
            flops=2 * 2 * 2048 * 4096 * 128, bytes_accessed=4 << 20, transcendentals=2048 * 4096
        ),
    )(info, *queries, near, far, *before, *after)


def combine_kernel(*refs):
    out_ref = refs[-1]
    eye = (
        lax.broadcasted_iota(jnp.int32, (SEG, SEG), 0)
        == lax.broadcasted_iota(jnp.int32, (SEG, SEG), 1)
    ).astype(jnp.float32)
    for head in range(3):
        parts = refs[:4] if head < 2 else refs[4:8]
        base = 4 * SEG + 64 if head == 1 else 0
        for slot in range(4):
            levels = []
            for part in parts:
                at = base + 4 * SEG + slot * 16
                lines = part[at : at + 16, :].astype(jnp.float32)
                levels.append(jnp.sum(lines, axis=0, keepdims=True))
            top = functools.reduce(jnp.maximum, levels)
            shares = [jnp.exp(level - top) for level in levels]
            total = functools.reduce(jnp.add, shares)
            spread = jnp.concatenate([eye * (share / total) for share in shares], axis=1)
            at = base + slot * SEG
            stacked = jnp.concatenate([part[at : at + SEG, :] for part in parts], axis=0)
            mixed = jnp.dot(spread.astype(jnp.bfloat16), stacked, preferred_element_type=jnp.float32)
            out_ref[slot, :, head * HEAD_DIM : (head + 1) * HEAD_DIM] = mixed.astype(jnp.bfloat16)


def combine(blocks):
    return pl.pallas_call(
        combine_kernel,
        out_shape=jax.ShapeDtypeStruct((4, SEG, 3 * HEAD_DIM), jnp.bfloat16),
        in_specs=[VMEM] * len(blocks),
        out_specs=VMEM,
        compiler_params=pltpu.CompilerParams(vmem_limit_bytes=32 << 20),
    )(*blocks)


def spread_pairs(a, b):
    pairs = []
    for z in range(4):
        for c in range(2):
            target = (2 * c + ((z % 2) ^ a)) * 2 + ((z // 2) ^ b)
            pairs.append((z * 2 + c, target))
    return pairs


def turn(step):
    return [(n, (n + step) % 4) for n in range(4)]


def body(tokens, clip_id, w_qkv, w_out):
    z, y, x, c = [lax.axis_index(name) for name in ("z", "y", "x", "core")]
    zl, zh = z % 2, z // 2
    swap = [(0, 1), (1, 0)]
    info = jnp.stack([zl, y, x, c, zh]).astype(jnp.int32)

    halves = clip_id.reshape(2, SEG)
    counts = jnp.stack([jnp.sum(halves < 1, axis=1), jnp.sum(halves < 2, axis=1)], axis=1)
    counts = jnp.pad(counts.astype(jnp.bfloat16), ((0, 0), (0, HEAD_DIM - 2)))
    blank = jnp.zeros((15, HEAD_DIM), jnp.bfloat16)
    header = jnp.stack(
        [jnp.concatenate([counts[:1], blank]), jnp.concatenate([counts[1:], blank]), jnp.concatenate([counts, blank[1:]])]
    )

    other = lax.ppermute(tokens, "core", swap)
    both = jnp.where(c == 0, jnp.concatenate([tokens, other], 1), jnp.concatenate([other, tokens], 1))
    own_q = jnp.dot(both, w_qkv[0], preferred_element_type=jnp.float32) * (1.0 / math.sqrt(HEAD_DIM))
    own_kv = jnp.einsum("td,sdc->stc", both, w_qkv[1:], preferred_element_type=jnp.float32)

    leaving = small_call(
        send_queries_kernel, SEG + 16, 384, [own_q.astype(jnp.bfloat16), header], (), info, 4
    )
    q_in = [lax.ppermute(block, ("z", "core"), spread_pairs(a, b)) for block, (a, b) in zip(leaving, SLOTS)]
    leaving = small_call(send_pairs_kernel, 528, 384, [own_kv.astype(jnp.bfloat16), header], q_in, info, 2)
    kv_in = [lax.ppermute(block, ("z", "core"), spread_pairs(a, 0)) for a, block in enumerate(leaving)]
    [mine] = small_call(queries_kernel, 4 * SEG + 16, 384, q_in, leaving[:1])
    queries = [mine] + [lax.ppermute(mine, "x", turn(step)) for step in (1, 2, 3)]

    def key_blocks(head, after=()):
        [own] = small_call(functools.partial(pairs_kernel, head), 1056, HEAD_DIM, kv_in, after)
        return [own] + [lax.ppermute(own, "y", turn(step)) for step in (1, 2, 3)]

    def merged(blocks, after=()):
        [near] = small_call(merge_kernel, KEYS + 128, HEAD_DIM, blocks, after, info)
        return near, lax.ppermute(near, "core", swap)

    kv = key_blocks(0, queries[:1])
    kv_next = key_blocks(1, kv[1:])
    part = attend(0, info, queries, *merged(kv, queries[1:]))
    kv_last = key_blocks(2, (*kv_next[1:], part[0]))
    part = attend(1, info, queries, *merged(kv_next, part[:1]), part)
    last = attend(2, info, queries, *merged(kv_last, part[:1]))
    results = []
    for blocks in (part, last):
        results.append(blocks[0])
        for step in (1, 2, 3):
            results.append(lax.ppermute(blocks[step], "x", turn(step)))
    mixed = combine(results)

    back = []
    for index, (a, b) in enumerate(SLOTS):
        returns = [(target, source) for source, target in spread_pairs(a, b)]
        back.append(lax.ppermute(mixed[index], ("z", "core"), returns))
    rows = []
    for half in range(2):
        by_a = [jnp.where(zh == half, back[2 * a], back[2 * a + 1]) for a in range(2)]
        rows.append(
            jnp.concatenate([jnp.where(zl == 0, by_a[0], by_a[1]), jnp.where(zl == 0, by_a[1], by_a[0])], 1)
        )
    attended = jnp.concatenate(rows, axis=0)
    half_cols = w_out.shape[1] // 2
    w_there = lax.dynamic_slice(w_out, (0, (1 - c) * half_cols), (w_out.shape[0], half_cols))
    w_here = lax.dynamic_slice(w_out, (0, c * half_cols), (w_out.shape[0], half_cols))
    there = jnp.dot(attended, w_there, preferred_element_type=jnp.float32).astype(jnp.bfloat16)
    received = lax.ppermute(there, "core", swap)
    here = jnp.dot(attended, w_here, preferred_element_type=jnp.float32)
    return (here + received.astype(jnp.float32)).astype(jnp.bfloat16)


def solution(mesh):
    fine = Mesh(mesh.devices.reshape(4, 4, 4, 2), ("z", "y", "x", "core"))
    seq = ("z", "y", "x")
    in_specs = (P(seq, "core"), P(seq), P(None, None, "core"), P("core", None))
    return jax.shard_map(body, mesh=fine, in_specs=in_specs, out_specs=P(seq, "core"), check_vma=False)
```

```python
import functools
import math

import jax
import jax.numpy as jnp
from jax import lax
from jax.experimental import pallas as pl
from jax.experimental.pallas import tpu as pltpu
from jax.sharding import Mesh
from jax.sharding import PartitionSpec as P

HEAD_DIM = 128
SEG = 128
TILE = 512
KEYS = 4096
NEG = -1e30
FLOOR = -1e29
WIDTHS = (768, 1536, 2048, 2688, 3328, 4096)
VMEM = pl.BlockSpec(memory_space=pltpu.VMEM)
SMEM = pl.BlockSpec(memory_space=pltpu.SMEM)


def send_kernel(parts, info, own_ref, header, *refs):
    out_refs, zl = refs[-2:], info[0]
    for a, out_ref in enumerate(out_refs):
        for group in range(2):

            @pl.when((zl ^ a) == group)
            def _():
                for n in range(parts):
                    out_ref[n * 256 : (n + 1) * 256, :] = own_ref[n, :, group * 384 : (group + 1) * 384]

        for n in range(3):
            out_ref[parts * 256 :, n * HEAD_DIM : (n + 1) * HEAD_DIM] = header[...]


def queries_kernel(*refs):
    blocks, q_ref = refs[:2], refs[-1]
    for a, block in enumerate(blocks):
        q_ref[a * 256 : (a + 1) * 256, :] = block[:256, :]
        q_ref[512 + 16 * a : 512 + 16 * (a + 1), :] = block[256:, :]


def pairs_kernel(place, *refs):
    blocks, kv_ref = refs[:2], refs[-1]
    cols = slice(place * HEAD_DIM, (place + 1) * HEAD_DIM)
    for a, block in enumerate(blocks):
        kv_ref[a * 512 : (a + 1) * 512, :] = block[:512, cols]
        kv_ref[1024 + 16 * a : 1024 + 16 * (a + 1), :] = block[512:, cols]


def merge_kernel(info, *refs):
    blocks, out_ref = refs[:4], refs[-1]
    zl, y = info[0], info[1]
    for step, block in enumerate(blocks):
        for a in range(2):
            at = pl.multiple_of(((zl ^ a) * 4 + ((y - step) & 3)) * 256, 256)
            out_ref[pl.ds(at, 256), :] = block[a * 512 : a * 512 + 256, :]
            out_ref[pl.ds(2048 + at, 256), :] = block[a * 512 + 256 : a * 512 + 512, :]
        out_ref[4096 + 32 * step : 4096 + 32 * (step + 1), :] = block[1024:, :]


def small_call(kernel, rows, cols, operands, after=(), info=None, outs=1):
    lead = [] if info is None else [info]
    return pl.pallas_call(
        kernel,
        out_shape=[jax.ShapeDtypeStruct((rows, cols), jnp.bfloat16)] * outs,
        in_specs=[SMEM] * len(lead) + [VMEM] * len(operands) + [pl.BlockSpec(memory_space=pl.ANY)] * len(after),
        out_specs=[VMEM] * outs,
        compiler_params=pltpu.CompilerParams(vmem_limit_bytes=32 << 20),
    )(*lead, *operands, *after)


def attend_kernel(head, info, *refs):
    q_refs, (near, far), refs = refs[:4], refs[4:6], refs[6:]
    before, refs = (refs[:4], refs[4:]) if head == 1 else ((), refs[-11:])
    o_refs, (queries, keys, vals, scores, tops, sums, flat) = refs[:4], refs[4:]
    base = 0
    for old, o_ref in zip(before, o_refs):
        base = old.shape[0]
        o_ref[:base, :] = old[...]
    zl, y, x, c = [info[n] for n in range(4)]
    lane = lax.broadcasted_iota(jnp.int32, (SEG, HEAD_DIM), 1)
    row = lax.broadcasted_iota(jnp.int32, (SEG, HEAD_DIM), 0)

    def bounds(lines):
        found = sum(line.astype(jnp.float32) for line in lines)
        return [
            jnp.sum(jnp.where(lane[:16] == n, found, 0.0), keepdims=True)[0, 0].astype(jnp.int32)
            for n in range(2)
        ]

    n1, n2 = bounds([ref[KEYS + 16 * n : KEYS + 16 * (n + 1), :] for ref in (near, far) for n in range(8)])
    m1, m2 = bounds([ref[512 + 16 * n : 528 + 16 * n, :HEAD_DIM] for ref in q_refs for n in range(2)])

    def clip_of(index, first, second):
        return (index >= first).astype(jnp.int32) + (index >= second).astype(jnp.int32)

    for n in range(KEYS // SEG):
        own = clip_of(row + n * SEG, n1, n2) == lane
        keys[n * SEG : (n + 1) * SEG, HEAD_DIM:] = own.astype(jnp.float32).astype(jnp.bfloat16)
    for n in range(2048 // SEG):
        differs = (clip_of(row + n * SEG, m1, m2) != lane) & (lane < 3)
        queries[n * SEG : (n + 1) * SEG, HEAD_DIM:] = jnp.where(differs, NEG, 0.0).astype(jnp.bfloat16)
    vals[:, HEAD_DIM:] = jnp.ones((KEYS, HEAD_DIM), jnp.bfloat16)
    cols = slice(head * HEAD_DIM, (head + 1) * HEAD_DIM)
    for step in range(4):
        xx = (x - step) & 3
        for a in range(2):
            zz = 2 * (c ^ (xx & 1)) + (zl ^ a)
            at = pl.multiple_of(zz * TILE + (xx >> 1) * 256, 256)
            queries[pl.ds(at, 256), :HEAD_DIM] = q_refs[step][a * 256 : (a + 1) * 256, cols]
    zh = c ^ (x & 1)
    for part, ref in ((zh, near), (1 - zh, far)):
        at = pl.ds(pl.multiple_of(part * 2048, 2048), 2048)
        keys[at, :HEAD_DIM] = ref[:2048, :]
        vals[at, :HEAD_DIM] = ref[2048:4096, :]

    eye = (lane == row).astype(jnp.float32)

    def tile(zz, carry):
        first, last = zz * TILE, zz * TILE + TILE - 1
        low = jnp.where(first >= m2, n2, jnp.where(first >= m1, n1, 0))
        high = jnp.where(last >= m2, KEYS, jnp.where(last >= m1, n2, n1))
        low = (low // SEG) * SEG
        need = high - low
        rows = pl.ds(pl.multiple_of(first, TILE), TILE)
        tops[...] = jnp.full((TILE, HEAD_DIM), NEG, jnp.float32)
        sums[...] = jnp.zeros((TILE, 2 * HEAD_DIM), jnp.float32)

        def runs(k):
            under = WIDTHS[k - 1] if k else 0
            return ((need > under) & (need <= WIDTHS[k])).astype(jnp.int32)

        for k, width in enumerate(WIDTHS):
            at = pl.multiple_of(jnp.minimum(low, KEYS - width), SEG)

            def first_pass(i, carry, width=width, at=at):
                s = lax.dot_general(
                    queries[rows, :],
                    keys[pl.ds(at, width), :],
                    (((1,), (1,)), ((), ())),
                    preferred_element_type=jnp.float32,
                )
                scores[:, :width] = s
                top = s[:, :128]
                for n in range(1, width // 128):
                    top = jnp.maximum(top, s[:, n * 128 : (n + 1) * 128])
                tops[...] = top
                return carry

            lax.fori_loop(0, runs(k), first_pass, 0)

        top = jnp.maximum(jnp.max(tops[...], axis=1, keepdims=True), FLOOR)

        for k, width in enumerate(WIDTHS):
            at = pl.multiple_of(jnp.minimum(low, KEYS - width), SEG)

            def second_pass(i, carry, width=width, at=at):
                weights = jnp.exp(scores[:, :width] - top).astype(jnp.bfloat16)
                sums[...] = jnp.dot(weights, vals[pl.ds(at, width), :], preferred_element_type=jnp.float32)
                return carry

            lax.fori_loop(0, runs(k), second_pass, 0)

        total = jnp.maximum(sums[:, HEAD_DIM:], 1e-30)
        flat[...] = (sums[:, :HEAD_DIM] / total).astype(jnp.bfloat16)
        tops[...] = top + jnp.log(total)
        a = (zz & 1) ^ zl
        for step in range(4):
            xx = (x + step) & 3

            @pl.when((xx & 1) == ((zz >> 1) ^ c))
            def _():
                for half in range(2):
                    at = pl.ds(pl.multiple_of((xx >> 1) * 256 + half * SEG, SEG), SEG)
                    to = pl.multiple_of(base + a * 256 + half * SEG, 64)
                    o_refs[step][pl.ds(to, SEG), :] = flat[at, :]
                    line = jnp.sum(tops[at, :] * eye, axis=0, keepdims=True)
                    big = line.astype(jnp.bfloat16).astype(jnp.float32)
                    middle = (line - big).astype(jnp.bfloat16).astype(jnp.float32)
                    rest = line - big - middle
                    sub = lax.broadcasted_iota(jnp.int32, (16, 128), 0)
                    parts = jnp.where(
                        sub == 0, big, jnp.where(sub == 1, middle, jnp.where(sub == 2, rest, 0.0))
                    )
                    to = pl.multiple_of(base + 512 + (2 * a + half) * 16, 16)
                    o_refs[step][pl.ds(to, 16), :] = parts.astype(jnp.bfloat16)

        return carry

    lax.fori_loop(0, 4, tile, 0)


def attend(head, info, queries, near, far, before=(), after=()):
    return pl.pallas_call(
        functools.partial(attend_kernel, head),
        out_shape=[jax.ShapeDtypeStruct(((2 if before else 1) * (4 * SEG + 64), HEAD_DIM), jnp.bfloat16)] * 4,
        in_specs=[SMEM] + [VMEM] * (6 + len(before)) + [pl.BlockSpec(memory_space=pl.ANY)] * len(after),
        out_specs=[VMEM] * 4,
        scratch_shapes=[
            pltpu.VMEM((2048, 2 * HEAD_DIM), jnp.bfloat16),
            pltpu.VMEM((KEYS, 2 * HEAD_DIM), jnp.bfloat16),
            pltpu.VMEM((KEYS, 2 * HEAD_DIM), jnp.bfloat16),
            pltpu.VMEM((TILE, KEYS), jnp.float32),
            pltpu.VMEM((TILE, HEAD_DIM), jnp.float32),
            pltpu.VMEM((TILE, 2 * HEAD_DIM), jnp.float32),
            pltpu.VMEM((TILE, HEAD_DIM), jnp.bfloat16),
        ],
        compiler_params=pltpu.CompilerParams(vmem_limit_bytes=48 << 20),
        cost_estimate=pl.CostEstimate(
            flops=2 * 2 * 2048 * 4096 * 128, bytes_accessed=4 << 20, transcendentals=2048 * 4096
        ),
    )(info, *queries, near, far, *before, *after)


def combine_kernel(*refs):
    out_ref = refs[-1]
    eye = (
        lax.broadcasted_iota(jnp.int32, (SEG, SEG), 0)
        == lax.broadcasted_iota(jnp.int32, (SEG, SEG), 1)
    ).astype(jnp.float32)
    for head in range(3):
        parts = refs[:4] if head < 2 else refs[4:8]
        base = 4 * SEG + 64 if head == 1 else 0
        for slot in range(4):
            levels = []
            for part in parts:
                at = base + 4 * SEG + slot * 16
                lines = part[at : at + 16, :].astype(jnp.float32)
                levels.append(jnp.sum(lines, axis=0, keepdims=True))
            top = functools.reduce(jnp.maximum, levels)
            shares = [jnp.exp(level - top) for level in levels]
            total = functools.reduce(jnp.add, shares)
            spread = jnp.concatenate([eye * (share / total) for share in shares], axis=1)
            at = base + slot * SEG
            stacked = jnp.concatenate([part[at : at + SEG, :] for part in parts], axis=0)
            mixed = jnp.dot(spread.astype(jnp.bfloat16), stacked, preferred_element_type=jnp.float32)
            out_ref[slot, :, head * HEAD_DIM : (head + 1) * HEAD_DIM] = mixed.astype(jnp.bfloat16)


def combine(blocks):
    return pl.pallas_call(
        combine_kernel,
        out_shape=jax.ShapeDtypeStruct((4, SEG, 3 * HEAD_DIM), jnp.bfloat16),
        in_specs=[VMEM] * len(blocks),
        out_specs=VMEM,
        compiler_params=pltpu.CompilerParams(vmem_limit_bytes=32 << 20),
    )(*blocks)


def outward_kernel(info, first_ref, second_ref, w_ref, *refs):
    out_ref, zl = refs[-1], info[0]
    total = 0.0
    for a, block in enumerate((first_ref, second_ref)):
        rows = pl.ds(pl.multiple_of((zl ^ a) * 384, 384), 384)
        total += jnp.dot(block[...], w_ref[rows, :], preferred_element_type=jnp.float32)
    out_ref[...] = total.astype(out_ref.dtype)


def outward(other_half, dtype, info, blocks, w_out, after=()):
    depth, width = w_out.shape[0], w_out.shape[1] // 2
    whole = lambda n, info_ref: (0, 0)
    grid_spec = pltpu.PrefetchScalarGridSpec(
        num_scalar_prefetch=1,
        grid=(1,),
        in_specs=[pl.BlockSpec((256, 384), whole)] * 2
        + [pl.BlockSpec((depth, width), lambda n, info_ref: (0, info_ref[3] ^ other_half))]
        + [pl.BlockSpec(memory_space=pl.ANY)] * len(after),
        out_specs=pl.BlockSpec((256, width), whole),
    )
    return pl.pallas_call(
        outward_kernel,
        grid_spec=grid_spec,
        out_shape=jax.ShapeDtypeStruct((256, width), dtype),
        compiler_params=pltpu.CompilerParams(vmem_limit_bytes=40 << 20),
        cost_estimate=pl.CostEstimate(
            flops=2 * 256 * depth * width, bytes_accessed=2 * depth * width, transcendentals=0
        ),
    )(info, *blocks, w_out, *after)


def spread_pairs(a):
    pairs = []
    for z in range(4):
        for x in range(4):
            for c in range(2):
                target = 2 * c + ((z % 2) ^ a)
                pairs.append(((z * 4 + x) * 2 + c, (target * 4 + x) * 2 + ((z // 2) ^ (x % 2))))
    return pairs


def turn(step):
    return [(n, (n + step) % 4) for n in range(4)]


def body(tokens, clip_id, w_qkv, w_out):
    z, y, x, c = [lax.axis_index(name) for name in ("z", "y", "x", "core")]
    zl, zh = z % 2, z // 2
    swap = [(0, 1), (1, 0)]
    info = jnp.stack([zl, y, x, c, zh]).astype(jnp.int32)

    halves = clip_id.reshape(2, SEG)
    counts = jnp.stack([jnp.sum(halves < 1, axis=1), jnp.sum(halves < 2, axis=1)], axis=1)
    header = jnp.pad(counts.astype(jnp.bfloat16), ((0, 14), (0, HEAD_DIM - 2)))

    other = lax.ppermute(tokens, "core", swap)
    both = jnp.where(c == 0, jnp.concatenate([tokens, other], 1), jnp.concatenate([other, tokens], 1))
    own_kv = jnp.einsum("td,sdc->stc", both, w_qkv[1:], preferred_element_type=jnp.float32)
    own_q = jnp.einsum("td,sdc->stc", both, w_qkv[:1], preferred_element_type=jnp.float32)
    own_q = own_q * (1.0 / math.sqrt(HEAD_DIM))

    def to_group(parts, own, after):
        kernel = functools.partial(send_kernel, parts)
        blocks = small_call(kernel, parts * 256 + 16, 384, [own.astype(jnp.bfloat16), header], after, info, 2)
        moved = [lax.ppermute(block, ("z", "x", "core"), spread_pairs(a)) for a, block in enumerate(blocks)]
        return blocks, moved

    _, q_in = to_group(1, own_q, ())
    leaving, kv_in = to_group(2, own_kv, q_in)
    [mine] = small_call(queries_kernel, 544, 384, q_in, leaving[:1])
    queries = [mine] + [lax.ppermute(mine, "x", turn(step)) for step in (1, 2, 3)]
    def key_blocks(head, after=()):
        [own] = small_call(functools.partial(pairs_kernel, head), 1056, HEAD_DIM, kv_in, after)
        return [own] + [lax.ppermute(own, "y", turn(step)) for step in (1, 2, 3)]

    def merged(blocks, after=()):
        [near] = small_call(merge_kernel, KEYS + 128, HEAD_DIM, blocks, after, info)
        return near, lax.ppermute(near, "core", swap)

    kv = key_blocks(0, queries[:1])
    kv_next = key_blocks(1, kv[1:])
    part = attend(0, info, queries, *merged(kv, queries[1:]))
    kv_last = key_blocks(2, (*kv_next[1:], part[0]))
    part = attend(1, info, queries, *merged(kv_next, part[:1]), part)
    last = attend(2, info, queries, *merged(kv_last, part[:1]))
    results = []
    for blocks in (part, last):
        results.append(blocks[0])
        for step in (1, 2, 3):
            results.append(lax.ppermute(blocks[step], "x", turn(step)))
    mixed = combine(results)

    back = []
    for a in range(2):
        returns = [(target, source) for source, target in spread_pairs(a)]
        block = mixed[2 * a : 2 * a + 2].reshape(256, 384)
        back.append(lax.ppermute(block, ("z", "x", "core"), returns))
    there = outward(1, jnp.bfloat16, info, back, w_out)
    received = lax.ppermute(there, "core", swap)
    here = outward(0, jnp.float32, info, back, w_out, (there,))
    return (here + received.astype(jnp.float32)).astype(jnp.bfloat16)


def solution(mesh):
    fine = Mesh(mesh.devices.reshape(4, 4, 4, 2), ("z", "y", "x", "core"))
    seq = ("z", "y", "x")
    in_specs = (P(seq, "core"), P(seq), P(None, None, "core"), P("core", None))
    return jax.shard_map(body, mesh=fine, in_specs=in_specs, out_specs=P(seq, "core"), check_vma=False)
```

```python
import functools
import math

import jax
import jax.numpy as jnp
from jax import lax
from jax.experimental import pallas as pl
from jax.experimental.pallas import tpu as pltpu
from jax.sharding import Mesh
from jax.sharding import PartitionSpec as P

HEAD_DIM = 128
SEG = 128
TILE = 512
KEYS = 4096
NEG = -1e30
FLOOR = -1e29
WIDTHS = (768, 1536, 2048, 2688, 3328, 4096)
VMEM = pl.BlockSpec(memory_space=pltpu.VMEM)
SMEM = pl.BlockSpec(memory_space=pltpu.SMEM)


def send_kernel(info, q_ref, kv_ref, header, *refs):
    out_refs, zl = refs[-2:], info[0]
    for a, out_ref in enumerate(out_refs):
        for group in range(2):

            @pl.when((zl ^ a) == group)
            def _():
                cols = slice(group * 384, (group + 1) * 384)
                out_ref[:256, :] = q_ref[0, :, cols]
                out_ref[256:512, :] = kv_ref[0, :, cols]
                out_ref[512:768, :] = kv_ref[1, :, cols]

        for n in range(3):
            out_ref[768:, n * HEAD_DIM : (n + 1) * HEAD_DIM] = header[...]


def queries_kernel(*refs):
    blocks, q_ref = refs[:2], refs[-1]
    for a, block in enumerate(blocks):
        q_ref[a * 256 : (a + 1) * 256, :] = block[:256, :]
        q_ref[512 + 16 * a : 512 + 16 * (a + 1), :] = block[768:, :]


def pairs_kernel(place, *refs):
    blocks, kv_ref = refs[:2], refs[-1]
    cols = slice(place * HEAD_DIM, (place + 1) * HEAD_DIM)
    for a, block in enumerate(blocks):
        kv_ref[a * 512 : (a + 1) * 512, :] = block[256:768, cols]
        kv_ref[1024 + 16 * a : 1024 + 16 * (a + 1), :] = block[768:, cols]


def merge_kernel(info, *refs):
    blocks, out_ref = refs[:4], refs[-1]
    zl, y = info[0], info[1]
    for step, block in enumerate(blocks):
        for a in range(2):
            at = pl.multiple_of(((zl ^ a) * 4 + ((y - step) & 3)) * 256, 256)
            out_ref[pl.ds(at, 256), :] = block[a * 512 : a * 512 + 256, :]
            out_ref[pl.ds(2048 + at, 256), :] = block[a * 512 + 256 : a * 512 + 512, :]
        out_ref[4096 + 32 * step : 4096 + 32 * (step + 1), :] = block[1024:, :]


def small_call(kernel, rows, cols, operands, after=(), info=None, outs=1):
    lead = [] if info is None else [info]
    return pl.pallas_call(
        kernel,
        out_shape=[jax.ShapeDtypeStruct((rows, cols), jnp.bfloat16)] * outs,
        in_specs=[SMEM] * len(lead) + [VMEM] * len(operands) + [pl.BlockSpec(memory_space=pl.ANY)] * len(after),
        out_specs=[VMEM] * outs,
        compiler_params=pltpu.CompilerParams(vmem_limit_bytes=32 << 20),
    )(*lead, *operands, *after)


def attend_kernel(head, info, *refs):
    q_refs, (near, far), refs = refs[:4], refs[4:6], refs[6:]
    before, refs = (refs[:4], refs[4:]) if head == 1 else ((), refs[-12:])
    o_refs, (queries, keys, vals, scores, tops, sums, flat, outs) = refs[:4], refs[4:]
    base = 0
    for old, o_ref in zip(before, o_refs):
        base = old.shape[0]
        o_ref[:base, :] = old[...]
    zl, y, x, c = [info[n] for n in range(4)]
    lane = lax.broadcasted_iota(jnp.int32, (SEG, HEAD_DIM), 1)
    row = lax.broadcasted_iota(jnp.int32, (SEG, HEAD_DIM), 0)

    def bounds(lines):
        found = sum(line.astype(jnp.float32) for line in lines)
        return [
            jnp.sum(jnp.where(lane[:16] == n, found, 0.0), keepdims=True)[0, 0].astype(jnp.int32)
            for n in range(2)
        ]

    n1, n2 = bounds([ref[KEYS + 16 * n : KEYS + 16 * (n + 1), :] for ref in (near, far) for n in range(8)])
    m1, m2 = bounds([ref[512 + 16 * n : 528 + 16 * n, :HEAD_DIM] for ref in q_refs for n in range(2)])

    def clip_of(index, first, second):
        return (index >= first).astype(jnp.int32) + (index >= second).astype(jnp.int32)

    for n in range(KEYS // SEG):
        own = clip_of(row + n * SEG, n1, n2) == lane
        keys[n * SEG : (n + 1) * SEG, HEAD_DIM:] = own.astype(jnp.float32).astype(jnp.bfloat16)
    for n in range(2048 // SEG):
        differs = (clip_of(row + n * SEG, m1, m2) != lane) & (lane < 3)
        queries[n * SEG : (n + 1) * SEG, HEAD_DIM:] = jnp.where(differs, NEG, 0.0).astype(jnp.bfloat16)
    vals[:, HEAD_DIM:] = jnp.ones((KEYS, HEAD_DIM), jnp.bfloat16)
    cols = slice(head * HEAD_DIM, (head + 1) * HEAD_DIM)
    for step in range(4):
        xx = (x - step) & 3
        for a in range(2):
            zz = 2 * ((1 - c) ^ (xx & 1)) + (zl ^ a)
            at = pl.multiple_of(zz * TILE + (xx >> 1) * 256, 256)
            queries[pl.ds(at, 256), :HEAD_DIM] = q_refs[step][a * 256 : (a + 1) * 256, cols]
    zh = (1 - c) ^ (x & 1)
    for part, ref in ((zh, near), (1 - zh, far)):
        at = pl.ds(pl.multiple_of(part * 2048, 2048), 2048)
        keys[at, :HEAD_DIM] = ref[:2048, :]
        vals[at, :HEAD_DIM] = ref[2048:4096, :]

    eye = (lane == row).astype(jnp.float32)
    sub = lax.broadcasted_iota(jnp.int32, (16, HEAD_DIM), 0)

    def tile(zz, carry):
        first, last = zz * TILE, zz * TILE + TILE - 1
        low = jnp.where(first >= m2, n2, jnp.where(first >= m1, n1, 0))
        high = jnp.where(last >= m2, KEYS, jnp.where(last >= m1, n2, n1))
        low = (low // SEG) * SEG
        need = high - low
        rows = pl.ds(pl.multiple_of(first, TILE), TILE)
        tops[...] = jnp.full((TILE, HEAD_DIM), NEG, jnp.float32)
        sums[...] = jnp.zeros((TILE, 2 * HEAD_DIM), jnp.float32)

        def runs(k):
            under = WIDTHS[k - 1] if k else 0
            return ((need > under) & (need <= WIDTHS[k])).astype(jnp.int32)

        for k, width in enumerate(WIDTHS):
            at = pl.multiple_of(jnp.minimum(low, KEYS - width), SEG)

            def first_pass(i, carry, width=width, at=at):
                s = lax.dot_general(
                    queries[rows, :],
                    keys[pl.ds(at, width), :],
                    (((1,), (1,)), ((), ())),
                    preferred_element_type=jnp.float32,
                )
                scores[:, :width] = s
                top = s[:, :128]
                for n in range(1, width // 128):
                    top = jnp.maximum(top, s[:, n * 128 : (n + 1) * 128])
                tops[...] = top
                return carry

            lax.fori_loop(0, runs(k), first_pass, 0)

        top = jnp.maximum(jnp.max(tops[...], axis=1, keepdims=True), FLOOR)

        for k, width in enumerate(WIDTHS):
            at = pl.multiple_of(jnp.minimum(low, KEYS - width), SEG)

            def second_pass(i, carry, width=width, at=at):
                weights = jnp.exp(scores[:, :width] - top).astype(jnp.bfloat16)
                sums[...] = jnp.dot(weights, vals[pl.ds(at, width), :], preferred_element_type=jnp.float32)
                return carry

            lax.fori_loop(0, runs(k), second_pass, 0)

        total = jnp.maximum(sums[:, HEAD_DIM:], 1e-30)
        flat[...] = (sums[:, :HEAD_DIM] / total).astype(jnp.bfloat16)
        tops[...] = top + jnp.log(total)
        a = (zz & 1) ^ zl
        for pair in range(2):
            xx = ((zz >> 1) ^ (1 - c)) + 2 * pair
            step = (xx - x) & 3
            for half in range(2):
                at = slice(pair * 256 + half * SEG, pair * 256 + (half + 1) * SEG)
                to = pl.multiple_of(a * 256 + half * SEG, SEG)
                outs[step, pl.ds(to, SEG), :] = flat[at, :]
                line = jnp.sum(tops[at, :] * eye, axis=0, keepdims=True)
                big = line.astype(jnp.bfloat16).astype(jnp.float32)
                middle = (line - big).astype(jnp.bfloat16).astype(jnp.float32)
                rest = line - big - middle
                parts = jnp.where(sub == 0, big, jnp.where(sub == 1, middle, jnp.where(sub == 2, rest, 0.0)))
                to = pl.multiple_of(512 + (2 * a + half) * 16, 16)
                outs[step, pl.ds(to, 16), :] = parts.astype(jnp.bfloat16)
        return carry

    lax.fori_loop(0, 4, tile, 0)
    for step in range(4):
        o_refs[step][base:, :] = outs[step]


def attend(head, info, queries, near, far, before=(), after=()):
    return pl.pallas_call(
        functools.partial(attend_kernel, head),
        out_shape=[jax.ShapeDtypeStruct(((2 if before else 1) * (4 * SEG + 64), HEAD_DIM), jnp.bfloat16)] * 4,
        in_specs=[SMEM] + [VMEM] * (6 + len(before)) + [pl.BlockSpec(memory_space=pl.ANY)] * len(after),
        out_specs=[VMEM] * 4,
        scratch_shapes=[
            pltpu.VMEM((2048, 2 * HEAD_DIM), jnp.bfloat16),
            pltpu.VMEM((KEYS, 2 * HEAD_DIM), jnp.bfloat16),
            pltpu.VMEM((KEYS, 2 * HEAD_DIM), jnp.bfloat16),
            pltpu.VMEM((TILE, KEYS), jnp.float32),
            pltpu.VMEM((TILE, HEAD_DIM), jnp.float32),
            pltpu.VMEM((TILE, 2 * HEAD_DIM), jnp.float32),
            pltpu.VMEM((TILE, HEAD_DIM), jnp.bfloat16),
            pltpu.VMEM((4, 4 * SEG + 64, HEAD_DIM), jnp.bfloat16),
        ],
        compiler_params=pltpu.CompilerParams(vmem_limit_bytes=48 << 20),
        cost_estimate=pl.CostEstimate(
            flops=2 * 2 * 2048 * 4096 * 128, bytes_accessed=4 << 20, transcendentals=2048 * 4096
        ),
    )(info, *queries, near, far, *before, *after)


def combine_kernel(*refs):
    out_ref = refs[-1]
    eye = (
        lax.broadcasted_iota(jnp.int32, (SEG, SEG), 0)
        == lax.broadcasted_iota(jnp.int32, (SEG, SEG), 1)
    ).astype(jnp.float32)
    for head in range(3):
        parts = refs[:4] if head < 2 else refs[4:8]
        base = 4 * SEG + 64 if head == 1 else 0
        for slot in range(4):
            levels = []
            for part in parts:
                at = base + 4 * SEG + slot * 16
                lines = part[at : at + 16, :].astype(jnp.float32)
                levels.append(jnp.sum(lines, axis=0, keepdims=True))
            top = functools.reduce(jnp.maximum, levels)
            shares = [jnp.exp(level - top) for level in levels]
            total = functools.reduce(jnp.add, shares)
            spread = jnp.concatenate([eye * (share / total) for share in shares], axis=1)
            at = base + slot * SEG
            stacked = jnp.concatenate([part[at : at + SEG, :] for part in parts], axis=0)
            mixed = jnp.dot(spread.astype(jnp.bfloat16), stacked, preferred_element_type=jnp.float32)
            out_ref[slot, :, head * HEAD_DIM : (head + 1) * HEAD_DIM] = mixed.astype(jnp.bfloat16)


def combine(blocks):
    return pl.pallas_call(
        combine_kernel,
        out_shape=jax.ShapeDtypeStruct((4, SEG, 3 * HEAD_DIM), jnp.bfloat16),
        in_specs=[VMEM] * len(blocks),
        out_specs=VMEM,
        compiler_params=pltpu.CompilerParams(vmem_limit_bytes=32 << 20),
    )(*blocks)


def outward_kernel(info, first_ref, second_ref, w_ref, *refs):
    out_ref, zl = refs[-1], info[0]
    total = 0.0
    for a, block in enumerate((first_ref, second_ref)):
        rows = pl.ds(pl.multiple_of((zl ^ a) * 384, 384), 384)
        total += jnp.dot(block[...], w_ref[rows, :], preferred_element_type=jnp.float32)
    out_ref[...] = total.astype(out_ref.dtype)


def outward(other_half, dtype, info, blocks, w_out, after=()):
    depth, width = w_out.shape[0], w_out.shape[1] // 2
    whole = lambda n, info_ref: (0, 0)
    grid_spec = pltpu.PrefetchScalarGridSpec(
        num_scalar_prefetch=1,
        grid=(1,),
        in_specs=[pl.BlockSpec((256, 384), whole)] * 2
        + [pl.BlockSpec((depth, width), lambda n, info_ref: (0, info_ref[3] ^ other_half))]
        + [pl.BlockSpec(memory_space=pl.ANY)] * len(after),
        out_specs=pl.BlockSpec((256, width), whole),
    )
    return pl.pallas_call(
        outward_kernel,
        grid_spec=grid_spec,
        out_shape=jax.ShapeDtypeStruct((256, width), dtype),
        compiler_params=pltpu.CompilerParams(vmem_limit_bytes=40 << 20),
        cost_estimate=pl.CostEstimate(
            flops=2 * 256 * depth * width, bytes_accessed=2 * depth * width, transcendentals=0
        ),
    )(info, *blocks, w_out, *after)


def spread_pairs(a):
    pairs = []
    for z in range(4):
        for x in range(4):
            for c in range(2):
                target = 2 * c + ((z % 2) ^ a)
                pairs.append(((z * 4 + x) * 2 + c, (target * 4 + x) * 2 + ((1 - z // 2) ^ (x % 2))))
    return pairs


def turn(step):
    return [(n, (n + step) % 4) for n in range(4)]


def body(tokens, clip_id, w_qkv, w_out):
    z, y, x, c = [lax.axis_index(name) for name in ("z", "y", "x", "core")]
    zl, zh = z % 2, z // 2
    swap = [(0, 1), (1, 0)]
    info = jnp.stack([zl, y, x, c, zh]).astype(jnp.int32)

    halves = clip_id.reshape(2, SEG)
    counts = jnp.stack([jnp.sum(halves < 1, axis=1), jnp.sum(halves < 2, axis=1)], axis=1)
    header = jnp.pad(counts.astype(jnp.bfloat16), ((0, 14), (0, HEAD_DIM - 2)))

    other = lax.ppermute(tokens, "core", swap)
    both = jnp.where(c == 0, jnp.concatenate([tokens, other], 1), jnp.concatenate([other, tokens], 1))
    own_kv = jnp.einsum("td,sdc->stc", both, w_qkv[1:], preferred_element_type=jnp.float32)
    own_q = jnp.einsum("td,sdc->stc", both, w_qkv[:1], preferred_element_type=jnp.float32)
    own_q = own_q * (1.0 / math.sqrt(HEAD_DIM))

    made = [own_q.astype(jnp.bfloat16), own_kv.astype(jnp.bfloat16), header]
    leaving = small_call(send_kernel, 784, 384, made, (), info, 2)
    arrived = [lax.ppermute(block, ("z", "x", "core"), spread_pairs(a)) for a, block in enumerate(leaving)]
    [mine] = small_call(queries_kernel, 544, 384, arrived)
    queries = [mine] + [lax.ppermute(mine, "x", turn(step)) for step in (1, 2, 3)]

    def key_blocks(head, after):
        [own] = small_call(functools.partial(pairs_kernel, head), 1056, HEAD_DIM, arrived, after)
        return [own] + [lax.ppermute(own, "y", turn(step)) for step in (1, 2, 3)]

    def merged(blocks, after=()):
        [near] = small_call(merge_kernel, KEYS + 128, HEAD_DIM, blocks, after, info)
        return near, lax.ppermute(near, "core", swap)

    kv = key_blocks(0, (mine,))
    kv_next = key_blocks(1, kv[1:])
    part = attend(0, info, queries, *merged(kv, queries[1:]))
    kv_last = key_blocks(2, (*kv_next[1:], part[0]))
    part = attend(1, info, queries, *merged(kv_next, part[:1]), part)
    last = attend(2, info, queries, *merged(kv_last, part[:1]))
    results = []
    for blocks in (part, last):
        results.append(blocks[0])
        for step in (1, 2, 3):
            results.append(lax.ppermute(blocks[step], "x", turn(step)))
    mixed = combine(results)

    back = []
    for a in range(2):
        returns = [(target, source) for source, target in spread_pairs(a)]
        block = mixed[2 * a : 2 * a + 2].reshape(256, 384)
        back.append(lax.ppermute(block, ("z", "x", "core"), returns))
    there = outward(1, jnp.bfloat16, info, back, w_out)
    received = lax.ppermute(there, "core", swap)
    here = outward(0, jnp.float32, info, back, w_out, (there,))
    return (here + received.astype(jnp.float32)).astype(jnp.bfloat16)


def solution(mesh):
    fine = Mesh(mesh.devices.reshape(4, 4, 4, 2), ("z", "y", "x", "core"))
    seq = ("z", "y", "x")
    in_specs = (P(seq, "core"), P(seq), P(None, None, "core"), P("core", None))
    return jax.shard_map(body, mesh=fine, in_specs=in_specs, out_specs=P(seq, "core"), check_vma=False)
```

```python
import functools
import math

import jax
import jax.numpy as jnp
from jax import lax
from jax.experimental import pallas as pl
from jax.experimental.pallas import tpu as pltpu
from jax.sharding import Mesh
from jax.sharding import PartitionSpec as P

HEAD_DIM = 128
SEG = 128
TILE = 512
KEYS = 4096
NEG = -1e30
FLOOR = -1e29
WIDTHS = (768, 1536, 2048, 2688, 3328, 4096)
VMEM = pl.BlockSpec(memory_space=pltpu.VMEM)
SMEM = pl.BlockSpec(memory_space=pltpu.SMEM)


def own_kernel(info, own_ref, w_ref, out_ref):
    out_ref[...] = jnp.dot(own_ref[...], w_ref[0], preferred_element_type=jnp.float32)


def other_kernel(info, other_ref, w_ref, begun, header, *out_refs):
    total = begun[...] + jnp.dot(other_ref[...], w_ref[0], preferred_element_type=jnp.float32)
    made = (total * (1.0 / math.sqrt(HEAD_DIM))).astype(jnp.bfloat16)
    for a, out_ref in enumerate(out_refs):
        for group in range(2):

            @pl.when((info[0] ^ a) == group)
            def _():
                out_ref[:256, :] = made[:, group * 384 : (group + 1) * 384]

        for n in range(3):
            out_ref[256:, n * HEAD_DIM : (n + 1) * HEAD_DIM] = header[...]


def project(kernel, which, info, tokens, w_qkv, operands, shapes):
    depth, width = tokens.shape[1], w_qkv.shape[2]
    whole = lambda n, info_ref: (0, 0)
    grid_spec = pltpu.PrefetchScalarGridSpec(
        num_scalar_prefetch=1,
        grid=(1,),
        in_specs=[
            pl.BlockSpec(tokens.shape, whole),
            pl.BlockSpec((1, depth, width), lambda n, info_ref: (0, info_ref[3] ^ which, 0)),
        ]
        + [pl.BlockSpec(operand.shape, whole) for operand in operands],
        out_specs=[pl.BlockSpec(shape.shape, whole) for shape in shapes],
    )
    return pl.pallas_call(
        kernel,
        grid_spec=grid_spec,
        out_shape=shapes,
        compiler_params=pltpu.CompilerParams(vmem_limit_bytes=32 << 20),
        cost_estimate=pl.CostEstimate(
            flops=2 * 256 * depth * width, bytes_accessed=2 * depth * width, transcendentals=0
        ),
    )(info, tokens, w_qkv, *operands)


def send_kernel(info, own_ref, header, *refs):
    out_refs, zl = refs[-2:], info[0]
    for a, out_ref in enumerate(out_refs):
        for group in range(2):

            @pl.when((zl ^ a) == group)
            def _():
                for n in range(2):
                    out_ref[n * 256 : (n + 1) * 256, :] = own_ref[n, :, group * 384 : (group + 1) * 384]

        for n in range(3):
            out_ref[512:, n * HEAD_DIM : (n + 1) * HEAD_DIM] = header[...]


def queries_kernel(*refs):
    blocks, q_ref = refs[:2], refs[-1]
    for a, block in enumerate(blocks):
        q_ref[a * 256 : (a + 1) * 256, :] = block[:256, :]
        q_ref[512 + 16 * a : 512 + 16 * (a + 1), :] = block[256:, :]


def pairs_kernel(place, *refs):
    blocks, kv_ref = refs[:2], refs[-1]
    cols = slice(place * HEAD_DIM, (place + 1) * HEAD_DIM)
    for a, block in enumerate(blocks):
        kv_ref[a * 512 : (a + 1) * 512, :] = block[:512, cols]
        kv_ref[1024 + 16 * a : 1024 + 16 * (a + 1), :] = block[512:, cols]


def merge_kernel(info, *refs):
    blocks, out_ref = refs[:4], refs[-1]
    zl, y = info[0], info[1]
    for step, block in enumerate(blocks):
        for a in range(2):
            at = pl.multiple_of(((zl ^ a) * 4 + ((y - step) & 3)) * 256, 256)
            out_ref[pl.ds(at, 256), :] = block[a * 512 : a * 512 + 256, :]
            out_ref[pl.ds(2048 + at, 256), :] = block[a * 512 + 256 : a * 512 + 512, :]
        out_ref[4096 + 32 * step : 4096 + 32 * (step + 1), :] = block[1024:, :]


def small_call(kernel, rows, cols, operands, after=(), info=None, outs=1):
    lead = [] if info is None else [info]
    return pl.pallas_call(
        kernel,
        out_shape=[jax.ShapeDtypeStruct((rows, cols), jnp.bfloat16)] * outs,
        in_specs=[SMEM] * len(lead) + [VMEM] * len(operands) + [pl.BlockSpec(memory_space=pl.ANY)] * len(after),
        out_specs=[VMEM] * outs,
        compiler_params=pltpu.CompilerParams(vmem_limit_bytes=32 << 20),
    )(*lead, *operands, *after)


def attend_kernel(head, info, *refs):
    q_refs, (near, far), refs = refs[:4], refs[4:6], refs[6:]
    before, refs = (refs[:4], refs[4:]) if head == 1 else ((), refs[-12:])
    o_refs, (queries, keys, vals, scores, tops, sums, flat, outs) = refs[:4], refs[4:]
    base = 0
    for old, o_ref in zip(before, o_refs):
        base = old.shape[0]
        o_ref[:base, :] = old[...]
    zl, y, x, c = [info[n] for n in range(4)]
    lane = lax.broadcasted_iota(jnp.int32, (SEG, HEAD_DIM), 1)
    row = lax.broadcasted_iota(jnp.int32, (SEG, HEAD_DIM), 0)

    def bounds(lines):
        found = sum(line.astype(jnp.float32) for line in lines)
        return [
            jnp.sum(jnp.where(lane[:16] == n, found, 0.0), keepdims=True)[0, 0].astype(jnp.int32)
            for n in range(2)
        ]

    n1, n2 = bounds([ref[KEYS + 16 * n : KEYS + 16 * (n + 1), :] for ref in (near, far) for n in range(8)])
    m1, m2 = bounds([ref[512 + 16 * n : 528 + 16 * n, :HEAD_DIM] for ref in q_refs for n in range(2)])

    def clip_of(index, first, second):
        return (index >= first).astype(jnp.int32) + (index >= second).astype(jnp.int32)

    for n in range(KEYS // SEG):
        own = clip_of(row + n * SEG, n1, n2) == lane
        keys[n * SEG : (n + 1) * SEG, HEAD_DIM:] = own.astype(jnp.float32).astype(jnp.bfloat16)
    for n in range(2048 // SEG):
        differs = (clip_of(row + n * SEG, m1, m2) != lane) & (lane < 3)
        queries[n * SEG : (n + 1) * SEG, HEAD_DIM:] = jnp.where(differs, NEG, 0.0).astype(jnp.bfloat16)
    vals[:, HEAD_DIM:] = jnp.ones((KEYS, HEAD_DIM), jnp.bfloat16)
    cols = slice(head * HEAD_DIM, (head + 1) * HEAD_DIM)
    for step in range(4):
        xx = (x - step) & 3
        for a in range(2):
            zz = 2 * ((1 - c) ^ (xx & 1)) + (zl ^ a)
            at = pl.multiple_of(zz * TILE + (xx >> 1) * 256, 256)
            queries[pl.ds(at, 256), :HEAD_DIM] = q_refs[step][a * 256 : (a + 1) * 256, cols]
    zh = 1 - c
    for part, ref in ((zh, near), (1 - zh, far)):
        at = pl.ds(pl.multiple_of(part * 2048, 2048), 2048)
        keys[at, :HEAD_DIM] = ref[:2048, :]
        vals[at, :HEAD_DIM] = ref[2048:4096, :]

    eye = (lane == row).astype(jnp.float32)
    sub = lax.broadcasted_iota(jnp.int32, (16, HEAD_DIM), 0)

    def tile(zz, carry):
        first, last = zz * TILE, zz * TILE + TILE - 1
        low = jnp.where(first >= m2, n2, jnp.where(first >= m1, n1, 0))
        high = jnp.where(last >= m2, KEYS, jnp.where(last >= m1, n2, n1))
        low = (low // SEG) * SEG
        need = high - low
        rows = pl.ds(pl.multiple_of(first, TILE), TILE)
        tops[...] = jnp.full((TILE, HEAD_DIM), NEG, jnp.float32)
        sums[...] = jnp.zeros((TILE, 2 * HEAD_DIM), jnp.float32)

        def runs(k):
            under = WIDTHS[k - 1] if k else 0
            return ((need > under) & (need <= WIDTHS[k])).astype(jnp.int32)

        for k, width in enumerate(WIDTHS):
            at = pl.multiple_of(jnp.minimum(low, KEYS - width), SEG)

            def first_pass(i, carry, width=width, at=at):
                s = lax.dot_general(
                    queries[rows, :],
                    keys[pl.ds(at, width), :],
                    (((1,), (1,)), ((), ())),
                    preferred_element_type=jnp.float32,
                )
                scores[:, :width] = s
                top = s[:, :128]
                for n in range(1, width // 128):
                    top = jnp.maximum(top, s[:, n * 128 : (n + 1) * 128])
                tops[...] = top
                return carry

            lax.fori_loop(0, runs(k), first_pass, 0)

        top = jnp.maximum(jnp.max(tops[...], axis=1, keepdims=True), FLOOR)

        for k, width in enumerate(WIDTHS):
            at = pl.multiple_of(jnp.minimum(low, KEYS - width), SEG)

            def second_pass(i, carry, width=width, at=at):
                weights = jnp.exp(scores[:, :width] - top).astype(jnp.bfloat16)
                sums[...] = jnp.dot(weights, vals[pl.ds(at, width), :], preferred_element_type=jnp.float32)
                return carry

            lax.fori_loop(0, runs(k), second_pass, 0)

        total = jnp.maximum(sums[:, HEAD_DIM:], 1e-30)
        flat[...] = (sums[:, :HEAD_DIM] / total).astype(jnp.bfloat16)
        tops[...] = top + jnp.log(total)
        a = (zz & 1) ^ zl
        for pair in range(2):
            xx = ((zz >> 1) ^ (1 - c)) + 2 * pair
            step = (xx - x) & 3
            for half in range(2):
                at = slice(pair * 256 + half * SEG, pair * 256 + (half + 1) * SEG)
                to = pl.multiple_of(a * 256 + half * SEG, SEG)
                outs[step, pl.ds(to, SEG), :] = flat[at, :]
                line = jnp.sum(tops[at, :] * eye, axis=0, keepdims=True)
                big = line.astype(jnp.bfloat16).astype(jnp.float32)
                middle = (line - big).astype(jnp.bfloat16).astype(jnp.float32)
                rest = line - big - middle
                parts = jnp.where(sub == 0, big, jnp.where(sub == 1, middle, jnp.where(sub == 2, rest, 0.0)))
                to = pl.multiple_of(512 + (2 * a + half) * 16, 16)
                outs[step, pl.ds(to, 16), :] = parts.astype(jnp.bfloat16)
        return carry

    lax.fori_loop(0, 4, tile, 0)
    for step in range(4):
        o_refs[step][base:, :] = outs[step]


def attend(head, info, queries, near, far, before=(), after=()):
    return pl.pallas_call(
        functools.partial(attend_kernel, head),
        out_shape=[jax.ShapeDtypeStruct(((2 if before else 1) * (4 * SEG + 64), HEAD_DIM), jnp.bfloat16)] * 4,
        in_specs=[SMEM] + [VMEM] * (6 + len(before)) + [pl.BlockSpec(memory_space=pl.ANY)] * len(after),
        out_specs=[VMEM] * 4,
        scratch_shapes=[
            pltpu.VMEM((2048, 2 * HEAD_DIM), jnp.bfloat16),
            pltpu.VMEM((KEYS, 2 * HEAD_DIM), jnp.bfloat16),
            pltpu.VMEM((KEYS, 2 * HEAD_DIM), jnp.bfloat16),
            pltpu.VMEM((TILE, KEYS), jnp.float32),
            pltpu.VMEM((TILE, HEAD_DIM), jnp.float32),
            pltpu.VMEM((TILE, 2 * HEAD_DIM), jnp.float32),
            pltpu.VMEM((TILE, HEAD_DIM), jnp.bfloat16),
            pltpu.VMEM((4, 4 * SEG + 64, HEAD_DIM), jnp.bfloat16),
        ],
        compiler_params=pltpu.CompilerParams(vmem_limit_bytes=48 << 20),
        cost_estimate=pl.CostEstimate(
            flops=2 * 2 * 2048 * 4096 * 128, bytes_accessed=4 << 20, transcendentals=2048 * 4096
        ),
    )(info, *queries, near, far, *before, *after)


def combine_kernel(*refs):
    out_ref = refs[-1]
    eye = (
        lax.broadcasted_iota(jnp.int32, (SEG, SEG), 0)
        == lax.broadcasted_iota(jnp.int32, (SEG, SEG), 1)
    ).astype(jnp.float32)
    for head in range(3):
        parts = refs[:4] if head < 2 else refs[4:8]
        base = 4 * SEG + 64 if head == 1 else 0
        for slot in range(4):
            levels = []
            for part in parts:
                at = base + 4 * SEG + slot * 16
                lines = part[at : at + 16, :].astype(jnp.float32)
                levels.append(jnp.sum(lines, axis=0, keepdims=True))
            top = functools.reduce(jnp.maximum, levels)
            shares = [jnp.exp(level - top) for level in levels]
            total = functools.reduce(jnp.add, shares)
            spread = jnp.concatenate([eye * (share / total) for share in shares], axis=1)
            at = base + slot * SEG
            stacked = jnp.concatenate([part[at : at + SEG, :] for part in parts], axis=0)
            mixed = jnp.dot(spread.astype(jnp.bfloat16), stacked, preferred_element_type=jnp.float32)
            out_ref[slot, :, head * HEAD_DIM : (head + 1) * HEAD_DIM] = mixed.astype(jnp.bfloat16)


def combine(blocks):
    return pl.pallas_call(
        combine_kernel,
        out_shape=jax.ShapeDtypeStruct((4, SEG, 3 * HEAD_DIM), jnp.bfloat16),
        in_specs=[VMEM] * len(blocks),
        out_specs=VMEM,
        compiler_params=pltpu.CompilerParams(vmem_limit_bytes=32 << 20),
    )(*blocks)


def outward_kernel(info, first_ref, second_ref, w_ref, *refs):
    out_ref, zl = refs[-1], info[0]
    total = 0.0
    for a, block in enumerate((first_ref, second_ref)):
        rows = pl.ds(pl.multiple_of((zl ^ a) * 384, 384), 384)
        total += jnp.dot(block[...], w_ref[rows, :], preferred_element_type=jnp.float32)
    out_ref[...] = total.astype(out_ref.dtype)


def outward(other_half, dtype, info, blocks, w_out, after=()):
    depth, width = w_out.shape[0], w_out.shape[1] // 2
    whole = lambda n, info_ref: (0, 0)
    grid_spec = pltpu.PrefetchScalarGridSpec(
        num_scalar_prefetch=1,
        grid=(1,),
        in_specs=[pl.BlockSpec((256, 384), whole)] * 2
        + [pl.BlockSpec((depth, width), lambda n, info_ref: (0, info_ref[3] ^ other_half))]
        + [pl.BlockSpec(memory_space=pl.ANY)] * len(after),
        out_specs=pl.BlockSpec((256, width), whole),
    )
    return pl.pallas_call(
        outward_kernel,
        grid_spec=grid_spec,
        out_shape=jax.ShapeDtypeStruct((256, width), dtype),
        compiler_params=pltpu.CompilerParams(vmem_limit_bytes=40 << 20),
        cost_estimate=pl.CostEstimate(
            flops=2 * 256 * depth * width, bytes_accessed=2 * depth * width, transcendentals=0
        ),
    )(info, *blocks, w_out, *after)


def spread_pairs(a, alternate):
    pairs = []
    for z in range(4):
        for x in range(4):
            for c in range(2):
                target = 2 * c + ((z % 2) ^ a)
                pairs.append(((z * 4 + x) * 2 + c, (target * 4 + x) * 2 + ((1 - z // 2) ^ (x % 2 if alternate else 0))))
    return pairs


def turn(step):
    return [(n, (n + step) % 4) for n in range(4)]


def body(tokens, clip_id, w_qkv, w_out):
    z, y, x, c = [lax.axis_index(name) for name in ("z", "y", "x", "core")]
    zl, zh = z % 2, z // 2
    swap = [(0, 1), (1, 0)]
    info = jnp.stack([zl, y, x, c, zh]).astype(jnp.int32)

    halves = clip_id.reshape(2, SEG)
    counts = jnp.stack([jnp.sum(halves < 1, axis=1), jnp.sum(halves < 2, axis=1)], axis=1)
    header = jnp.pad(counts.astype(jnp.bfloat16), ((0, 14), (0, HEAD_DIM - 2)))

    other = lax.ppermute(tokens, "core", swap)
    [begun] = project(
        own_kernel, 0, info, tokens, w_qkv, [], [jax.ShapeDtypeStruct((256, w_qkv.shape[2]), jnp.float32)]
    )
    leaving = project(
        other_kernel, 1, info, other, w_qkv, [begun, header], [jax.ShapeDtypeStruct((272, 384), jnp.bfloat16)] * 2
    )
    both = jnp.where(c == 0, jnp.concatenate([tokens, other], 1), jnp.concatenate([other, tokens], 1))
    own_kv = jnp.einsum("td,sdc->stc", both, w_qkv[1:], preferred_element_type=jnp.float32)

    def to_group(blocks, alternate):
        return [
            lax.ppermute(block, ("z", "x", "core"), spread_pairs(a, alternate)) for a, block in enumerate(blocks)
        ]

    q_in = to_group(leaving, True)
    leaving = small_call(send_kernel, 528, 384, [own_kv.astype(jnp.bfloat16), header], q_in, info, 2)
    kv_in = to_group(leaving, False)
    [mine] = small_call(queries_kernel, 544, 384, q_in, leaving[:1])
    queries = [mine] + [lax.ppermute(mine, "x", turn(step)) for step in (1, 2, 3)]

    def key_blocks(head, after):
        [own] = small_call(functools.partial(pairs_kernel, head), 1056, HEAD_DIM, kv_in, after)
        return [own] + [lax.ppermute(own, "y", turn(step)) for step in (1, 2, 3)]

    def merged(blocks, after=()):
        [near] = small_call(merge_kernel, KEYS + 128, HEAD_DIM, blocks, after, info)
        return near, lax.ppermute(near, "core", swap)

    kv = key_blocks(0, queries[:1])
    kv_next = key_blocks(1, kv[1:])
    part = attend(0, info, queries, *merged(kv, queries[1:]))
    kv_last = key_blocks(2, (*kv_next[1:], part[0]))
    part = attend(1, info, queries, *merged(kv_next, part[:1]), part)
    last = attend(2, info, queries, *merged(kv_last, part[:1]))
    results = []
    for blocks in (part, last):
        results.append(blocks[0])
        for step in (1, 2, 3):
            results.append(lax.ppermute(blocks[step], "x", turn(step)))
    mixed = combine(results)

    back = []
    for a in range(2):
        returns = [(target, source) for source, target in spread_pairs(a, True)]
        block = mixed[2 * a : 2 * a + 2].reshape(256, 384)
        back.append(lax.ppermute(block, ("z", "x", "core"), returns))
    there = outward(1, jnp.bfloat16, info, back, w_out)
    received = lax.ppermute(there, "core", swap)
    here = outward(0, jnp.float32, info, back, w_out, (there,))
    return (here + received.astype(jnp.float32)).astype(jnp.bfloat16)


def solution(mesh):
    fine = Mesh(mesh.devices.reshape(4, 4, 4, 2), ("z", "y", "x", "core"))
    seq = ("z", "y", "x")
    in_specs = (P(seq, "core"), P(seq), P(None, None, "core"), P("core", None))
    return jax.shard_map(body, mesh=fine, in_specs=in_specs, out_specs=P(seq, "core"), check_vma=False)
```

```python
import functools
import math

import jax
import jax.numpy as jnp
from jax import lax
from jax.experimental import pallas as pl
from jax.experimental.pallas import tpu as pltpu
from jax.sharding import Mesh
from jax.sharding import PartitionSpec as P

HEAD_DIM = 128
SEG = 128
TILE = 512
KEYS = 4096
NEG = -1e30
FLOOR = -1e29
WIDTHS = (768, 1536, 2048, 2688, 3328, 4096)
VMEM = pl.BlockSpec(memory_space=pltpu.VMEM)
SMEM = pl.BlockSpec(memory_space=pltpu.SMEM)


def own_kernel(info, own_ref, w_ref, out_ref):
    out_ref[...] = jnp.dot(own_ref[...], w_ref[0], preferred_element_type=jnp.float32)


def other_kernel(info, other_ref, w_ref, begun, header, *out_refs):
    total = begun[...] + jnp.dot(other_ref[...], w_ref[0], preferred_element_type=jnp.float32)
    made = (total * (1.0 / math.sqrt(HEAD_DIM))).astype(jnp.bfloat16)
    for a, out_ref in enumerate(out_refs):
        for group in range(2):

            @pl.when((info[0] ^ a) == group)
            def _():
                out_ref[:256, :] = made[:, group * 384 : (group + 1) * 384]

        for n in range(3):
            out_ref[256:, n * HEAD_DIM : (n + 1) * HEAD_DIM] = header[...]


def project(kernel, which, info, tokens, w_qkv, operands, shapes):
    depth, width = tokens.shape[1], w_qkv.shape[2]
    whole = lambda n, info_ref: (0, 0)
    grid_spec = pltpu.PrefetchScalarGridSpec(
        num_scalar_prefetch=1,
        grid=(1,),
        in_specs=[
            pl.BlockSpec(tokens.shape, whole),
            pl.BlockSpec((1, depth, width), lambda n, info_ref: (0, info_ref[3] ^ which, 0)),
        ]
        + [pl.BlockSpec(operand.shape, whole) for operand in operands],
        out_specs=[pl.BlockSpec(shape.shape, whole) for shape in shapes],
    )
    return pl.pallas_call(
        kernel,
        grid_spec=grid_spec,
        out_shape=shapes,
        compiler_params=pltpu.CompilerParams(vmem_limit_bytes=52 << 20),
        cost_estimate=pl.CostEstimate(
            flops=2 * 256 * depth * width, bytes_accessed=2 * depth * width, transcendentals=0
        ),
    )(info, tokens, w_qkv, *operands)


def send_kernel(info, own_ref, header, *refs):
    out_refs, zl = refs[-2:], info[0]
    for a, out_ref in enumerate(out_refs):
        for group in range(2):

            @pl.when((zl ^ a) == group)
            def _():
                for n in range(2):
                    out_ref[n * 256 : (n + 1) * 256, :] = own_ref[n, :, group * 384 : (group + 1) * 384]

        for n in range(3):
            out_ref[512:, n * HEAD_DIM : (n + 1) * HEAD_DIM] = header[...]


def queries_kernel(*refs):
    blocks, q_ref = refs[:2], refs[-1]
    for a, block in enumerate(blocks):
        q_ref[a * 256 : (a + 1) * 256, :] = block[:256, :]
        q_ref[512 + 16 * a : 512 + 16 * (a + 1), :] = block[256:, :]


def pairs_kernel(place, *refs):
    blocks, kv_ref = refs[:2], refs[-1]
    cols = slice(place * HEAD_DIM, (place + 1) * HEAD_DIM)
    for a, block in enumerate(blocks):
        kv_ref[a * 512 : (a + 1) * 512, :] = block[:512, cols]
        kv_ref[1024 + 16 * a : 1024 + 16 * (a + 1), :] = block[512:, cols]


def merge_kernel(info, *refs):
    blocks, out_ref = refs[:4], refs[-1]
    zl, y = info[0], info[1]
    for step, block in enumerate(blocks):
        for a in range(2):
            at = pl.multiple_of(((zl ^ a) * 4 + ((y - step) & 3)) * 256, 256)
            out_ref[pl.ds(at, 256), :] = block[a * 512 : a * 512 + 256, :]
            out_ref[pl.ds(2048 + at, 256), :] = block[a * 512 + 256 : a * 512 + 512, :]
        out_ref[4096 + 32 * step : 4096 + 32 * (step + 1), :] = block[1024:, :]


def small_call(kernel, rows, cols, operands, after=(), info=None, outs=1):
    lead = [] if info is None else [info]
    return pl.pallas_call(
        kernel,
        out_shape=[jax.ShapeDtypeStruct((rows, cols), jnp.bfloat16)] * outs,
        in_specs=[SMEM] * len(lead) + [VMEM] * len(operands) + [pl.BlockSpec(memory_space=pl.ANY)] * len(after),
        out_specs=[VMEM] * outs,
        compiler_params=pltpu.CompilerParams(vmem_limit_bytes=32 << 20),
    )(*lead, *operands, *after)


def attend_kernel(head, info, *refs):
    q_refs, (near, far), refs = refs[:4], refs[4:6], refs[6:]
    before, refs = (refs[:4], refs[4:]) if head == 1 else ((), refs[-12:])
    o_refs, (queries, keys, vals, scores, tops, sums, flat, outs) = refs[:4], refs[4:]
    base = 0
    for old, o_ref in zip(before, o_refs):
        base = old.shape[0]
        o_ref[:base, :] = old[...]
    zl, y, x, c = [info[n] for n in range(4)]
    lane = lax.broadcasted_iota(jnp.int32, (SEG, HEAD_DIM), 1)
    row = lax.broadcasted_iota(jnp.int32, (SEG, HEAD_DIM), 0)

    def bounds(lines):
        found = sum(line.astype(jnp.float32) for line in lines)
        return [
            jnp.sum(jnp.where(lane[:16] == n, found, 0.0), keepdims=True)[0, 0].astype(jnp.int32)
            for n in range(2)
        ]

    n1, n2 = bounds([ref[KEYS + 16 * n : KEYS + 16 * (n + 1), :] for ref in (near, far) for n in range(8)])
    m1, m2 = bounds([ref[512 + 16 * n : 528 + 16 * n, :HEAD_DIM] for ref in q_refs for n in range(2)])

    def clip_of(index, first, second):
        return (index >= first).astype(jnp.int32) + (index >= second).astype(jnp.int32)

    for n in range(KEYS // SEG):
        own = clip_of(row + n * SEG, n1, n2) == lane
        keys[n * SEG : (n + 1) * SEG, HEAD_DIM:] = own.astype(jnp.float32).astype(jnp.bfloat16)
    for n in range(2048 // SEG):
        differs = (clip_of(row + n * SEG, m1, m2) != lane) & (lane < 3)
        queries[n * SEG : (n + 1) * SEG, HEAD_DIM:] = jnp.where(differs, NEG, 0.0).astype(jnp.bfloat16)
    vals[:, HEAD_DIM:] = jnp.ones((KEYS, HEAD_DIM), jnp.bfloat16)
    cols = slice(head * HEAD_DIM, (head + 1) * HEAD_DIM)
    for step in range(4):
        xx = (x - step) & 3
        for a in range(2):
            zz = 2 * ((1 - c) ^ (xx & 1)) + (zl ^ a)
            at = pl.multiple_of(zz * TILE + (xx >> 1) * 256, 256)
            queries[pl.ds(at, 256), :HEAD_DIM] = q_refs[step][a * 256 : (a + 1) * 256, cols]
    zh = 1 - c
    for part, ref in ((zh, near), (1 - zh, far)):
        at = pl.ds(pl.multiple_of(part * 2048, 2048), 2048)
        keys[at, :HEAD_DIM] = ref[:2048, :]
        vals[at, :HEAD_DIM] = ref[2048:4096, :]

    eye = (lane == row).astype(jnp.float32)
    sub = lax.broadcasted_iota(jnp.int32, (16, HEAD_DIM), 0)

    def tile(zz, carry):
        first, last = zz * TILE, zz * TILE + TILE - 1
        low = jnp.where(first >= m2, n2, jnp.where(first >= m1, n1, 0))
        high = jnp.where(last >= m2, KEYS, jnp.where(last >= m1, n2, n1))
        low = (low // SEG) * SEG
        need = high - low
        rows = pl.ds(pl.multiple_of(first, TILE), TILE)
        tops[...] = jnp.full((TILE, HEAD_DIM), NEG, jnp.float32)
        sums[...] = jnp.zeros((TILE, 2 * HEAD_DIM), jnp.float32)

        def runs(k):
            under = WIDTHS[k - 1] if k else 0
            return ((need > under) & (need <= WIDTHS[k])).astype(jnp.int32)

        for k, width in enumerate(WIDTHS):
            at = pl.multiple_of(jnp.minimum(low, KEYS - width), SEG)

            def first_pass(i, carry, width=width, at=at):
                s = lax.dot_general(
                    queries[rows, :],
                    keys[pl.ds(at, width), :],
                    (((1,), (1,)), ((), ())),
                    preferred_element_type=jnp.float32,
                )
                scores[:, :width] = s
                top = s[:, :128]
                for n in range(1, width // 128):
                    top = jnp.maximum(top, s[:, n * 128 : (n + 1) * 128])
                tops[...] = top
                return carry

            lax.fori_loop(0, runs(k), first_pass, 0)

        top = jnp.maximum(jnp.max(tops[...], axis=1, keepdims=True), FLOOR)

        for k, width in enumerate(WIDTHS):
            at = pl.multiple_of(jnp.minimum(low, KEYS - width), SEG)

            def second_pass(i, carry, width=width, at=at):
                weights = jnp.exp(scores[:, :width] - top).astype(jnp.bfloat16)
                sums[...] = jnp.dot(weights, vals[pl.ds(at, width), :], preferred_element_type=jnp.float32)
                return carry

            lax.fori_loop(0, runs(k), second_pass, 0)

        total = jnp.maximum(sums[:, HEAD_DIM:], 1e-30)
        flat[...] = (sums[:, :HEAD_DIM] / total).astype(jnp.bfloat16)
        tops[...] = top + jnp.log(total)
        a = (zz & 1) ^ zl
        for pair in range(2):
            xx = ((zz >> 1) ^ (1 - c)) + 2 * pair
            step = (xx - x) & 3
            for half in range(2):
                at = slice(pair * 256 + half * SEG, pair * 256 + (half + 1) * SEG)
                to = pl.multiple_of(a * 256 + half * SEG, SEG)
                outs[step, pl.ds(to, SEG), :] = flat[at, :]
                line = jnp.sum(tops[at, :] * eye, axis=0, keepdims=True)
                big = line.astype(jnp.bfloat16).astype(jnp.float32)
                middle = (line - big).astype(jnp.bfloat16).astype(jnp.float32)
                rest = line - big - middle
                parts = jnp.where(sub == 0, big, jnp.where(sub == 1, middle, jnp.where(sub == 2, rest, 0.0)))
                to = pl.multiple_of(512 + (2 * a + half) * 16, 16)
                outs[step, pl.ds(to, 16), :] = parts.astype(jnp.bfloat16)
        return carry

    lax.fori_loop(0, 4, tile, 0)
    for step in range(4):
        o_refs[step][base:, :] = outs[step]


def attend(head, info, queries, near, far, before=(), after=()):
    return pl.pallas_call(
        functools.partial(attend_kernel, head),
        out_shape=[jax.ShapeDtypeStruct(((2 if before else 1) * (4 * SEG + 64), HEAD_DIM), jnp.bfloat16)] * 4,
        in_specs=[SMEM] + [VMEM] * (6 + len(before)) + [pl.BlockSpec(memory_space=pl.ANY)] * len(after),
        out_specs=[VMEM] * 4,
        scratch_shapes=[
            pltpu.VMEM((2048, 2 * HEAD_DIM), jnp.bfloat16),
            pltpu.VMEM((KEYS, 2 * HEAD_DIM), jnp.bfloat16),
            pltpu.VMEM((KEYS, 2 * HEAD_DIM), jnp.bfloat16),
            pltpu.VMEM((TILE, KEYS), jnp.float32),
            pltpu.VMEM((TILE, HEAD_DIM), jnp.float32),
            pltpu.VMEM((TILE, 2 * HEAD_DIM), jnp.float32),
            pltpu.VMEM((TILE, HEAD_DIM), jnp.bfloat16),
            pltpu.VMEM((4, 4 * SEG + 64, HEAD_DIM), jnp.bfloat16),
        ],
        compiler_params=pltpu.CompilerParams(vmem_limit_bytes=48 << 20),
        cost_estimate=pl.CostEstimate(
            flops=2 * 2 * 2048 * 4096 * 128, bytes_accessed=4 << 20, transcendentals=2048 * 4096
        ),
    )(info, *queries, near, far, *before, *after)


def combine_kernel(*refs):
    out_ref = refs[-1]
    eye = (
        lax.broadcasted_iota(jnp.int32, (SEG, SEG), 0)
        == lax.broadcasted_iota(jnp.int32, (SEG, SEG), 1)
    ).astype(jnp.float32)
    for head in range(3):
        parts = refs[:4] if head < 2 else refs[4:8]
        base = 4 * SEG + 64 if head == 1 else 0
        for slot in range(4):
            levels = []
            for part in parts:
                at = base + 4 * SEG + slot * 16
                lines = part[at : at + 16, :].astype(jnp.float32)
                levels.append(jnp.sum(lines, axis=0, keepdims=True))
            top = functools.reduce(jnp.maximum, levels)
            shares = [jnp.exp(level - top) for level in levels]
            total = functools.reduce(jnp.add, shares)
            spread = jnp.concatenate([eye * (share / total) for share in shares], axis=1)
            at = base + slot * SEG
            stacked = jnp.concatenate([part[at : at + SEG, :] for part in parts], axis=0)
            mixed = jnp.dot(spread.astype(jnp.bfloat16), stacked, preferred_element_type=jnp.float32)
            out_ref[slot, :, head * HEAD_DIM : (head + 1) * HEAD_DIM] = mixed.astype(jnp.bfloat16)


def combine(blocks):
    return pl.pallas_call(
        combine_kernel,
        out_shape=jax.ShapeDtypeStruct((4, SEG, 3 * HEAD_DIM), jnp.bfloat16),
        in_specs=[VMEM] * len(blocks),
        out_specs=VMEM,
        compiler_params=pltpu.CompilerParams(vmem_limit_bytes=32 << 20),
    )(*blocks)


def outward_kernel(info, first_ref, second_ref, w_ref, *refs):
    out_ref, zl = refs[-1], info[0]
    total = 0.0
    for a, block in enumerate((first_ref, second_ref)):
        rows = pl.ds(pl.multiple_of((zl ^ a) * 384, 384), 384)
        total += jnp.dot(block[...], w_ref[rows, :], preferred_element_type=jnp.float32)
    out_ref[...] = total.astype(out_ref.dtype)


def outward(other_half, dtype, info, blocks, w_out, after=()):
    depth, width = w_out.shape[0], w_out.shape[1] // 2
    whole = lambda n, info_ref: (0, 0)
    grid_spec = pltpu.PrefetchScalarGridSpec(
        num_scalar_prefetch=1,
        grid=(1,),
        in_specs=[pl.BlockSpec((256, 384), whole)] * 2
        + [pl.BlockSpec((depth, width), lambda n, info_ref: (0, info_ref[3] ^ other_half))]
        + [pl.BlockSpec(memory_space=pl.ANY)] * len(after),
        out_specs=pl.BlockSpec((256, width), whole),
    )
    return pl.pallas_call(
        outward_kernel,
        grid_spec=grid_spec,
        out_shape=jax.ShapeDtypeStruct((256, width), dtype),
        compiler_params=pltpu.CompilerParams(vmem_limit_bytes=40 << 20),
        cost_estimate=pl.CostEstimate(
            flops=2 * 256 * depth * width, bytes_accessed=2 * depth * width, transcendentals=0
        ),
    )(info, *blocks, w_out, *after)


def spread_pairs(a, alternate):
    pairs = []
    for z in range(4):
        for x in range(4):
            for c in range(2):
                target = 2 * c + ((z % 2) ^ a)
                pairs.append(((z * 4 + x) * 2 + c, (target * 4 + x) * 2 + ((1 - z // 2) ^ (x % 2 if alternate else 0))))
    return pairs


def turn(step):
    return [(n, (n + step) % 4) for n in range(4)]


def body(tokens, clip_id, w_qkv, w_out):
    z, y, x, c = [lax.axis_index(name) for name in ("z", "y", "x", "core")]
    zl, zh = z % 2, z // 2
    swap = [(0, 1), (1, 0)]
    info = jnp.stack([zl, y, x, c, zh]).astype(jnp.int32)

    halves = clip_id.reshape(2, SEG)
    counts = jnp.stack([jnp.sum(halves < 1, axis=1), jnp.sum(halves < 2, axis=1)], axis=1)
    header = jnp.pad(counts.astype(jnp.bfloat16), ((0, 14), (0, HEAD_DIM - 2)))

    other = lax.ppermute(tokens, "core", swap)
    [begun] = project(
        own_kernel, 0, info, tokens, w_qkv, [], [jax.ShapeDtypeStruct((256, w_qkv.shape[2]), jnp.float32)]
    )
    leaving = project(
        other_kernel, 1, info, other, w_qkv, [begun, header], [jax.ShapeDtypeStruct((272, 384), jnp.bfloat16)] * 2
    )
    both = jnp.where(c == 0, jnp.concatenate([tokens, other], 1), jnp.concatenate([other, tokens], 1))
    own_kv = jnp.einsum("td,sdc->stc", both, w_qkv[1:], preferred_element_type=jnp.float32)

    def to_group(blocks, alternate):
        return [
            lax.ppermute(block, ("z", "x", "core"), spread_pairs(a, alternate)) for a, block in enumerate(blocks)
        ]

    q_in = to_group(leaving, True)
    leaving = small_call(send_kernel, 528, 384, [own_kv.astype(jnp.bfloat16), header], q_in, info, 2)
    kv_in = to_group(leaving, False)
    [mine] = small_call(queries_kernel, 544, 384, q_in, leaving[:1])
    queries = [mine] + [lax.ppermute(mine, "x", turn(step)) for step in (1, 2, 3)]

    def key_blocks(head, after):
        [own] = small_call(functools.partial(pairs_kernel, head), 1056, HEAD_DIM, kv_in, after)
        return [own] + [lax.ppermute(own, "y", turn(step)) for step in (1, 2, 3)]

    def merged(blocks, after=()):
        [near] = small_call(merge_kernel, KEYS + 128, HEAD_DIM, blocks, after, info)
        return near, lax.ppermute(near, "core", swap)

    kv = key_blocks(0, queries[:1])
    kv_next = key_blocks(1, kv[1:])
    part = attend(0, info, queries, *merged(kv, queries[1:]))
    kv_last = key_blocks(2, (*kv_next[1:], part[0]))
    part = attend(1, info, queries, *merged(kv_next, part[:1]), part)
    last = attend(2, info, queries, *merged(kv_last, part[:1]))
    results = []
    for blocks in (part, last):
        results.append(blocks[0])
        for step in (1, 2, 3):
            results.append(lax.ppermute(blocks[step], "x", turn(step)))
    mixed = combine(results)

    back = []
    for a in range(2):
        returns = [(target, source) for source, target in spread_pairs(a, True)]
        block = mixed[2 * a : 2 * a + 2].reshape(256, 384)
        back.append(lax.ppermute(block, ("z", "x", "core"), returns))
    there = outward(1, jnp.bfloat16, info, back, w_out)
    received = lax.ppermute(there, "core", swap)
    here = outward(0, jnp.float32, info, back, w_out, (there,))
    return (here + received.astype(jnp.float32)).astype(jnp.bfloat16)


def solution(mesh):
    fine = Mesh(mesh.devices.reshape(4, 4, 4, 2), ("z", "y", "x", "core"))
    seq = ("z", "y", "x")
    in_specs = (P(seq, "core"), P(seq), P(None, None, "core"), P("core", None))
    return jax.shard_map(body, mesh=fine, in_specs=in_specs, out_specs=P(seq, "core"), check_vma=False)
```

```python
import functools
import math

import jax
import jax.numpy as jnp
from jax import lax
from jax.experimental import pallas as pl
from jax.experimental.pallas import tpu as pltpu
from jax.sharding import Mesh
from jax.sharding import PartitionSpec as P

HEAD_DIM = 128
SEG = 128
TILE = 512
KEYS = 4096
NEG = -1e30
FLOOR = -1e29
WIDTHS = (768, 1536, 2048, 2688, 3328, 4096)
VMEM = pl.BlockSpec(memory_space=pltpu.VMEM)
SMEM = pl.BlockSpec(memory_space=pltpu.SMEM)


def send_kernel(parts, info, own_ref, header, *refs):
    out_refs, zl = refs[-2:], info[0]
    for a, out_ref in enumerate(out_refs):
        for group in range(2):

            @pl.when((zl ^ a) == group)
            def _():
                for n in range(parts):
                    out_ref[n * 256 : (n + 1) * 256, :] = own_ref[n, :, group * 384 : (group + 1) * 384]

        for n in range(3):
            out_ref[parts * 256 :, n * HEAD_DIM : (n + 1) * HEAD_DIM] = header[...]


def queries_kernel(*refs):
    blocks, q_ref = refs[:2], refs[-1]
    for a, block in enumerate(blocks):
        q_ref[a * 256 : (a + 1) * 256, :] = block[:256, :]
        q_ref[512 + 16 * a : 512 + 16 * (a + 1), :] = block[256:, :]


def pairs_kernel(place, *refs):
    blocks, kv_ref = refs[:2], refs[-1]
    cols = slice(place * HEAD_DIM, (place + 1) * HEAD_DIM)
    for a, block in enumerate(blocks):
        kv_ref[a * 512 : (a + 1) * 512, :] = block[:512, cols]
        kv_ref[1024 + 16 * a : 1024 + 16 * (a + 1), :] = block[512:, cols]


def merge_kernel(info, *refs):
    blocks, out_ref = refs[:4], refs[-1]
    zl, y = info[0], info[1]
    for step, block in enumerate(blocks):
        for a in range(2):
            at = pl.multiple_of(((zl ^ a) * 4 + ((y - step) & 3)) * 256, 256)
            out_ref[pl.ds(at, 256), :] = block[a * 512 : a * 512 + 256, :]
            out_ref[pl.ds(2048 + at, 256), :] = block[a * 512 + 256 : a * 512 + 512, :]
        out_ref[4096 + 32 * step : 4096 + 32 * (step + 1), :] = block[1024:, :]


def small_call(kernel, rows, cols, operands, after=(), info=None, outs=1):
    lead = [] if info is None else [info]
    return pl.pallas_call(
        kernel,
        out_shape=[jax.ShapeDtypeStruct((rows, cols), jnp.bfloat16)] * outs,
        in_specs=[SMEM] * len(lead) + [VMEM] * len(operands) + [pl.BlockSpec(memory_space=pl.ANY)] * len(after),
        out_specs=[VMEM] * outs,
        compiler_params=pltpu.CompilerParams(vmem_limit_bytes=32 << 20),
    )(*lead, *operands, *after)


def attend_kernel(head, info, *refs):
    q_refs, (near, far), refs = refs[:4], refs[4:6], refs[6:]
    before, refs = (refs[:4], refs[4:]) if head == 1 else ((), refs[-12:])
    o_refs, (queries, keys, vals, scores, tops, sums, flat, outs) = refs[:4], refs[4:]
    base = 0
    for old, o_ref in zip(before, o_refs):
        base = old.shape[0]
        o_ref[:base, :] = old[...]
    zl, y, x, c = [info[n] for n in range(4)]
    lane = lax.broadcasted_iota(jnp.int32, (SEG, HEAD_DIM), 1)
    row = lax.broadcasted_iota(jnp.int32, (SEG, HEAD_DIM), 0)

    def bounds(lines):
        found = sum(line.astype(jnp.float32) for line in lines)
        return [
            jnp.sum(jnp.where(lane[:16] == n, found, 0.0), keepdims=True)[0, 0].astype(jnp.int32)
            for n in range(2)
        ]

    n1, n2 = bounds([ref[KEYS + 16 * n : KEYS + 16 * (n + 1), :] for ref in (near, far) for n in range(8)])
    m1, m2 = bounds([ref[512 + 16 * n : 528 + 16 * n, :HEAD_DIM] for ref in q_refs for n in range(2)])

    def clip_of(index, first, second):
        return (index >= first).astype(jnp.int32) + (index >= second).astype(jnp.int32)

    for n in range(KEYS // SEG):
        own = clip_of(row + n * SEG, n1, n2) == lane
        keys[n * SEG : (n + 1) * SEG, HEAD_DIM:] = own.astype(jnp.float32).astype(jnp.bfloat16)
    for n in range(2048 // SEG):
        differs = (clip_of(row + n * SEG, m1, m2) != lane) & (lane < 3)
        queries[n * SEG : (n + 1) * SEG, HEAD_DIM:] = jnp.where(differs, NEG, 0.0).astype(jnp.bfloat16)
    vals[:, HEAD_DIM:] = jnp.ones((KEYS, HEAD_DIM), jnp.bfloat16)
    cols = slice(head * HEAD_DIM, (head + 1) * HEAD_DIM)
    for step in range(4):
        xx = (x - step) & 3
        for a in range(2):
            zz = 2 * (c ^ (xx & 1)) + (zl ^ a)
            at = pl.multiple_of(zz * TILE + (xx >> 1) * 256, 256)
            queries[pl.ds(at, 256), :HEAD_DIM] = q_refs[step][a * 256 : (a + 1) * 256, cols]
    zh = c ^ (x & 1)
    for part, ref in ((zh, near), (1 - zh, far)):
        at = pl.ds(pl.multiple_of(part * 2048, 2048), 2048)
        keys[at, :HEAD_DIM] = ref[:2048, :]
        vals[at, :HEAD_DIM] = ref[2048:4096, :]

    eye = (lane == row).astype(jnp.float32)
    sub = lax.broadcasted_iota(jnp.int32, (16, HEAD_DIM), 0)

    def tile(zz, carry):
        first, last = zz * TILE, zz * TILE + TILE - 1
        low = jnp.where(first >= m2, n2, jnp.where(first >= m1, n1, 0))
        high = jnp.where(last >= m2, KEYS, jnp.where(last >= m1, n2, n1))
        low = (low // SEG) * SEG
        need = high - low
        rows = pl.ds(pl.multiple_of(first, TILE), TILE)
        tops[...] = jnp.full((TILE, HEAD_DIM), NEG, jnp.float32)
        sums[...] = jnp.zeros((TILE, 2 * HEAD_DIM), jnp.float32)

        def runs(k):
            under = WIDTHS[k - 1] if k else 0
            return ((need > under) & (need <= WIDTHS[k])).astype(jnp.int32)

        for k, width in enumerate(WIDTHS):
            at = pl.multiple_of(jnp.minimum(low, KEYS - width), SEG)

            def first_pass(i, carry, width=width, at=at):
                s = lax.dot_general(
                    queries[rows, :],
                    keys[pl.ds(at, width), :],
                    (((1,), (1,)), ((), ())),
                    preferred_element_type=jnp.float32,
                )
                scores[:, :width] = s
                top = s[:, :128]
                for n in range(1, width // 128):
                    top = jnp.maximum(top, s[:, n * 128 : (n + 1) * 128])
                tops[...] = top
                return carry

            lax.fori_loop(0, runs(k), first_pass, 0)

        top = jnp.maximum(jnp.max(tops[...], axis=1, keepdims=True), FLOOR)

        for k, width in enumerate(WIDTHS):
            at = pl.multiple_of(jnp.minimum(low, KEYS - width), SEG)

            def second_pass(i, carry, width=width, at=at):
                weights = jnp.exp(scores[:, :width] - top).astype(jnp.bfloat16)
                sums[...] = jnp.dot(weights, vals[pl.ds(at, width), :], preferred_element_type=jnp.float32)
                return carry

            lax.fori_loop(0, runs(k), second_pass, 0)

        total = jnp.maximum(sums[:, HEAD_DIM:], 1e-30)
        flat[...] = (sums[:, :HEAD_DIM] / total).astype(jnp.bfloat16)
        tops[...] = top + jnp.log(total)
        a = (zz & 1) ^ zl
        for pair in range(2):
            xx = ((zz >> 1) ^ c) + 2 * pair
            step = (xx - x) & 3
            for half in range(2):
                at = slice(pair * 256 + half * SEG, pair * 256 + (half + 1) * SEG)
                to = pl.multiple_of(a * 256 + half * SEG, SEG)
                outs[step, pl.ds(to, SEG), :] = flat[at, :]
                line = jnp.sum(tops[at, :] * eye, axis=0, keepdims=True)
                big = line.astype(jnp.bfloat16).astype(jnp.float32)
                middle = (line - big).astype(jnp.bfloat16).astype(jnp.float32)
                rest = line - big - middle
                parts = jnp.where(sub == 0, big, jnp.where(sub == 1, middle, jnp.where(sub == 2, rest, 0.0)))
                to = pl.multiple_of(512 + (2 * a + half) * 16, 16)
                outs[step, pl.ds(to, 16), :] = parts.astype(jnp.bfloat16)
        return carry

    lax.fori_loop(0, 4, tile, 0)
    for step in range(4):
        o_refs[step][base:, :] = outs[step]


def attend(head, info, queries, near, far, before=(), after=()):
    return pl.pallas_call(
        functools.partial(attend_kernel, head),
        out_shape=[jax.ShapeDtypeStruct(((2 if before else 1) * (4 * SEG + 64), HEAD_DIM), jnp.bfloat16)] * 4,
        in_specs=[SMEM] + [VMEM] * (6 + len(before)) + [pl.BlockSpec(memory_space=pl.ANY)] * len(after),
        out_specs=[VMEM] * 4,
        scratch_shapes=[
            pltpu.VMEM((2048, 2 * HEAD_DIM), jnp.bfloat16),
            pltpu.VMEM((KEYS, 2 * HEAD_DIM), jnp.bfloat16),
            pltpu.VMEM((KEYS, 2 * HEAD_DIM), jnp.bfloat16),
            pltpu.VMEM((TILE, KEYS), jnp.float32),
            pltpu.VMEM((TILE, HEAD_DIM), jnp.float32),
            pltpu.VMEM((TILE, 2 * HEAD_DIM), jnp.float32),
            pltpu.VMEM((TILE, HEAD_DIM), jnp.bfloat16),
            pltpu.VMEM((4, 4 * SEG + 64, HEAD_DIM), jnp.bfloat16),
        ],
        compiler_params=pltpu.CompilerParams(vmem_limit_bytes=48 << 20),
        cost_estimate=pl.CostEstimate(
            flops=2 * 2 * 2048 * 4096 * 128, bytes_accessed=4 << 20, transcendentals=2048 * 4096
        ),
    )(info, *queries, near, far, *before, *after)


def combine_kernel(heads, *refs):
    parts, out_ref = refs[:4], refs[-1]
    eye = (
        lax.broadcasted_iota(jnp.int32, (SEG, SEG), 0)
        == lax.broadcasted_iota(jnp.int32, (SEG, SEG), 1)
    ).astype(jnp.float32)
    for head in range(heads):
        base = head * (4 * SEG + 64)
        for slot in range(4):
            levels = []
            for part in parts:
                at = base + 4 * SEG + slot * 16
                lines = part[at : at + 16, :].astype(jnp.float32)
                levels.append(jnp.sum(lines, axis=0, keepdims=True))
            top = functools.reduce(jnp.maximum, levels)
            shares = [jnp.exp(level - top) for level in levels]
            total = functools.reduce(jnp.add, shares)
            spread = jnp.concatenate([eye * (share / total) for share in shares], axis=1)
            at = base + slot * SEG
            stacked = jnp.concatenate([part[at : at + SEG, :] for part in parts], axis=0)
            mixed = jnp.dot(spread.astype(jnp.bfloat16), stacked, preferred_element_type=jnp.float32)
            rows = slice(slot * SEG, (slot + 1) * SEG)
            out_ref[rows, head * HEAD_DIM : (head + 1) * HEAD_DIM] = mixed.astype(jnp.bfloat16)


def outward_kernel(first_row, begun, info, first_ref, second_ref, w_ref, *refs):
    out_ref, zl = refs[-1], info[0]
    total = refs[0][...] if begun else 0.0
    for a, block in enumerate((first_ref, second_ref)):
        rows = pl.ds(pl.multiple_of((zl ^ a) * 384 + first_row, HEAD_DIM), block.shape[1])
        total += jnp.dot(block[...], w_ref[rows, :], preferred_element_type=jnp.float32)
    out_ref[...] = total.astype(out_ref.dtype)


def outward(other_half, first_row, dtype, info, blocks, w_out, begun=(), after=()):
    depth, width = w_out.shape[0], w_out.shape[1] // 2
    whole = lambda n, info_ref: (0, 0)
    grid_spec = pltpu.PrefetchScalarGridSpec(
        num_scalar_prefetch=1,
        grid=(1,),
        in_specs=[pl.BlockSpec(block.shape, whole) for block in blocks]
        + [pl.BlockSpec((depth, width), lambda n, info_ref: (0, info_ref[3] ^ other_half))]
        + [pl.BlockSpec((256, width), whole)] * len(begun)
        + [pl.BlockSpec(memory_space=pl.ANY)] * len(after),
        out_specs=pl.BlockSpec((256, width), whole),
    )
    return pl.pallas_call(
        functools.partial(outward_kernel, first_row, len(begun)),
        grid_spec=grid_spec,
        out_shape=jax.ShapeDtypeStruct((256, width), dtype),
        compiler_params=pltpu.CompilerParams(vmem_limit_bytes=40 << 20),
        cost_estimate=pl.CostEstimate(
            flops=4 * 256 * blocks[0].shape[1] * width, bytes_accessed=2 * depth * width, transcendentals=0
        ),
    )(info, *blocks, w_out, *begun, *after)


def spread_pairs(a):
    pairs = []
    for z in range(4):
        for x in range(4):
            for c in range(2):
                target = 2 * c + ((z % 2) ^ a)
                pairs.append(((z * 4 + x) * 2 + c, (target * 4 + x) * 2 + ((z // 2) ^ (x % 2))))
    return pairs


def turn(step):
    return [(n, (n + step) % 4) for n in range(4)]


def body(tokens, clip_id, w_qkv, w_out):
    z, y, x, c = [lax.axis_index(name) for name in ("z", "y", "x", "core")]
    zl, zh = z % 2, z // 2
    swap = [(0, 1), (1, 0)]
    info = jnp.stack([zl, y, x, c, zh]).astype(jnp.int32)

    halves = clip_id.reshape(2, SEG)
    counts = jnp.stack([jnp.sum(halves < 1, axis=1), jnp.sum(halves < 2, axis=1)], axis=1)
    header = jnp.pad(counts.astype(jnp.bfloat16), ((0, 14), (0, HEAD_DIM - 2)))

    other = lax.ppermute(tokens, "core", swap)
    both = jnp.where(c == 0, jnp.concatenate([tokens, other], 1), jnp.concatenate([other, tokens], 1))
    own_kv = jnp.einsum("td,sdc->stc", both, w_qkv[1:], preferred_element_type=jnp.float32)
    own_q = jnp.einsum("td,sdc->stc", both, w_qkv[:1], preferred_element_type=jnp.float32)
    own_q = own_q * (1.0 / math.sqrt(HEAD_DIM))

    def to_group(parts, own, after):
        kernel = functools.partial(send_kernel, parts)
        blocks = small_call(kernel, parts * 256 + 16, 384, [own.astype(jnp.bfloat16), header], after, info, 2)
        moved = [lax.ppermute(block, ("z", "x", "core"), spread_pairs(a)) for a, block in enumerate(blocks)]
        return blocks, moved

    _, q_in = to_group(1, own_q, ())
    leaving, kv_in = to_group(2, own_kv, q_in)
    [mine] = small_call(queries_kernel, 544, 384, q_in, leaving[:1])
    queries = [mine] + [lax.ppermute(mine, "x", turn(step)) for step in (1, 2, 3)]
    def key_blocks(head, after=()):
        [own] = small_call(functools.partial(pairs_kernel, head), 1056, HEAD_DIM, kv_in, after)
        return [own] + [lax.ppermute(own, "y", turn(step)) for step in (1, 2, 3)]

    def merged(blocks, after=()):
        [near] = small_call(merge_kernel, KEYS + 128, HEAD_DIM, blocks, after, info)
        return near, lax.ppermute(near, "core", swap)

    kv = key_blocks(0, queries[:1])
    kv_next = key_blocks(1, queries[1:])
    part = attend(0, info, queries, *merged(kv, (*queries[1:], kv_next[0])))
    kv_last = key_blocks(2, (*kv_next[1:], part[0]))
    part = attend(1, info, queries, *merged(kv_next, part[:1]), part)
    last = attend(2, info, queries, *merged(kv_last, part[:1]))

    def gather_results(blocks):
        return [blocks[0]] + [lax.ppermute(blocks[step], "x", turn(step)) for step in (1, 2, 3)]

    def go_back(heads, blocks, after=()):
        kernel = functools.partial(combine_kernel, heads)
        [mixed] = small_call(kernel, 512, heads * HEAD_DIM, gather_results(blocks), after)
        back = []
        for a in range(2):
            returns = [(target, source) for source, target in spread_pairs(a)]
            back.append(lax.ppermute(mixed[256 * a : 256 * (a + 1)], ("z", "x", "core"), returns))
        return mixed, back

    mixed, early = go_back(2, part, last[:1])
    _, late = go_back(1, last, (mixed,))
    there = outward(1, 0, jnp.float32, info, early, w_out)
    here = outward(0, 0, jnp.float32, info, early, w_out)
    there = outward(1, 256, jnp.bfloat16, info, late, w_out, (there,), (here,))
    received = lax.ppermute(there, "core", swap)
    here = outward(0, 256, jnp.float32, info, late, w_out, (here,), (there,))
    return (here + received.astype(jnp.float32)).astype(jnp.bfloat16)


def solution(mesh):
    fine = Mesh(mesh.devices.reshape(4, 4, 4, 2), ("z", "y", "x", "core"))
    seq = ("z", "y", "x")
    in_specs = (P(seq, "core"), P(seq), P(None, None, "core"), P("core", None))
    return jax.shard_map(body, mesh=fine, in_specs=in_specs, out_specs=P(seq, "core"), check_vma=False)
```

```python
import functools
import math

import jax
import jax.numpy as jnp
from jax import lax
from jax.experimental import pallas as pl
from jax.experimental.pallas import tpu as pltpu
from jax.sharding import Mesh
from jax.sharding import PartitionSpec as P

HEAD_DIM = 128
SEG = 128
TILE = 512
KEYS = 4096
NEG = -1e30
FLOOR = -1e29
WIDTHS = (768, 1536, 2048, 2688, 3328, 4096)
VMEM = pl.BlockSpec(memory_space=pltpu.VMEM)
SMEM = pl.BlockSpec(memory_space=pltpu.SMEM)


def send_kernel(parts, info, own_ref, header, *refs):
    out_refs, zl = refs[-2:], info[0]
    for a, out_ref in enumerate(out_refs):
        for group in range(2):

            @pl.when((zl ^ a) == group)
            def _():
                for n in range(parts):
                    out_ref[n * 256 : (n + 1) * 256, :] = own_ref[n, :, group * 384 : (group + 1) * 384]

        for n in range(3):
            out_ref[parts * 256 : parts * 256 + 16, n * HEAD_DIM : (n + 1) * HEAD_DIM] = header[...]


def queries_kernel(*refs):
    blocks, q_ref = refs[:2], refs[-1]
    counts = blocks[0][256:, :].astype(jnp.float32) + blocks[1][256:, :].astype(jnp.float32)
    q_ref[512:, :] = counts.astype(jnp.bfloat16)
    for a, block in enumerate(blocks):
        q_ref[a * 256 : (a + 1) * 256, :] = block[:256, :]


def pairs_kernel(place, *refs):
    blocks, kv_ref = refs[:2], refs[-1]
    cols = slice(place * HEAD_DIM, (place + 1) * HEAD_DIM)
    for a, block in enumerate(blocks):
        kv_ref[a * 512 : (a + 1) * 512, :] = block[:512, cols]
        kv_ref[1024 + 16 * a : 1024 + 16 * (a + 1), :] = block[512:528, cols]


def merge_kernel(info, *refs):
    blocks, out_ref = refs[:4], refs[-1]
    zl, y = info[0], info[1]
    for step, block in enumerate(blocks):
        for a in range(2):
            at = pl.multiple_of(((zl ^ a) * 4 + ((y - step) & 3)) * 256, 256)
            out_ref[pl.ds(at, 256), :] = block[a * 512 : a * 512 + 256, :]
            out_ref[pl.ds(2048 + at, 256), :] = block[a * 512 + 256 : a * 512 + 512, :]
        out_ref[4096 + 32 * step : 4096 + 32 * (step + 1), :] = block[1024:, :]


def small_call(kernel, rows, cols, operands, after=(), info=None, outs=1):
    lead = [] if info is None else [info]
    return pl.pallas_call(
        kernel,
        out_shape=[jax.ShapeDtypeStruct((rows, cols), jnp.bfloat16)] * outs,
        in_specs=[SMEM] * len(lead) + [VMEM] * len(operands) + [pl.BlockSpec(memory_space=pl.ANY)] * len(after),
        out_specs=[VMEM] * outs,
        compiler_params=pltpu.CompilerParams(vmem_limit_bytes=32 << 20),
    )(*lead, *operands, *after)


def attend_kernel(head, info, *refs):
    q_refs, (near, far), refs = refs[:4], refs[4:6], refs[6:]
    before, refs = (refs[:4], refs[4:]) if head == 1 else ((), refs[-12:])
    o_refs, (queries, keys, vals, scores, tops, sums, flat, outs) = refs[:4], refs[4:]
    base = 0
    for old, o_ref in zip(before, o_refs):
        base = old.shape[0]
        o_ref[:base, :] = old[...]
    zl, y, x, c = [info[n] for n in range(4)]
    lane = lax.broadcasted_iota(jnp.int32, (SEG, HEAD_DIM), 1)
    row = lax.broadcasted_iota(jnp.int32, (SEG, HEAD_DIM), 0)

    def bounds(lines):
        found = sum(line.astype(jnp.float32) for line in lines)
        return [
            jnp.sum(jnp.where(lane[:16] == n, found, 0.0), keepdims=True)[0, 0].astype(jnp.int32)
            for n in range(2)
        ]

    n1, n2 = bounds([ref[KEYS + 16 * n : KEYS + 16 * (n + 1), :] for ref in (near, far) for n in range(8)])
    m1, m2 = bounds([ref[512:, :HEAD_DIM] for ref in q_refs])

    def clip_of(index, first, second):
        return (index >= first).astype(jnp.int32) + (index >= second).astype(jnp.int32)

    for n in range(KEYS // SEG):
        own = clip_of(row + n * SEG, n1, n2) == lane
        keys[n * SEG : (n + 1) * SEG, HEAD_DIM:] = own.astype(jnp.float32).astype(jnp.bfloat16)
    for n in range(2048 // SEG):
        differs = (clip_of(row + n * SEG, m1, m2) != lane) & (lane < 3)
        queries[n * SEG : (n + 1) * SEG, HEAD_DIM:] = jnp.where(differs, NEG, 0.0).astype(jnp.bfloat16)
    vals[:, HEAD_DIM:] = jnp.ones((KEYS, HEAD_DIM), jnp.bfloat16)
    cols = slice(head * HEAD_DIM, (head + 1) * HEAD_DIM)
    for step in range(4):
        xx = (x - step) & 3
        for a in range(2):
            zz = 2 * (c ^ (xx & 1)) + (zl ^ a)
            at = pl.multiple_of(zz * TILE + (xx >> 1) * 256, 256)
            queries[pl.ds(at, 256), :HEAD_DIM] = q_refs[step][a * 256 : (a + 1) * 256, cols]
    zh = c ^ (x & 1)
    for part, ref in ((zh, near), (1 - zh, far)):
        at = pl.ds(pl.multiple_of(part * 2048, 2048), 2048)
        keys[at, :HEAD_DIM] = ref[:2048, :]
        vals[at, :HEAD_DIM] = ref[2048:4096, :]

    eye = (lane == row).astype(jnp.float32)
    sub = lax.broadcasted_iota(jnp.int32, (16, HEAD_DIM), 0)

    def tile(zz, carry):
        first, last = zz * TILE, zz * TILE + TILE - 1
        low = jnp.where(first >= m2, n2, jnp.where(first >= m1, n1, 0))
        high = jnp.where(last >= m2, KEYS, jnp.where(last >= m1, n2, n1))
        low = (low // SEG) * SEG
        need = high - low
        rows = pl.ds(pl.multiple_of(first, TILE), TILE)
        tops[...] = jnp.full((TILE, HEAD_DIM), NEG, jnp.float32)
        sums[...] = jnp.zeros((TILE, 2 * HEAD_DIM), jnp.float32)

        def runs(k):
            under = WIDTHS[k - 1] if k else 0
            return ((need > under) & (need <= WIDTHS[k])).astype(jnp.int32)

        for k, width in enumerate(WIDTHS):
            at = pl.multiple_of(jnp.minimum(low, KEYS - width), SEG)

            def first_pass(i, carry, width=width, at=at):
                s = lax.dot_general(
                    queries[rows, :],
                    keys[pl.ds(at, width), :],
                    (((1,), (1,)), ((), ())),
                    preferred_element_type=jnp.float32,
                )
                scores[:, :width] = s
                top = s[:, :128]
                for n in range(1, width // 128):
                    top = jnp.maximum(top, s[:, n * 128 : (n + 1) * 128])
                tops[...] = top
                return carry

            lax.fori_loop(0, runs(k), first_pass, 0)

        top = jnp.maximum(jnp.max(tops[...], axis=1, keepdims=True), FLOOR)

        for k, width in enumerate(WIDTHS):
            at = pl.multiple_of(jnp.minimum(low, KEYS - width), SEG)

            def second_pass(i, carry, width=width, at=at):
                weights = jnp.exp(scores[:, :width] - top).astype(jnp.bfloat16)
                sums[...] = jnp.dot(weights, vals[pl.ds(at, width), :], preferred_element_type=jnp.float32)
                return carry

            lax.fori_loop(0, runs(k), second_pass, 0)

        total = jnp.maximum(sums[:, HEAD_DIM:], 1e-30)
        flat[...] = (sums[:, :HEAD_DIM] / total).astype(jnp.bfloat16)
        tops[...] = top + jnp.log(total)
        a = (zz & 1) ^ zl
        for pair in range(2):
            xx = ((zz >> 1) ^ c) + 2 * pair
            step = (xx - x) & 3
            for half in range(2):
                at = slice(pair * 256 + half * SEG, pair * 256 + (half + 1) * SEG)
                to = pl.multiple_of(a * 256 + half * SEG, SEG)
                outs[step, pl.ds(to, SEG), :] = flat[at, :]
                line = jnp.sum(tops[at, :] * eye, axis=0, keepdims=True)
                big = line.astype(jnp.bfloat16).astype(jnp.float32)
                middle = (line - big).astype(jnp.bfloat16).astype(jnp.float32)
                rest = line - big - middle
                parts = jnp.where(sub == 0, big, jnp.where(sub == 1, middle, jnp.where(sub == 2, rest, 0.0)))
                to = pl.multiple_of(512 + (2 * a + half) * 16, 16)
                outs[step, pl.ds(to, 16), :] = parts.astype(jnp.bfloat16)
        return carry

    lax.fori_loop(0, 4, tile, 0)
    for step in range(4):
        o_refs[step][base:, :] = outs[step]


def attend(head, info, queries, near, far, before=(), after=()):
    return pl.pallas_call(
        functools.partial(attend_kernel, head),
        out_shape=[jax.ShapeDtypeStruct(((2 if before else 1) * (4 * SEG + 64), HEAD_DIM), jnp.bfloat16)] * 4,
        in_specs=[SMEM] + [VMEM] * (6 + len(before)) + [pl.BlockSpec(memory_space=pl.ANY)] * len(after),
        out_specs=[VMEM] * 4,
        scratch_shapes=[
            pltpu.VMEM((2048, 2 * HEAD_DIM), jnp.bfloat16),
            pltpu.VMEM((KEYS, 2 * HEAD_DIM), jnp.bfloat16),
            pltpu.VMEM((KEYS, 2 * HEAD_DIM), jnp.bfloat16),
            pltpu.VMEM((TILE, KEYS), jnp.float32),
            pltpu.VMEM((TILE, HEAD_DIM), jnp.float32),
            pltpu.VMEM((TILE, 2 * HEAD_DIM), jnp.float32),
            pltpu.VMEM((TILE, HEAD_DIM), jnp.bfloat16),
            pltpu.VMEM((4, 4 * SEG + 64, HEAD_DIM), jnp.bfloat16),
        ],
        compiler_params=pltpu.CompilerParams(vmem_limit_bytes=48 << 20),
        cost_estimate=pl.CostEstimate(
            flops=2 * 2 * 2048 * 4096 * 128, bytes_accessed=4 << 20, transcendentals=2048 * 4096
        ),
    )(info, *queries, near, far, *before, *after)


def combine_kernel(heads, *refs):
    parts, out_ref = refs[:4], refs[-1]
    eye = (
        lax.broadcasted_iota(jnp.int32, (SEG, SEG), 0)
        == lax.broadcasted_iota(jnp.int32, (SEG, SEG), 1)
    ).astype(jnp.float32)
    for head in range(heads):
        base = head * (4 * SEG + 64)
        for slot in range(4):
            levels = []
            for part in parts:
                at = base + 4 * SEG + slot * 16
                lines = part[at : at + 16, :].astype(jnp.float32)
                levels.append(jnp.sum(lines, axis=0, keepdims=True))
            top = functools.reduce(jnp.maximum, levels)
            shares = [jnp.exp(level - top) for level in levels]
            total = functools.reduce(jnp.add, shares)
            spread = jnp.concatenate([eye * (share / total) for share in shares], axis=1)
            at = base + slot * SEG
            stacked = jnp.concatenate([part[at : at + SEG, :] for part in parts], axis=0)
            mixed = jnp.dot(spread.astype(jnp.bfloat16), stacked, preferred_element_type=jnp.float32)
            rows = slice(slot * SEG, (slot + 1) * SEG)
            out_ref[rows, head * HEAD_DIM : (head + 1) * HEAD_DIM] = mixed.astype(jnp.bfloat16)


def outward_kernel(first_row, begun, info, first_ref, second_ref, w_ref, *refs):
    out_ref, zl = refs[-1], info[0]
    total = refs[0][...] if begun else 0.0
    for a, block in enumerate((first_ref, second_ref)):
        rows = pl.ds(pl.multiple_of((zl ^ a) * 384 + first_row, HEAD_DIM), block.shape[1])
        total += jnp.dot(block[...], w_ref[rows, :], preferred_element_type=jnp.float32)
    out_ref[...] = total.astype(out_ref.dtype)


def outward(other_half, first_row, dtype, info, blocks, w_out, begun=(), after=()):
    depth, width = w_out.shape[0], w_out.shape[1] // 2
    whole = lambda n, info_ref: (0, 0)
    grid_spec = pltpu.PrefetchScalarGridSpec(
        num_scalar_prefetch=1,
        grid=(1,),
        in_specs=[pl.BlockSpec(block.shape, whole) for block in blocks]
        + [pl.BlockSpec((depth, width), lambda n, info_ref: (0, info_ref[3] ^ other_half))]
        + [pl.BlockSpec((256, width), whole)] * len(begun)
        + [pl.BlockSpec(memory_space=pl.ANY)] * len(after),
        out_specs=pl.BlockSpec((256, width), whole),
    )
    return pl.pallas_call(
        functools.partial(outward_kernel, first_row, len(begun)),
        grid_spec=grid_spec,
        out_shape=jax.ShapeDtypeStruct((256, width), dtype),
        compiler_params=pltpu.CompilerParams(vmem_limit_bytes=40 << 20),
        cost_estimate=pl.CostEstimate(
            flops=4 * 256 * blocks[0].shape[1] * width, bytes_accessed=2 * depth * width, transcendentals=0
        ),
    )(info, *blocks, w_out, *begun, *after)


def spread_pairs(a):
    pairs = []
    for z in range(4):
        for x in range(4):
            for c in range(2):
                target = 2 * c + ((z % 2) ^ a)
                pairs.append(((z * 4 + x) * 2 + c, (target * 4 + x) * 2 + ((z // 2) ^ (x % 2))))
    return pairs


def turn(step):
    return [(n, (n + step) % 4) for n in range(4)]


def body(tokens, clip_id, w_qkv, w_out):
    z, y, x, c = [lax.axis_index(name) for name in ("z", "y", "x", "core")]
    zl, zh = z % 2, z // 2
    swap = [(0, 1), (1, 0)]
    info = jnp.stack([zl, y, x, c, zh]).astype(jnp.int32)

    halves = clip_id.reshape(2, SEG)
    counts = jnp.stack([jnp.sum(halves < 1, axis=1), jnp.sum(halves < 2, axis=1)], axis=1)
    header = jnp.pad(counts.astype(jnp.bfloat16), ((0, 14), (0, HEAD_DIM - 2)))

    other = lax.ppermute(tokens, "core", swap)
    both = jnp.where(c == 0, jnp.concatenate([tokens, other], 1), jnp.concatenate([other, tokens], 1))
    own_kv = jnp.einsum("td,sdc->stc", both, w_qkv[1:], preferred_element_type=jnp.float32)
    own_q = jnp.einsum("td,sdc->stc", both, w_qkv[:1], preferred_element_type=jnp.float32)
    own_q = own_q * (1.0 / math.sqrt(HEAD_DIM))

    def to_group(parts, own, after):
        kernel = functools.partial(send_kernel, parts)
        blocks = small_call(kernel, parts * 256 + (16 if parts == 1 else 32), 384, [own.astype(jnp.bfloat16), header], after, info, 2)
        moved = [lax.ppermute(block, ("z", "x", "core"), spread_pairs(a)) for a, block in enumerate(blocks)]
        return blocks, moved

    leaving, q_in = to_group(1, own_q, ())
    leaving, kv_in = to_group(2, own_kv, leaving[:1])
    [mine] = small_call(queries_kernel, 528, 384, q_in, leaving[:1])
    queries = [mine] + [lax.ppermute(mine, "x", turn(step)) for step in (1, 2, 3)]
    def key_blocks(head, after=()):
        [own] = small_call(functools.partial(pairs_kernel, head), 1056, HEAD_DIM, kv_in, after)
        return [own] + [lax.ppermute(own, "y", turn(step)) for step in (1, 2, 3)]

    def merged(blocks, after=()):
        [near] = small_call(merge_kernel, KEYS + 128, HEAD_DIM, blocks, after, info)
        return near, lax.ppermute(near, "core", swap)

    kv = key_blocks(0, queries[:1])
    kv_next = key_blocks(1, queries[1:])
    part = attend(0, info, queries, *merged(kv, (*queries[1:], kv_next[0])))
    kv_last = key_blocks(2, (*kv_next[1:], part[0]))
    part = attend(1, info, queries, *merged(kv_next, part[:1]), part)
    last = attend(2, info, queries, *merged(kv_last, part[:1]))

    def gather_results(blocks):
        return [blocks[0]] + [lax.ppermute(blocks[step], "x", turn(step)) for step in (1, 2, 3)]

    def go_back(heads, blocks, after=()):
        kernel = functools.partial(combine_kernel, heads)
        [mixed] = small_call(kernel, 512, heads * HEAD_DIM, gather_results(blocks), after)
        back = []
        for a in range(2):
            returns = [(target, source) for source, target in spread_pairs(a)]
            back.append(lax.ppermute(mixed[256 * a : 256 * (a + 1)], ("z", "x", "core"), returns))
        return mixed, back

    mixed, early = go_back(2, part, last[:1])
    _, late = go_back(1, last, (mixed,))
    there = outward(1, 0, jnp.float32, info, early, w_out)
    here = outward(0, 0, jnp.float32, info, early, w_out)
    there = outward(1, 256, jnp.bfloat16, info, late, w_out, (there,), (here,))
    received = lax.ppermute(there, "core", swap)
    here = outward(0, 256, jnp.float32, info, late, w_out, (here,), (there,))
    return (here + received.astype(jnp.float32)).astype(jnp.bfloat16)


def solution(mesh):
    fine = Mesh(mesh.devices.reshape(4, 4, 4, 2), ("z", "y", "x", "core"))
    seq = ("z", "y", "x")
    in_specs = (P(seq, "core"), P(seq), P(None, None, "core"), P("core", None))
    return jax.shard_map(body, mesh=fine, in_specs=in_specs, out_specs=P(seq, "core"), check_vma=False)
```

```python
import functools
import math

import jax
import jax.numpy as jnp
from jax import lax
from jax.experimental import pallas as pl
from jax.experimental.pallas import tpu as pltpu
from jax.sharding import Mesh
from jax.sharding import PartitionSpec as P

HEAD_DIM = 128
SEG = 128
TILE = 512
KEYS = 4096
NEG = -1e30
FLOOR = -1e29
WIDTHS = (768, 1536, 2048, 2688, 3328, 4096)
VMEM = pl.BlockSpec(memory_space=pltpu.VMEM)
SMEM = pl.BlockSpec(memory_space=pltpu.SMEM)


def own_kernel(info, own_ref, w_ref, out_ref):
    out_ref[...] = jnp.dot(own_ref[...], w_ref[0], preferred_element_type=jnp.float32)


def other_kernel(info, other_ref, w_ref, begun, header, *out_refs):
    total = begun[...] + jnp.dot(other_ref[...], w_ref[0], preferred_element_type=jnp.float32)
    made = (total * (1.0 / math.sqrt(HEAD_DIM))).astype(jnp.bfloat16)
    for a, out_ref in enumerate(out_refs):
        for group in range(2):

            @pl.when((info[0] ^ a) == group)
            def _():
                out_ref[:256, :] = made[:, group * 384 : (group + 1) * 384]

        for n in range(3):
            out_ref[256:, n * HEAD_DIM : (n + 1) * HEAD_DIM] = header[...]


def project(kernel, which, info, tokens, w_qkv, operands, shapes):
    depth, width = tokens.shape[1], w_qkv.shape[2]
    whole = lambda n, info_ref: (0, 0)
    grid_spec = pltpu.PrefetchScalarGridSpec(
        num_scalar_prefetch=1,
        grid=(1,),
        in_specs=[
            pl.BlockSpec(tokens.shape, whole),
            pl.BlockSpec((1, depth, width), lambda n, info_ref: (0, info_ref[3] ^ which, 0)),
        ]
        + [pl.BlockSpec(operand.shape, whole) for operand in operands],
        out_specs=[pl.BlockSpec(shape.shape, whole) for shape in shapes],
    )
    return pl.pallas_call(
        kernel,
        grid_spec=grid_spec,
        out_shape=shapes,
        compiler_params=pltpu.CompilerParams(vmem_limit_bytes=40 << 20),
        cost_estimate=pl.CostEstimate(
            flops=2 * 256 * depth * width, bytes_accessed=2 * depth * width, transcendentals=0
        ),
    )(info, tokens, w_qkv, *operands)


def send_kernel(parts, info, own_ref, header, *refs):
    out_refs, zl = refs[-2:], info[0]
    for a, out_ref in enumerate(out_refs):
        for group in range(2):

            @pl.when((zl ^ a) == group)
            def _():
                for n in range(parts):
                    out_ref[n * 256 : (n + 1) * 256, :] = own_ref[n, :, group * 384 : (group + 1) * 384]

        for n in range(3):
            out_ref[parts * 256 : parts * 256 + 16, n * HEAD_DIM : (n + 1) * HEAD_DIM] = header[...]


def queries_kernel(*refs):
    blocks, q_ref = refs[:2], refs[-1]
    counts = blocks[0][256:, :].astype(jnp.float32) + blocks[1][256:, :].astype(jnp.float32)
    q_ref[512:, :] = counts.astype(jnp.bfloat16)
    for a, block in enumerate(blocks):
        q_ref[a * 256 : (a + 1) * 256, :] = block[:256, :]


def pairs_kernel(place, *refs):
    blocks, kv_ref = refs[:2], refs[-1]
    cols = slice(place * HEAD_DIM, (place + 1) * HEAD_DIM)
    for a, block in enumerate(blocks):
        kv_ref[a * 512 : (a + 1) * 512, :] = block[:512, cols]
        kv_ref[1024 + 16 * a : 1024 + 16 * (a + 1), :] = block[512:528, cols]


def merge_kernel(info, *refs):
    blocks, out_ref = refs[:4], refs[-1]
    zl, y = info[0], info[1]
    for step, block in enumerate(blocks):
        for a in range(2):
            at = pl.multiple_of(((zl ^ a) * 4 + ((y - step) & 3)) * 256, 256)
            out_ref[pl.ds(at, 256), :] = block[a * 512 : a * 512 + 256, :]
            out_ref[pl.ds(2048 + at, 256), :] = block[a * 512 + 256 : a * 512 + 512, :]
        out_ref[4096 + 32 * step : 4096 + 32 * (step + 1), :] = block[1024:, :]


def small_call(kernel, rows, cols, operands, after=(), info=None, outs=1):
    lead = [] if info is None else [info]
    return pl.pallas_call(
        kernel,
        out_shape=[jax.ShapeDtypeStruct((rows, cols), jnp.bfloat16)] * outs,
        in_specs=[SMEM] * len(lead) + [VMEM] * len(operands) + [pl.BlockSpec(memory_space=pl.ANY)] * len(after),
        out_specs=[VMEM] * outs,
        compiler_params=pltpu.CompilerParams(vmem_limit_bytes=32 << 20),
    )(*lead, *operands, *after)


def attend_kernel(head, info, *refs):
    q_refs, (near, far), refs = refs[:4], refs[4:6], refs[6:]
    before, refs = (refs[:4], refs[4:]) if head == 1 else ((), refs[-12:])
    o_refs, (queries, keys, vals, scores, tops, sums, flat, outs) = refs[:4], refs[4:]
    base = 0
    for old, o_ref in zip(before, o_refs):
        base = old.shape[0]
        o_ref[:base, :] = old[...]
    zl, y, x, c = [info[n] for n in range(4)]
    lane = lax.broadcasted_iota(jnp.int32, (SEG, HEAD_DIM), 1)
    row = lax.broadcasted_iota(jnp.int32, (SEG, HEAD_DIM), 0)

    def bounds(lines):
        found = sum(line.astype(jnp.float32) for line in lines)
        return [
            jnp.sum(jnp.where(lane[:16] == n, found, 0.0), keepdims=True)[0, 0].astype(jnp.int32)
            for n in range(2)
        ]

    n1, n2 = bounds([ref[KEYS + 16 * n : KEYS + 16 * (n + 1), :] for ref in (near, far) for n in range(8)])
    m1, m2 = bounds([ref[512:, :HEAD_DIM] for ref in q_refs])

    def clip_of(index, first, second):
        return (index >= first).astype(jnp.int32) + (index >= second).astype(jnp.int32)

    for n in range(KEYS // SEG):
        own = clip_of(row + n * SEG, n1, n2) == lane
        keys[n * SEG : (n + 1) * SEG, HEAD_DIM:] = own.astype(jnp.float32).astype(jnp.bfloat16)
    for n in range(2048 // SEG):
        differs = (clip_of(row + n * SEG, m1, m2) != lane) & (lane < 3)
        queries[n * SEG : (n + 1) * SEG, HEAD_DIM:] = jnp.where(differs, NEG, 0.0).astype(jnp.bfloat16)
    vals[:, HEAD_DIM:] = jnp.ones((KEYS, HEAD_DIM), jnp.bfloat16)
    cols = slice(head * HEAD_DIM, (head + 1) * HEAD_DIM)
    for step in range(4):
        xx = (x - step) & 3
        for a in range(2):
            zz = 2 * (c ^ (xx & 1)) + (zl ^ a)
            at = pl.multiple_of(zz * TILE + (xx >> 1) * 256, 256)
            queries[pl.ds(at, 256), :HEAD_DIM] = q_refs[step][a * 256 : (a + 1) * 256, cols]
    zh = c ^ (x & 1)
    for part, ref in ((zh, near), (1 - zh, far)):
        at = pl.ds(pl.multiple_of(part * 2048, 2048), 2048)
        keys[at, :HEAD_DIM] = ref[:2048, :]
        vals[at, :HEAD_DIM] = ref[2048:4096, :]

    eye = (lane == row).astype(jnp.float32)
    sub = lax.broadcasted_iota(jnp.int32, (16, HEAD_DIM), 0)

    def tile(zz, carry):
        first, last = zz * TILE, zz * TILE + TILE - 1
        low = jnp.where(first >= m2, n2, jnp.where(first >= m1, n1, 0))
        high = jnp.where(last >= m2, KEYS, jnp.where(last >= m1, n2, n1))
        low = (low // SEG) * SEG
        need = high - low
        rows = pl.ds(pl.multiple_of(first, TILE), TILE)
        tops[...] = jnp.full((TILE, HEAD_DIM), NEG, jnp.float32)
        sums[...] = jnp.zeros((TILE, 2 * HEAD_DIM), jnp.float32)

        def runs(k):
            under = WIDTHS[k - 1] if k else 0
            return ((need > under) & (need <= WIDTHS[k])).astype(jnp.int32)

        for k, width in enumerate(WIDTHS):
            at = pl.multiple_of(jnp.minimum(low, KEYS - width), SEG)

            def first_pass(i, carry, width=width, at=at):
                s = lax.dot_general(
                    queries[rows, :],
                    keys[pl.ds(at, width), :],
                    (((1,), (1,)), ((), ())),
                    preferred_element_type=jnp.float32,
                )
                scores[:, :width] = s
                top = s[:, :128]
                for n in range(1, width // 128):
                    top = jnp.maximum(top, s[:, n * 128 : (n + 1) * 128])
                tops[...] = top
                return carry

            lax.fori_loop(0, runs(k), first_pass, 0)

        top = jnp.maximum(jnp.max(tops[...], axis=1, keepdims=True), FLOOR)

        for k, width in enumerate(WIDTHS):
            at = pl.multiple_of(jnp.minimum(low, KEYS - width), SEG)

            def second_pass(i, carry, width=width, at=at):
                weights = jnp.exp(scores[:, :width] - top).astype(jnp.bfloat16)
                sums[...] = jnp.dot(weights, vals[pl.ds(at, width), :], preferred_element_type=jnp.float32)
                return carry

            lax.fori_loop(0, runs(k), second_pass, 0)

        total = jnp.maximum(sums[:, HEAD_DIM:], 1e-30)
        flat[...] = (sums[:, :HEAD_DIM] / total).astype(jnp.bfloat16)
        tops[...] = top + jnp.log(total)
        a = (zz & 1) ^ zl
        for pair in range(2):
            xx = ((zz >> 1) ^ c) + 2 * pair
            step = (xx - x) & 3
            for half in range(2):
                at = slice(pair * 256 + half * SEG, pair * 256 + (half + 1) * SEG)
                to = pl.multiple_of(a * 256 + half * SEG, SEG)
                outs[step, pl.ds(to, SEG), :] = flat[at, :]
                line = jnp.sum(tops[at, :] * eye, axis=0, keepdims=True)
                big = line.astype(jnp.bfloat16).astype(jnp.float32)
                middle = (line - big).astype(jnp.bfloat16).astype(jnp.float32)
                rest = line - big - middle
                parts = jnp.where(sub == 0, big, jnp.where(sub == 1, middle, jnp.where(sub == 2, rest, 0.0)))
                to = pl.multiple_of(512 + (2 * a + half) * 16, 16)
                outs[step, pl.ds(to, 16), :] = parts.astype(jnp.bfloat16)
        return carry

    lax.fori_loop(0, 4, tile, 0)
    for step in range(4):
        o_refs[step][base:, :] = outs[step]


def attend(head, info, queries, near, far, before=(), after=()):
    return pl.pallas_call(
        functools.partial(attend_kernel, head),
        out_shape=[jax.ShapeDtypeStruct(((2 if before else 1) * (4 * SEG + 64), HEAD_DIM), jnp.bfloat16)] * 4,
        in_specs=[SMEM] + [VMEM] * (6 + len(before)) + [pl.BlockSpec(memory_space=pl.ANY)] * len(after),
        out_specs=[VMEM] * 4,
        scratch_shapes=[
            pltpu.VMEM((2048, 2 * HEAD_DIM), jnp.bfloat16),
            pltpu.VMEM((KEYS, 2 * HEAD_DIM), jnp.bfloat16),
            pltpu.VMEM((KEYS, 2 * HEAD_DIM), jnp.bfloat16),
            pltpu.VMEM((TILE, KEYS), jnp.float32),
            pltpu.VMEM((TILE, HEAD_DIM), jnp.float32),
            pltpu.VMEM((TILE, 2 * HEAD_DIM), jnp.float32),
            pltpu.VMEM((TILE, HEAD_DIM), jnp.bfloat16),
            pltpu.VMEM((4, 4 * SEG + 64, HEAD_DIM), jnp.bfloat16),
        ],
        compiler_params=pltpu.CompilerParams(vmem_limit_bytes=48 << 20),
        cost_estimate=pl.CostEstimate(
            flops=2 * 2 * 2048 * 4096 * 128, bytes_accessed=4 << 20, transcendentals=2048 * 4096
        ),
    )(info, *queries, near, far, *before, *after)


def combine_kernel(heads, *refs):
    parts, out_ref = refs[:4], refs[-1]
    eye = (
        lax.broadcasted_iota(jnp.int32, (SEG, SEG), 0)
        == lax.broadcasted_iota(jnp.int32, (SEG, SEG), 1)
    ).astype(jnp.float32)
    for head in range(heads):
        base = head * (4 * SEG + 64)
        for slot in range(4):
            levels = []
            for part in parts:
                at = base + 4 * SEG + slot * 16
                lines = part[at : at + 16, :].astype(jnp.float32)
                levels.append(jnp.sum(lines, axis=0, keepdims=True))
            top = functools.reduce(jnp.maximum, levels)
            shares = [jnp.exp(level - top) for level in levels]
            total = functools.reduce(jnp.add, shares)
            spread = jnp.concatenate([eye * (share / total) for share in shares], axis=1)
            at = base + slot * SEG
            stacked = jnp.concatenate([part[at : at + SEG, :] for part in parts], axis=0)
            mixed = jnp.dot(spread.astype(jnp.bfloat16), stacked, preferred_element_type=jnp.float32)
            rows = slice(slot * SEG, (slot + 1) * SEG)
            out_ref[rows, head * HEAD_DIM : (head + 1) * HEAD_DIM] = mixed.astype(jnp.bfloat16)


def outward_kernel(first_row, begun, info, first_ref, second_ref, w_ref, *refs):
    out_ref, zl = refs[-1], info[0]
    total = refs[0][...] if begun else 0.0
    for a, block in enumerate((first_ref, second_ref)):
        rows = pl.ds(pl.multiple_of((zl ^ a) * 384 + first_row, HEAD_DIM), block.shape[1])
        total += jnp.dot(block[...], w_ref[rows, :], preferred_element_type=jnp.float32)
    out_ref[...] = total.astype(out_ref.dtype)


def outward(other_half, first_row, dtype, info, blocks, w_out, begun=(), after=()):
    depth, width = w_out.shape[0], w_out.shape[1] // 2
    whole = lambda n, info_ref: (0, 0)
    grid_spec = pltpu.PrefetchScalarGridSpec(
        num_scalar_prefetch=1,
        grid=(1,),
        in_specs=[pl.BlockSpec(block.shape, whole) for block in blocks]
        + [pl.BlockSpec((depth, width), lambda n, info_ref: (0, info_ref[3] ^ other_half))]
        + [pl.BlockSpec((256, width), whole)] * len(begun)
        + [pl.BlockSpec(memory_space=pl.ANY)] * len(after),
        out_specs=pl.BlockSpec((256, width), whole),
    )
    return pl.pallas_call(
        functools.partial(outward_kernel, first_row, len(begun)),
        grid_spec=grid_spec,
        out_shape=jax.ShapeDtypeStruct((256, width), dtype),
        compiler_params=pltpu.CompilerParams(vmem_limit_bytes=40 << 20),
        cost_estimate=pl.CostEstimate(
            flops=4 * 256 * blocks[0].shape[1] * width, bytes_accessed=2 * depth * width, transcendentals=0
        ),
    )(info, *blocks, w_out, *begun, *after)


def spread_pairs(a):
    pairs = []
    for z in range(4):
        for x in range(4):
            for c in range(2):
                target = 2 * c + ((z % 2) ^ a)
                pairs.append(((z * 4 + x) * 2 + c, (target * 4 + x) * 2 + ((z // 2) ^ (x % 2))))
    return pairs


def turn(step):
    return [(n, (n + step) % 4) for n in range(4)]


def body(tokens, clip_id, w_qkv, w_out):
    z, y, x, c = [lax.axis_index(name) for name in ("z", "y", "x", "core")]
    zl, zh = z % 2, z // 2
    swap = [(0, 1), (1, 0)]
    info = jnp.stack([zl, y, x, c, zh]).astype(jnp.int32)

    halves = clip_id.reshape(2, SEG)
    counts = jnp.stack([jnp.sum(halves < 1, axis=1), jnp.sum(halves < 2, axis=1)], axis=1)
    header = jnp.pad(counts.astype(jnp.bfloat16), ((0, 14), (0, HEAD_DIM - 2)))

    other = lax.ppermute(tokens, "core", swap)
    both = jnp.where(c == 0, jnp.concatenate([tokens, other], 1), jnp.concatenate([other, tokens], 1))
    own_kv = jnp.einsum("td,sdc->stc", both, w_qkv[1:], preferred_element_type=jnp.float32)
    w_q = w_qkv[:1]
    [begun] = project(
        own_kernel, 0, info, tokens, w_q, [], [jax.ShapeDtypeStruct((256, w_qkv.shape[2]), jnp.float32)]
    )
    leaving = project(
        other_kernel, 1, info, other, w_q, [begun, header], [jax.ShapeDtypeStruct((272, 384), jnp.bfloat16)] * 2
    )

    def to_group(blocks):
        return [lax.ppermute(block, ("z", "x", "core"), spread_pairs(a)) for a, block in enumerate(blocks)]

    q_in = to_group(leaving)
    operands = [own_kv.astype(jnp.bfloat16), header]
    leaving = small_call(functools.partial(send_kernel, 2), 544, 384, operands, leaving[:1], info, 2)
    kv_in = to_group(leaving)
    [mine] = small_call(queries_kernel, 528, 384, q_in, leaving[:1])
    beside = [lax.ppermute(mine, "x", turn(step)) for step in (1, 3)]
    def key_blocks(head, after=()):
        [own] = small_call(functools.partial(pairs_kernel, head), 1056, HEAD_DIM, kv_in, after)
        return [own] + [lax.ppermute(own, "y", turn(step)) for step in (1, 2, 3)]

    def merged(blocks, after=()):
        [near] = small_call(merge_kernel, KEYS + 128, HEAD_DIM, blocks, after, info)
        return near, lax.ppermute(near, "core", swap)

    kv = key_blocks(0, (mine,))
    [again] = small_call(queries_kernel, 528, 384, q_in, (*beside, kv[0]))
    queries = [mine, beside[0], lax.ppermute(again, "x", turn(2)), beside[1]]
    kv_next = key_blocks(1, queries[1:])
    part = attend(0, info, queries, *merged(kv, (*queries[1:], kv_next[0])))
    kv_last = key_blocks(2, (*kv_next[1:], part[0]))
    part = attend(1, info, queries, *merged(kv_next, part[:1]), part)
    last = attend(2, info, queries, *merged(kv_last, part[:1]))

    def gather_results(blocks):
        return [blocks[0]] + [lax.ppermute(blocks[step], "x", turn(step)) for step in (1, 2, 3)]

    def go_back(heads, blocks, after=()):
        kernel = functools.partial(combine_kernel, heads)
        [mixed] = small_call(kernel, 512, heads * HEAD_DIM, gather_results(blocks), after)
        back = []
        for a in range(2):
            returns = [(target, source) for source, target in spread_pairs(a)]
            back.append(lax.ppermute(mixed[256 * a : 256 * (a + 1)], ("z", "x", "core"), returns))
        return mixed, back

    mixed, early = go_back(2, part, last[:1])
    _, late = go_back(1, last, (mixed,))
    there = outward(1, 0, jnp.float32, info, early, w_out)
    here = outward(0, 0, jnp.float32, info, early, w_out)
    there = outward(1, 256, jnp.bfloat16, info, late, w_out, (there,), (here,))
    received = lax.ppermute(there, "core", swap)
    here = outward(0, 256, jnp.float32, info, late, w_out, (here,), (there,))
    return (here + received.astype(jnp.float32)).astype(jnp.bfloat16)


def solution(mesh):
    fine = Mesh(mesh.devices.reshape(4, 4, 4, 2), ("z", "y", "x", "core"))
    seq = ("z", "y", "x")
    in_specs = (P(seq, "core"), P(seq), P(None, None, "core"), P("core", None))
    return jax.shard_map(body, mesh=fine, in_specs=in_specs, out_specs=P(seq, "core"), check_vma=False)
```

```python
import functools
import math

import jax
import jax.numpy as jnp
from jax import lax
from jax.experimental import pallas as pl
from jax.experimental.pallas import tpu as pltpu
from jax.sharding import Mesh
from jax.sharding import PartitionSpec as P

HEAD_DIM = 128
SEG = 128
TILE = 512
KEYS = 4096
NEG = -1e30
FLOOR = -1e29
WIDTHS = (512, 1024, 1536, 2048, 2688, 3200, 3712, 4096)
VMEM = pl.BlockSpec(memory_space=pltpu.VMEM)
SMEM = pl.BlockSpec(memory_space=pltpu.SMEM)


def send_kernel(parts, info, own_ref, header, *refs):
    out_refs, zl = refs[-2:], info[0]
    for a, out_ref in enumerate(out_refs):
        for group in range(2):

            @pl.when((zl ^ a) == group)
            def _():
                for n in range(parts):
                    out_ref[n * 256 : (n + 1) * 256, :] = own_ref[n, :, group * 384 : (group + 1) * 384]

        for n in range(3):
            out_ref[parts * 256 : parts * 256 + 16, n * HEAD_DIM : (n + 1) * HEAD_DIM] = header[...]


def queries_kernel(*refs):
    blocks, q_ref = refs[:2], refs[-1]
    counts = blocks[0][256:, :].astype(jnp.float32) + blocks[1][256:, :].astype(jnp.float32)
    q_ref[512:, :] = counts.astype(jnp.bfloat16)
    for a, block in enumerate(blocks):
        q_ref[a * 256 : (a + 1) * 256, :] = block[:256, :]


def pairs_kernel(place, *refs):
    blocks, kv_ref = refs[:2], refs[-1]
    cols = slice(place * HEAD_DIM, (place + 1) * HEAD_DIM)
    for a, block in enumerate(blocks):
        kv_ref[a * 512 : (a + 1) * 512, :] = block[:512, cols]
        kv_ref[1024 + 16 * a : 1024 + 16 * (a + 1), :] = block[512:528, cols]


def merge_kernel(info, *refs):
    blocks, out_ref = refs[:4], refs[-1]
    zl, y = info[0], info[1]
    for step, block in enumerate(blocks):
        for a in range(2):
            at = pl.multiple_of(((zl ^ a) * 4 + ((y - step) & 3)) * 256, 256)
            out_ref[pl.ds(at, 256), :] = block[a * 512 : a * 512 + 256, :]
            out_ref[pl.ds(2048 + at, 256), :] = block[a * 512 + 256 : a * 512 + 512, :]
        out_ref[4096 + 32 * step : 4096 + 32 * (step + 1), :] = block[1024:, :]


def small_call(kernel, rows, cols, operands, after=(), info=None, outs=1):
    lead = [] if info is None else [info]
    return pl.pallas_call(
        kernel,
        out_shape=[jax.ShapeDtypeStruct((rows, cols), jnp.bfloat16)] * outs,
        in_specs=[SMEM] * len(lead) + [VMEM] * len(operands) + [pl.BlockSpec(memory_space=pl.ANY)] * len(after),
        out_specs=[VMEM] * outs,
        compiler_params=pltpu.CompilerParams(vmem_limit_bytes=32 << 20),
    )(*lead, *operands, *after)


def attend_kernel(head, info, *refs):
    q_refs, (near, far), refs = refs[:4], refs[4:6], refs[6:]
    before, refs = (refs[:4], refs[4:]) if head == 1 else ((), refs[-12:])
    o_refs, (queries, keys, vals, scores, tops, sums, flat, outs) = refs[:4], refs[4:]
    base = 0
    for old, o_ref in zip(before, o_refs):
        base = old.shape[0]
        o_ref[:base, :] = old[...]
    zl, y, x, c = [info[n] for n in range(4)]
    lane = lax.broadcasted_iota(jnp.int32, (SEG, HEAD_DIM), 1)
    row = lax.broadcasted_iota(jnp.int32, (SEG, HEAD_DIM), 0)

    def bounds(lines):
        found = sum(line.astype(jnp.float32) for line in lines)
        return [
            jnp.sum(jnp.where(lane[:16] == n, found, 0.0), keepdims=True)[0, 0].astype(jnp.int32)
            for n in range(2)
        ]

    n1, n2 = bounds([ref[KEYS + 16 * n : KEYS + 16 * (n + 1), :] for ref in (near, far) for n in range(8)])
    m1, m2 = bounds([ref[512:, :HEAD_DIM] for ref in q_refs])

    def clip_of(index, first, second):
        return (index >= first).astype(jnp.int32) + (index >= second).astype(jnp.int32)

    for n in range(KEYS // SEG):
        own = clip_of(row + n * SEG, n1, n2) == lane
        keys[n * SEG : (n + 1) * SEG, HEAD_DIM:] = own.astype(jnp.float32).astype(jnp.bfloat16)
    for n in range(2048 // SEG):
        differs = (clip_of(row + n * SEG, m1, m2) != lane) & (lane < 3)
        queries[n * SEG : (n + 1) * SEG, HEAD_DIM:] = jnp.where(differs, NEG, 0.0).astype(jnp.bfloat16)
    vals[:, HEAD_DIM:] = jnp.ones((KEYS, HEAD_DIM), jnp.bfloat16)
    cols = slice(head * HEAD_DIM, (head + 1) * HEAD_DIM)
    for step in range(4):
        xx = (x - step) & 3
        for a in range(2):
            zz = 2 * (c ^ (xx & 1)) + (zl ^ a)
            at = pl.multiple_of(zz * TILE + (xx >> 1) * 256, 256)
            queries[pl.ds(at, 256), :HEAD_DIM] = q_refs[step][a * 256 : (a + 1) * 256, cols]
    zh = c ^ (x & 1)
    for part, ref in ((zh, near), (1 - zh, far)):
        at = pl.ds(pl.multiple_of(part * 2048, 2048), 2048)
        keys[at, :HEAD_DIM] = ref[:2048, :]
        vals[at, :HEAD_DIM] = ref[2048:4096, :]

    eye = (lane == row).astype(jnp.float32)
    sub = lax.broadcasted_iota(jnp.int32, (16, HEAD_DIM), 0)

    def tile(zz, carry):
        first, last = zz * TILE, zz * TILE + TILE - 1
        low = jnp.where(first >= m2, n2, jnp.where(first >= m1, n1, 0))
        high = jnp.where(last >= m2, KEYS, jnp.where(last >= m1, n2, n1))
        low = (low // SEG) * SEG
        need = high - low
        rows = pl.ds(pl.multiple_of(first, TILE), TILE)
        tops[...] = jnp.full((TILE, HEAD_DIM), NEG, jnp.float32)
        sums[...] = jnp.zeros((TILE, 2 * HEAD_DIM), jnp.float32)

        def runs(k):
            under = WIDTHS[k - 1] if k else 0
            return ((need > under) & (need <= WIDTHS[k])).astype(jnp.int32)

        for k, width in enumerate(WIDTHS):
            at = pl.multiple_of(jnp.minimum(low, KEYS - width), SEG)

            def first_pass(i, carry, width=width, at=at):
                s = lax.dot_general(
                    queries[rows, :],
                    keys[pl.ds(at, width), :],
                    (((1,), (1,)), ((), ())),
                    preferred_element_type=jnp.float32,
                )
                scores[:, :width] = s
                top = s[:, :128]
                for n in range(1, width // 128):
                    top = jnp.maximum(top, s[:, n * 128 : (n + 1) * 128])
                tops[...] = top
                return carry

            lax.fori_loop(0, runs(k), first_pass, 0)

        top = jnp.maximum(jnp.max(tops[...], axis=1, keepdims=True), FLOOR)

        for k, width in enumerate(WIDTHS):
            at = pl.multiple_of(jnp.minimum(low, KEYS - width), SEG)

            def second_pass(i, carry, width=width, at=at):
                weights = jnp.exp(scores[:, :width] - top).astype(jnp.bfloat16)
                sums[...] = jnp.dot(weights, vals[pl.ds(at, width), :], preferred_element_type=jnp.float32)
                return carry

            lax.fori_loop(0, runs(k), second_pass, 0)

        total = jnp.maximum(sums[:, HEAD_DIM:], 1e-30)
        flat[...] = (sums[:, :HEAD_DIM] / total).astype(jnp.bfloat16)
        tops[...] = top + jnp.log(total)
        a = (zz & 1) ^ zl
        for pair in range(2):
            xx = ((zz >> 1) ^ c) + 2 * pair
            step = (xx - x) & 3
            for half in range(2):
                at = slice(pair * 256 + half * SEG, pair * 256 + (half + 1) * SEG)
                to = pl.multiple_of(a * 256 + half * SEG, SEG)
                outs[step, pl.ds(to, SEG), :] = flat[at, :]
                line = jnp.sum(tops[at, :] * eye, axis=0, keepdims=True)
                big = line.astype(jnp.bfloat16).astype(jnp.float32)
                middle = (line - big).astype(jnp.bfloat16).astype(jnp.float32)
                rest = line - big - middle
                parts = jnp.where(sub == 0, big, jnp.where(sub == 1, middle, jnp.where(sub == 2, rest, 0.0)))
                to = pl.multiple_of(512 + (2 * a + half) * 16, 16)
                outs[step, pl.ds(to, 16), :] = parts.astype(jnp.bfloat16)
        return carry

    lax.fori_loop(0, 4, tile, 0)
    for step in range(4):
        o_refs[step][base:, :] = outs[step]


def attend(head, info, queries, near, far, before=(), after=()):
    return pl.pallas_call(
        functools.partial(attend_kernel, head),
        out_shape=[jax.ShapeDtypeStruct(((2 if before else 1) * (4 * SEG + 64), HEAD_DIM), jnp.bfloat16)] * 4,
        in_specs=[SMEM] + [VMEM] * (6 + len(before)) + [pl.BlockSpec(memory_space=pl.ANY)] * len(after),
        out_specs=[VMEM] * 4,
        scratch_shapes=[
            pltpu.VMEM((2048, 2 * HEAD_DIM), jnp.bfloat16),
            pltpu.VMEM((KEYS, 2 * HEAD_DIM), jnp.bfloat16),
            pltpu.VMEM((KEYS, 2 * HEAD_DIM), jnp.bfloat16),
            pltpu.VMEM((TILE, KEYS), jnp.float32),
            pltpu.VMEM((TILE, HEAD_DIM), jnp.float32),
            pltpu.VMEM((TILE, 2 * HEAD_DIM), jnp.float32),
            pltpu.VMEM((TILE, HEAD_DIM), jnp.bfloat16),
            pltpu.VMEM((4, 4 * SEG + 64, HEAD_DIM), jnp.bfloat16),
        ],
        compiler_params=pltpu.CompilerParams(vmem_limit_bytes=48 << 20),
        cost_estimate=pl.CostEstimate(
            flops=2 * 2 * 2048 * 4096 * 128, bytes_accessed=4 << 20, transcendentals=2048 * 4096
        ),
    )(info, *queries, near, far, *before, *after)


def combine_kernel(heads, *refs):
    parts, out_ref = refs[:4], refs[-1]
    eye = (
        lax.broadcasted_iota(jnp.int32, (SEG, SEG), 0)
        == lax.broadcasted_iota(jnp.int32, (SEG, SEG), 1)
    ).astype(jnp.float32)
    for head in range(heads):
        base = head * (4 * SEG + 64)
        for slot in range(4):
            levels = []
            for part in parts:
                at = base + 4 * SEG + slot * 16
                lines = part[at : at + 16, :].astype(jnp.float32)
                levels.append(jnp.sum(lines, axis=0, keepdims=True))
            top = functools.reduce(jnp.maximum, levels)
            shares = [jnp.exp(level - top) for level in levels]
            total = functools.reduce(jnp.add, shares)
            spread = jnp.concatenate([eye * (share / total) for share in shares], axis=1)
            at = base + slot * SEG
            stacked = jnp.concatenate([part[at : at + SEG, :] for part in parts], axis=0)
            mixed = jnp.dot(spread.astype(jnp.bfloat16), stacked, preferred_element_type=jnp.float32)
            rows = slice(slot * SEG, (slot + 1) * SEG)
            out_ref[rows, head * HEAD_DIM : (head + 1) * HEAD_DIM] = mixed.astype(jnp.bfloat16)


def outward_kernel(first_row, begun, info, first_ref, second_ref, w_ref, *refs):
    out_ref, zl = refs[-1], info[0]
    total = refs[0][...] if begun else 0.0
    for a, block in enumerate((first_ref, second_ref)):
        rows = pl.ds(pl.multiple_of((zl ^ a) * 384 + first_row, HEAD_DIM), block.shape[1])
        total += jnp.dot(block[...], w_ref[rows, :], preferred_element_type=jnp.float32)
    out_ref[...] = total.astype(out_ref.dtype)


def outward(other_half, first_row, dtype, info, blocks, w_out, begun=(), after=()):
    depth, width = w_out.shape[0], w_out.shape[1] // 2
    whole = lambda n, info_ref: (0, 0)
    grid_spec = pltpu.PrefetchScalarGridSpec(
        num_scalar_prefetch=1,
        grid=(1,),
        in_specs=[pl.BlockSpec(block.shape, whole) for block in blocks]
        + [pl.BlockSpec((depth, width), lambda n, info_ref: (0, info_ref[3] ^ other_half))]
        + [pl.BlockSpec((256, width), whole)] * len(begun)
        + [pl.BlockSpec(memory_space=pl.ANY)] * len(after),
        out_specs=pl.BlockSpec((256, width), whole),
    )
    return pl.pallas_call(
        functools.partial(outward_kernel, first_row, len(begun)),
        grid_spec=grid_spec,
        out_shape=jax.ShapeDtypeStruct((256, width), dtype),
        compiler_params=pltpu.CompilerParams(vmem_limit_bytes=40 << 20),
        cost_estimate=pl.CostEstimate(
            flops=4 * 256 * blocks[0].shape[1] * width, bytes_accessed=2 * depth * width, transcendentals=0
        ),
    )(info, *blocks, w_out, *begun, *after)


def spread_pairs(a):
    pairs = []
    for z in range(4):
        for x in range(4):
            for c in range(2):
                target = 2 * c + ((z % 2) ^ a)
                pairs.append(((z * 4 + x) * 2 + c, (target * 4 + x) * 2 + ((z // 2) ^ (x % 2))))
    return pairs


def turn(step):
    return [(n, (n + step) % 4) for n in range(4)]


def body(tokens, clip_id, w_qkv, w_out):
    z, y, x, c = [lax.axis_index(name) for name in ("z", "y", "x", "core")]
    zl, zh = z % 2, z // 2
    swap = [(0, 1), (1, 0)]
    info = jnp.stack([zl, y, x, c, zh]).astype(jnp.int32)

    halves = clip_id.reshape(2, SEG)
    counts = jnp.stack([jnp.sum(halves < 1, axis=1), jnp.sum(halves < 2, axis=1)], axis=1)
    header = jnp.pad(counts.astype(jnp.bfloat16), ((0, 14), (0, HEAD_DIM - 2)))

    other = lax.ppermute(tokens, "core", swap)
    both = jnp.where(c == 0, jnp.concatenate([tokens, other], 1), jnp.concatenate([other, tokens], 1))
    own_kv = jnp.einsum("td,sdc->stc", both, w_qkv[1:], preferred_element_type=jnp.float32)
    own_q = jnp.einsum("td,sdc->stc", both, w_qkv[:1], preferred_element_type=jnp.float32)
    own_q = own_q * (1.0 / math.sqrt(HEAD_DIM))

    def to_group(parts, own, after):
        kernel = functools.partial(send_kernel, parts)
        blocks = small_call(kernel, parts * 256 + (16 if parts == 1 else 32), 384, [own.astype(jnp.bfloat16), header], after, info, 2)
        moved = [lax.ppermute(block, ("z", "x", "core"), spread_pairs(a)) for a, block in enumerate(blocks)]
        return blocks, moved

    leaving, q_in = to_group(1, own_q, ())
    leaving, kv_in = to_group(2, own_kv, leaving[:1])
    [mine] = small_call(queries_kernel, 528, 384, q_in, leaving[:1])
    queries = [mine] + [lax.ppermute(mine, "x", turn(step)) for step in (1, 2, 3)]
    def key_blocks(head, after=()):
        [own] = small_call(functools.partial(pairs_kernel, head), 1056, HEAD_DIM, kv_in, after)
        return [own] + [lax.ppermute(own, "y", turn(step)) for step in (1, 2, 3)]

    def merged(blocks, after=()):
        [near] = small_call(merge_kernel, KEYS + 128, HEAD_DIM, blocks, after, info)
        return near, lax.ppermute(near, "core", swap)

    kv = key_blocks(0, queries[:1])
    kv_next = key_blocks(1, queries[1:])
    part = attend(0, info, queries, *merged(kv, (*queries[1:], kv_next[0])))
    kv_last = key_blocks(2, (*kv_next[1:], part[0]))
    part = attend(1, info, queries, *merged(kv_next, part[:1]), part)
    last = attend(2, info, queries, *merged(kv_last, part[:1]))

    def gather_results(blocks):
        return [blocks[0]] + [lax.ppermute(blocks[step], "x", turn(step)) for step in (1, 2, 3)]

    def go_back(heads, blocks, after=()):
        kernel = functools.partial(combine_kernel, heads)
        [mixed] = small_call(kernel, 512, heads * HEAD_DIM, gather_results(blocks), after)
        back = []
        for a in range(2):
            returns = [(target, source) for source, target in spread_pairs(a)]
            back.append(lax.ppermute(mixed[256 * a : 256 * (a + 1)], ("z", "x", "core"), returns))
        return mixed, back

    mixed, early = go_back(2, part, last[:1])
    _, late = go_back(1, last, (mixed,))
    there = outward(1, 0, jnp.float32, info, early, w_out)
    here = outward(0, 0, jnp.float32, info, early, w_out)
    there = outward(1, 256, jnp.bfloat16, info, late, w_out, (there,), (here,))
    received = lax.ppermute(there, "core", swap)
    here = outward(0, 256, jnp.float32, info, late, w_out, (here,), (there,))
    return (here + received.astype(jnp.float32)).astype(jnp.bfloat16)


def solution(mesh):
    fine = Mesh(mesh.devices.reshape(4, 4, 4, 2), ("z", "y", "x", "core"))
    seq = ("z", "y", "x")
    in_specs = (P(seq, "core"), P(seq), P(None, None, "core"), P("core", None))
    return jax.shard_map(body, mesh=fine, in_specs=in_specs, out_specs=P(seq, "core"), check_vma=False)
```

```python
import functools
import math

import jax
import jax.numpy as jnp
from jax import lax
from jax.experimental import pallas as pl
from jax.experimental.pallas import tpu as pltpu
from jax.sharding import Mesh
from jax.sharding import PartitionSpec as P

HEAD_DIM = 128
SEG = 128
TILE = 512
KEYS = 4096
NEG = -1e30
FLOOR = -1e29
WIDTHS = (1536, 2688, 4096)
VMEM = pl.BlockSpec(memory_space=pltpu.VMEM)
SMEM = pl.BlockSpec(memory_space=pltpu.SMEM)


def send_kernel(parts, info, own_ref, header, *refs):
    out_refs, zl = refs[-2:], info[0]
    for a, out_ref in enumerate(out_refs):
        for group in range(2):

            @pl.when((zl ^ a) == group)
            def _():
                for n in range(parts):
                    out_ref[n * 256 : (n + 1) * 256, :] = own_ref[n, :, group * 384 : (group + 1) * 384]

        for n in range(3):
            out_ref[parts * 256 : parts * 256 + 16, n * HEAD_DIM : (n + 1) * HEAD_DIM] = header[...]


def queries_kernel(*refs):
    blocks, q_ref = refs[:2], refs[-1]
    counts = blocks[0][256:, :].astype(jnp.float32) + blocks[1][256:, :].astype(jnp.float32)
    q_ref[512:, :] = counts.astype(jnp.bfloat16)
    for a, block in enumerate(blocks):
        q_ref[a * 256 : (a + 1) * 256, :] = block[:256, :]


def pairs_kernel(place, *refs):
    blocks, kv_ref = refs[:2], refs[-1]
    cols = slice(place * HEAD_DIM, (place + 1) * HEAD_DIM)
    for a, block in enumerate(blocks):
        kv_ref[a * 512 : (a + 1) * 512, :] = block[:512, cols]
        kv_ref[1024 + 16 * a : 1024 + 16 * (a + 1), :] = block[512:528, cols]


def merge_kernel(info, *refs):
    blocks, out_ref = refs[:4], refs[-1]
    zl, y = info[0], info[1]
    for step, block in enumerate(blocks):
        for a in range(2):
            at = pl.multiple_of(((zl ^ a) * 4 + ((y - step) & 3)) * 256, 256)
            out_ref[pl.ds(at, 256), :] = block[a * 512 : a * 512 + 256, :]
            out_ref[pl.ds(2048 + at, 256), :] = block[a * 512 + 256 : a * 512 + 512, :]
        out_ref[4096 + 32 * step : 4096 + 32 * (step + 1), :] = block[1024:, :]


def small_call(kernel, rows, cols, operands, after=(), info=None, outs=1):
    lead = [] if info is None else [info]
    return pl.pallas_call(
        kernel,
        out_shape=[jax.ShapeDtypeStruct((rows, cols), jnp.bfloat16)] * outs,
        in_specs=[SMEM] * len(lead) + [VMEM] * len(operands) + [pl.BlockSpec(memory_space=pl.ANY)] * len(after),
        out_specs=[VMEM] * outs,
        compiler_params=pltpu.CompilerParams(vmem_limit_bytes=32 << 20),
    )(*lead, *operands, *after)


def attend_kernel(head, info, *refs):
    q_refs, (near, far), refs = refs[:4], refs[4:6], refs[6:]
    before, refs = (refs[:4], refs[4:]) if head == 1 else ((), refs[-12:])
    o_refs, (queries, keys, vals, scores, tops, sums, flat, outs) = refs[:4], refs[4:]
    base = 0
    for old, o_ref in zip(before, o_refs):
        base = old.shape[0]
        o_ref[:base, :] = old[...]
    zl, y, x, c = [info[n] for n in range(4)]
    lane = lax.broadcasted_iota(jnp.int32, (SEG, HEAD_DIM), 1)
    row = lax.broadcasted_iota(jnp.int32, (SEG, HEAD_DIM), 0)

    def bounds(lines):
        found = sum(line.astype(jnp.float32) for line in lines)
        return [
            jnp.sum(jnp.where(lane[:16] == n, found, 0.0), keepdims=True)[0, 0].astype(jnp.int32)
            for n in range(2)
        ]

    n1, n2 = bounds([ref[KEYS + 16 * n : KEYS + 16 * (n + 1), :] for ref in (near, far) for n in range(8)])
    m1, m2 = bounds([ref[512:, :HEAD_DIM] for ref in q_refs])

    def clip_of(index, first, second):
        return (index >= first).astype(jnp.int32) + (index >= second).astype(jnp.int32)

    for n in range(KEYS // SEG):
        own = clip_of(row + n * SEG, n1, n2) == lane
        keys[n * SEG : (n + 1) * SEG, HEAD_DIM:] = own.astype(jnp.float32).astype(jnp.bfloat16)
    for n in range(2048 // SEG):
        differs = (clip_of(row + n * SEG, m1, m2) != lane) & (lane < 3)
        queries[n * SEG : (n + 1) * SEG, HEAD_DIM:] = jnp.where(differs, NEG, 0.0).astype(jnp.bfloat16)
    vals[:, HEAD_DIM:] = jnp.ones((KEYS, HEAD_DIM), jnp.bfloat16)
    cols = slice(head * HEAD_DIM, (head + 1) * HEAD_DIM)
    for step in range(4):
        xx = (x - step) & 3
        for a in range(2):
            zz = 2 * (c ^ (xx & 1)) + (zl ^ a)
            at = pl.multiple_of(zz * TILE + (xx >> 1) * 256, 256)
            queries[pl.ds(at, 256), :HEAD_DIM] = q_refs[step][a * 256 : (a + 1) * 256, cols]
    zh = c ^ (x & 1)
    for part, ref in ((zh, near), (1 - zh, far)):
        at = pl.ds(pl.multiple_of(part * 2048, 2048), 2048)
        keys[at, :HEAD_DIM] = ref[:2048, :]
        vals[at, :HEAD_DIM] = ref[2048:4096, :]

    eye = (lane == row).astype(jnp.float32)
    sub = lax.broadcasted_iota(jnp.int32, (16, HEAD_DIM), 0)

    def tile(zz, carry):
        first, last = zz * TILE, zz * TILE + TILE - 1
        low = jnp.where(first >= m2, n2, jnp.where(first >= m1, n1, 0))
        high = jnp.where(last >= m2, KEYS, jnp.where(last >= m1, n2, n1))
        low = (low // SEG) * SEG
        need = high - low
        rows = pl.ds(pl.multiple_of(first, TILE), TILE)
        tops[...] = jnp.full((TILE, HEAD_DIM), NEG, jnp.float32)
        sums[...] = jnp.zeros((TILE, 2 * HEAD_DIM), jnp.float32)

        def runs(k):
            under = WIDTHS[k - 1] if k else 0
            return ((need > under) & (need <= WIDTHS[k])).astype(jnp.int32)

        for k, width in enumerate(WIDTHS):
            at = pl.multiple_of(jnp.minimum(low, KEYS - width), SEG)

            def first_pass(i, carry, width=width, at=at):
                s = lax.dot_general(
                    queries[rows, :],
                    keys[pl.ds(at, width), :],
                    (((1,), (1,)), ((), ())),
                    preferred_element_type=jnp.float32,
                )
                scores[:, :width] = s
                top = s[:, :128]
                for n in range(1, width // 128):
                    top = jnp.maximum(top, s[:, n * 128 : (n + 1) * 128])
                tops[...] = top
                return carry

            lax.fori_loop(0, runs(k), first_pass, 0)

        top = jnp.maximum(jnp.max(tops[...], axis=1, keepdims=True), FLOOR)

        for k, width in enumerate(WIDTHS):
            at = pl.multiple_of(jnp.minimum(low, KEYS - width), SEG)

            def second_pass(i, carry, width=width, at=at):
                weights = jnp.exp(scores[:, :width] - top).astype(jnp.bfloat16)
                sums[...] = jnp.dot(weights, vals[pl.ds(at, width), :], preferred_element_type=jnp.float32)
                return carry

            lax.fori_loop(0, runs(k), second_pass, 0)

        total = jnp.maximum(sums[:, HEAD_DIM:], 1e-30)
        flat[...] = (sums[:, :HEAD_DIM] / total).astype(jnp.bfloat16)
        tops[...] = top + jnp.log(total)
        a = (zz & 1) ^ zl
        for pair in range(2):
            xx = ((zz >> 1) ^ c) + 2 * pair
            step = (xx - x) & 3
            for half in range(2):
                at = slice(pair * 256 + half * SEG, pair * 256 + (half + 1) * SEG)
                to = pl.multiple_of(a * 256 + half * SEG, SEG)
                outs[step, pl.ds(to, SEG), :] = flat[at, :]
                line = jnp.sum(tops[at, :] * eye, axis=0, keepdims=True)
                big = line.astype(jnp.bfloat16).astype(jnp.float32)
                middle = (line - big).astype(jnp.bfloat16).astype(jnp.float32)
                rest = line - big - middle
                parts = jnp.where(sub == 0, big, jnp.where(sub == 1, middle, jnp.where(sub == 2, rest, 0.0)))
                to = pl.multiple_of(512 + (2 * a + half) * 16, 16)
                outs[step, pl.ds(to, 16), :] = parts.astype(jnp.bfloat16)
        return carry

    lax.fori_loop(0, 4, tile, 0)
    for step in range(4):
        o_refs[step][base:, :] = outs[step]


def attend(head, info, queries, near, far, before=(), after=()):
    return pl.pallas_call(
        functools.partial(attend_kernel, head),
        out_shape=[jax.ShapeDtypeStruct(((2 if before else 1) * (4 * SEG + 64), HEAD_DIM), jnp.bfloat16)] * 4,
        in_specs=[SMEM] + [VMEM] * (6 + len(before)) + [pl.BlockSpec(memory_space=pl.ANY)] * len(after),
        out_specs=[VMEM] * 4,
        scratch_shapes=[
            pltpu.VMEM((2048, 2 * HEAD_DIM), jnp.bfloat16),
            pltpu.VMEM((KEYS, 2 * HEAD_DIM), jnp.bfloat16),
            pltpu.VMEM((KEYS, 2 * HEAD_DIM), jnp.bfloat16),
            pltpu.VMEM((TILE, KEYS), jnp.float32),
            pltpu.VMEM((TILE, HEAD_DIM), jnp.float32),
            pltpu.VMEM((TILE, 2 * HEAD_DIM), jnp.float32),
            pltpu.VMEM((TILE, HEAD_DIM), jnp.bfloat16),
            pltpu.VMEM((4, 4 * SEG + 64, HEAD_DIM), jnp.bfloat16),
        ],
        compiler_params=pltpu.CompilerParams(vmem_limit_bytes=48 << 20),
        cost_estimate=pl.CostEstimate(
            flops=2 * 2 * 2048 * 4096 * 128, bytes_accessed=4 << 20, transcendentals=2048 * 4096
        ),
    )(info, *queries, near, far, *before, *after)


def combine_kernel(heads, *refs):
    parts, out_ref = refs[:4], refs[-1]
    eye = (
        lax.broadcasted_iota(jnp.int32, (SEG, SEG), 0)
        == lax.broadcasted_iota(jnp.int32, (SEG, SEG), 1)
    ).astype(jnp.float32)
    for head in range(heads):
        base = head * (4 * SEG + 64)
        for slot in range(4):
            levels = []
            for part in parts:
                at = base + 4 * SEG + slot * 16
                lines = part[at : at + 16, :].astype(jnp.float32)
                levels.append(jnp.sum(lines, axis=0, keepdims=True))
            top = functools.reduce(jnp.maximum, levels)
            shares = [jnp.exp(level - top) for level in levels]
            total = functools.reduce(jnp.add, shares)
            spread = jnp.concatenate([eye * (share / total) for share in shares], axis=1)
            at = base + slot * SEG
            stacked = jnp.concatenate([part[at : at + SEG, :] for part in parts], axis=0)
            mixed = jnp.dot(spread.astype(jnp.bfloat16), stacked, preferred_element_type=jnp.float32)
            rows = slice(slot * SEG, (slot + 1) * SEG)
            out_ref[rows, head * HEAD_DIM : (head + 1) * HEAD_DIM] = mixed.astype(jnp.bfloat16)


def outward_kernel(first_row, begun, info, first_ref, second_ref, w_ref, *refs):
    out_ref, zl = refs[-1], info[0]
    total = refs[0][...] if begun else 0.0
    for a, block in enumerate((first_ref, second_ref)):
        rows = pl.ds(pl.multiple_of((zl ^ a) * 384 + first_row, HEAD_DIM), block.shape[1])
        total += jnp.dot(block[...], w_ref[rows, :], preferred_element_type=jnp.float32)
    out_ref[...] = total.astype(out_ref.dtype)


def outward(other_half, first_row, dtype, info, blocks, w_out, begun=(), after=()):
    depth, width = w_out.shape[0], w_out.shape[1] // 2
    whole = lambda n, info_ref: (0, 0)
    grid_spec = pltpu.PrefetchScalarGridSpec(
        num_scalar_prefetch=1,
        grid=(1,),
        in_specs=[pl.BlockSpec(block.shape, whole) for block in blocks]
        + [pl.BlockSpec((depth, width), lambda n, info_ref: (0, info_ref[3] ^ other_half))]
        + [pl.BlockSpec((256, width), whole)] * len(begun)
        + [pl.BlockSpec(memory_space=pl.ANY)] * len(after),
        out_specs=pl.BlockSpec((256, width), whole),
    )
    return pl.pallas_call(
        functools.partial(outward_kernel, first_row, len(begun)),
        grid_spec=grid_spec,
        out_shape=jax.ShapeDtypeStruct((256, width), dtype),
        compiler_params=pltpu.CompilerParams(vmem_limit_bytes=40 << 20),
        cost_estimate=pl.CostEstimate(
            flops=4 * 256 * blocks[0].shape[1] * width, bytes_accessed=2 * depth * width, transcendentals=0
        ),
    )(info, *blocks, w_out, *begun, *after)


def spread_pairs(a):
    pairs = []
    for z in range(4):
        for x in range(4):
            for c in range(2):
                target = 2 * c + ((z % 2) ^ a)
                pairs.append(((z * 4 + x) * 2 + c, (target * 4 + x) * 2 + ((z // 2) ^ (x % 2))))
    return pairs


def turn(step):
    return [(n, (n + step) % 4) for n in range(4)]


def body(tokens, clip_id, w_qkv, w_out):
    z, y, x, c = [lax.axis_index(name) for name in ("z", "y", "x", "core")]
    zl, zh = z % 2, z // 2
    swap = [(0, 1), (1, 0)]
    info = jnp.stack([zl, y, x, c, zh]).astype(jnp.int32)

    halves = clip_id.reshape(2, SEG)
    counts = jnp.stack([jnp.sum(halves < 1, axis=1), jnp.sum(halves < 2, axis=1)], axis=1)
    header = jnp.pad(counts.astype(jnp.bfloat16), ((0, 14), (0, HEAD_DIM - 2)))

    other = lax.ppermute(tokens, "core", swap)
    both = jnp.where(c == 0, jnp.concatenate([tokens, other], 1), jnp.concatenate([other, tokens], 1))
    own_kv = jnp.einsum("td,sdc->stc", both, w_qkv[1:], preferred_element_type=jnp.float32)
    own_q = jnp.einsum("td,sdc->stc", both, w_qkv[:1], preferred_element_type=jnp.float32)
    own_q = own_q * (1.0 / math.sqrt(HEAD_DIM))

    def to_group(parts, own, after):
        kernel = functools.partial(send_kernel, parts)
        blocks = small_call(kernel, parts * 256 + (16 if parts == 1 else 32), 384, [own.astype(jnp.bfloat16), header], after, info, 2)
        moved = [lax.ppermute(block, ("z", "x", "core"), spread_pairs(a)) for a, block in enumerate(blocks)]
        return blocks, moved

    leaving, q_in = to_group(1, own_q, ())
    leaving, kv_in = to_group(2, own_kv, leaving[:1])
    [mine] = small_call(queries_kernel, 528, 384, q_in, leaving[:1])
    queries = [mine] + [lax.ppermute(mine, "x", turn(step)) for step in (1, 2, 3)]
    def key_blocks(head, after=()):
        [own] = small_call(functools.partial(pairs_kernel, head), 1056, HEAD_DIM, kv_in, after)
        return [own] + [lax.ppermute(own, "y", turn(step)) for step in (1, 2, 3)]

    def merged(blocks, after=()):
        [near] = small_call(merge_kernel, KEYS + 128, HEAD_DIM, blocks, after, info)
        return near, lax.ppermute(near, "core", swap)

    kv = key_blocks(0, queries[:1])
    kv_next = key_blocks(1, queries[1:])
    part = attend(0, info, queries, *merged(kv, (*queries[1:], kv_next[0])))
    kv_last = key_blocks(2, (*kv_next[1:], part[0]))
    part = attend(1, info, queries, *merged(kv_next, part[:1]), part)
    last = attend(2, info, queries, *merged(kv_last, part[:1]))

    def gather_results(blocks):
        return [blocks[0]] + [lax.ppermute(blocks[step], "x", turn(step)) for step in (1, 2, 3)]

    def go_back(heads, blocks, after=()):
        kernel = functools.partial(combine_kernel, heads)
        [mixed] = small_call(kernel, 512, heads * HEAD_DIM, gather_results(blocks), after)
        back = []
        for a in range(2):
            returns = [(target, source) for source, target in spread_pairs(a)]
            back.append(lax.ppermute(mixed[256 * a : 256 * (a + 1)], ("z", "x", "core"), returns))
        return mixed, back

    mixed, early = go_back(2, part, last[:1])
    _, late = go_back(1, last, (mixed,))
    there = outward(1, 0, jnp.float32, info, early, w_out)
    here = outward(0, 0, jnp.float32, info, early, w_out)
    there = outward(1, 256, jnp.bfloat16, info, late, w_out, (there,), (here,))
    received = lax.ppermute(there, "core", swap)
    here = outward(0, 256, jnp.float32, info, late, w_out, (here,), (there,))
    return (here + received.astype(jnp.float32)).astype(jnp.bfloat16)


def solution(mesh):
    fine = Mesh(mesh.devices.reshape(4, 4, 4, 2), ("z", "y", "x", "core"))
    seq = ("z", "y", "x")
    in_specs = (P(seq, "core"), P(seq), P(None, None, "core"), P("core", None))
    return jax.shard_map(body, mesh=fine, in_specs=in_specs, out_specs=P(seq, "core"), check_vma=False)
```

```python
import functools
import math

import jax
import jax.numpy as jnp
from jax import lax
from jax.experimental import pallas as pl
from jax.experimental.pallas import tpu as pltpu
from jax.sharding import Mesh
from jax.sharding import PartitionSpec as P

HEAD_DIM = 128
SEG = 128
TILE = 512
KEYS = 4096
NEG = -1e30
FLOOR = -1e29
WIDTHS = (768, 1536, 2048, 2688, 3328, 4096)
VMEM = pl.BlockSpec(memory_space=pltpu.VMEM)
SMEM = pl.BlockSpec(memory_space=pltpu.SMEM)


def send_kernel(parts, info, own_ref, header, *refs):
    out_refs, zl = refs[-2:], info[0]
    for a, out_ref in enumerate(out_refs):
        for group in range(2):

            @pl.when((zl ^ a) == group)
            def _():
                for n in range(parts):
                    out_ref[n * 256 : (n + 1) * 256, :] = own_ref[n, :, group * 384 : (group + 1) * 384]

        for n in range(3):
            out_ref[parts * 256 : parts * 256 + 16, n * HEAD_DIM : (n + 1) * HEAD_DIM] = header[...]


def pass_kernel(*refs):
    for block, out_ref in zip(refs[:2], refs[-2:]):
        out_ref[...] = block[...]


def queries_kernel(*refs):
    blocks, q_ref = refs[:2], refs[-1]
    counts = blocks[0][256:, :].astype(jnp.float32) + blocks[1][256:, :].astype(jnp.float32)
    q_ref[512:, :] = counts.astype(jnp.bfloat16)
    for a, block in enumerate(blocks):
        q_ref[a * 256 : (a + 1) * 256, :] = block[:256, :]


def pairs_kernel(place, *refs):
    blocks, kv_ref = refs[:2], refs[-1]
    cols = slice(place * HEAD_DIM, (place + 1) * HEAD_DIM)
    for a, block in enumerate(blocks):
        kv_ref[a * 512 : (a + 1) * 512, :] = block[:512, cols]
        kv_ref[1024 + 16 * a : 1024 + 16 * (a + 1), :] = block[512:528, cols]


def merge_kernel(info, *refs):
    blocks, out_ref = refs[:4], refs[-1]
    zl, y = info[0], info[1]
    for step, block in enumerate(blocks):
        for a in range(2):
            at = pl.multiple_of(((zl ^ a) * 4 + ((y - step) & 3)) * 256, 256)
            out_ref[pl.ds(at, 256), :] = block[a * 512 : a * 512 + 256, :]
            out_ref[pl.ds(2048 + at, 256), :] = block[a * 512 + 256 : a * 512 + 512, :]
        out_ref[4096 + 32 * step : 4096 + 32 * (step + 1), :] = block[1024:, :]


def small_call(kernel, rows, cols, operands, after=(), info=None, outs=1):
    lead = [] if info is None else [info]
    return pl.pallas_call(
        kernel,
        out_shape=[jax.ShapeDtypeStruct((rows, cols), jnp.bfloat16)] * outs,
        in_specs=[SMEM] * len(lead) + [VMEM] * len(operands) + [pl.BlockSpec(memory_space=pl.ANY)] * len(after),
        out_specs=[VMEM] * outs,
        compiler_params=pltpu.CompilerParams(vmem_limit_bytes=32 << 20),
    )(*lead, *operands, *after)


def attend_kernel(head, info, *refs):
    q_refs, across, (near, far), refs = refs[:3], refs[3:5], refs[5:7], refs[7:]
    before, refs = (refs[:4], refs[4:]) if head == 1 else ((), refs[-12:])
    o_refs, (queries, keys, vals, scores, tops, sums, flat, outs) = refs[:4], refs[4:]
    base = 0
    for old, o_ref in zip(before, o_refs):
        base = old.shape[0]
        o_ref[:base, :] = old[...]
    zl, y, x, c = [info[n] for n in range(4)]
    lane = lax.broadcasted_iota(jnp.int32, (SEG, HEAD_DIM), 1)
    row = lax.broadcasted_iota(jnp.int32, (SEG, HEAD_DIM), 0)

    def bounds(lines):
        found = sum(line.astype(jnp.float32) for line in lines)
        return [
            jnp.sum(jnp.where(lane[:16] == n, found, 0.0), keepdims=True)[0, 0].astype(jnp.int32)
            for n in range(2)
        ]

    n1, n2 = bounds([ref[KEYS + 16 * n : KEYS + 16 * (n + 1), :] for ref in (near, far) for n in range(8)])
    m1, m2 = bounds([ref[512:, :HEAD_DIM] for ref in q_refs] + [ref[256:, :HEAD_DIM] for ref in across])

    def clip_of(index, first, second):
        return (index >= first).astype(jnp.int32) + (index >= second).astype(jnp.int32)

    for n in range(KEYS // SEG):
        own = clip_of(row + n * SEG, n1, n2) == lane
        keys[n * SEG : (n + 1) * SEG, HEAD_DIM:] = own.astype(jnp.float32).astype(jnp.bfloat16)
    for n in range(2048 // SEG):
        differs = (clip_of(row + n * SEG, m1, m2) != lane) & (lane < 3)
        queries[n * SEG : (n + 1) * SEG, HEAD_DIM:] = jnp.where(differs, NEG, 0.0).astype(jnp.bfloat16)
    vals[:, HEAD_DIM:] = jnp.ones((KEYS, HEAD_DIM), jnp.bfloat16)
    cols = slice(head * HEAD_DIM, (head + 1) * HEAD_DIM)
    for step in range(4):
        xx = (x - step) & 3
        for a in range(2):
            zz = 2 * (c ^ (xx & 1)) + (zl ^ a)
            at = pl.multiple_of(zz * TILE + (xx >> 1) * 256, 256)
            block = across[a][:256, cols] if step == 2 else q_refs[(0, 1, 2, 2)[step]][a * 256 : (a + 1) * 256, cols]
            queries[pl.ds(at, 256), :HEAD_DIM] = block
    zh = c ^ (x & 1)
    for part, ref in ((zh, near), (1 - zh, far)):
        at = pl.ds(pl.multiple_of(part * 2048, 2048), 2048)
        keys[at, :HEAD_DIM] = ref[:2048, :]
        vals[at, :HEAD_DIM] = ref[2048:4096, :]

    eye = (lane == row).astype(jnp.float32)
    sub = lax.broadcasted_iota(jnp.int32, (16, HEAD_DIM), 0)

    def tile(zz, carry):
        first, last = zz * TILE, zz * TILE + TILE - 1
        low = jnp.where(first >= m2, n2, jnp.where(first >= m1, n1, 0))
        high = jnp.where(last >= m2, KEYS, jnp.where(last >= m1, n2, n1))
        low = (low // SEG) * SEG
        need = high - low
        rows = pl.ds(pl.multiple_of(first, TILE), TILE)
        tops[...] = jnp.full((TILE, HEAD_DIM), NEG, jnp.float32)
        sums[...] = jnp.zeros((TILE, 2 * HEAD_DIM), jnp.float32)

        def runs(k):
            under = WIDTHS[k - 1] if k else 0
            return ((need > under) & (need <= WIDTHS[k])).astype(jnp.int32)

        for k, width in enumerate(WIDTHS):
            at = pl.multiple_of(jnp.minimum(low, KEYS - width), SEG)

            def first_pass(i, carry, width=width, at=at):
                s = lax.dot_general(
                    queries[rows, :],
                    keys[pl.ds(at, width), :],
                    (((1,), (1,)), ((), ())),
                    preferred_element_type=jnp.float32,
                )
                scores[:, :width] = s
                top = s[:, :128]
                for n in range(1, width // 128):
                    top = jnp.maximum(top, s[:, n * 128 : (n + 1) * 128])
                tops[...] = top
                return carry

            lax.fori_loop(0, runs(k), first_pass, 0)

        top = jnp.maximum(jnp.max(tops[...], axis=1, keepdims=True), FLOOR)

        for k, width in enumerate(WIDTHS):
            at = pl.multiple_of(jnp.minimum(low, KEYS - width), SEG)

            def second_pass(i, carry, width=width, at=at):
                weights = jnp.exp(scores[:, :width] - top).astype(jnp.bfloat16)
                sums[...] = jnp.dot(weights, vals[pl.ds(at, width), :], preferred_element_type=jnp.float32)
                return carry

            lax.fori_loop(0, runs(k), second_pass, 0)

        total = jnp.maximum(sums[:, HEAD_DIM:], 1e-30)
        flat[...] = (sums[:, :HEAD_DIM] / total).astype(jnp.bfloat16)
        tops[...] = top + jnp.log(total)
        a = (zz & 1) ^ zl
        for pair in range(2):
            xx = ((zz >> 1) ^ c) + 2 * pair
            step = (xx - x) & 3
            for half in range(2):
                at = slice(pair * 256 + half * SEG, pair * 256 + (half + 1) * SEG)
                to = pl.multiple_of(a * 256 + half * SEG, SEG)
                outs[step, pl.ds(to, SEG), :] = flat[at, :]
                line = jnp.sum(tops[at, :] * eye, axis=0, keepdims=True)
                big = line.astype(jnp.bfloat16).astype(jnp.float32)
                middle = (line - big).astype(jnp.bfloat16).astype(jnp.float32)
                rest = line - big - middle
                parts = jnp.where(sub == 0, big, jnp.where(sub == 1, middle, jnp.where(sub == 2, rest, 0.0)))
                to = pl.multiple_of(512 + (2 * a + half) * 16, 16)
                outs[step, pl.ds(to, 16), :] = parts.astype(jnp.bfloat16)
        return carry

    lax.fori_loop(0, 4, tile, 0)
    for step in range(4):
        o_refs[step][base:, :] = outs[step]


def attend(head, info, queries, near, far, before=(), after=()):
    return pl.pallas_call(
        functools.partial(attend_kernel, head),
        out_shape=[jax.ShapeDtypeStruct(((2 if before else 1) * (4 * SEG + 64), HEAD_DIM), jnp.bfloat16)] * 4,
        in_specs=[SMEM] + [VMEM] * (7 + len(before)) + [pl.BlockSpec(memory_space=pl.ANY)] * len(after),
        out_specs=[VMEM] * 4,
        scratch_shapes=[
            pltpu.VMEM((2048, 2 * HEAD_DIM), jnp.bfloat16),
            pltpu.VMEM((KEYS, 2 * HEAD_DIM), jnp.bfloat16),
            pltpu.VMEM((KEYS, 2 * HEAD_DIM), jnp.bfloat16),
            pltpu.VMEM((TILE, KEYS), jnp.float32),
            pltpu.VMEM((TILE, HEAD_DIM), jnp.float32),
            pltpu.VMEM((TILE, 2 * HEAD_DIM), jnp.float32),
            pltpu.VMEM((TILE, HEAD_DIM), jnp.bfloat16),
            pltpu.VMEM((4, 4 * SEG + 64, HEAD_DIM), jnp.bfloat16),
        ],
        compiler_params=pltpu.CompilerParams(vmem_limit_bytes=48 << 20),
        cost_estimate=pl.CostEstimate(
            flops=2 * 2 * 2048 * 4096 * 128, bytes_accessed=4 << 20, transcendentals=2048 * 4096
        ),
    )(info, *queries, near, far, *before, *after)


def combine_kernel(heads, *refs):
    parts, out_ref = refs[:4], refs[-1]
    eye = (
        lax.broadcasted_iota(jnp.int32, (SEG, SEG), 0)
        == lax.broadcasted_iota(jnp.int32, (SEG, SEG), 1)
    ).astype(jnp.float32)
    for head in range(heads):
        base = head * (4 * SEG + 64)
        for slot in range(4):
            levels = []
            for part in parts:
                at = base + 4 * SEG + slot * 16
                lines = part[at : at + 16, :].astype(jnp.float32)
                levels.append(jnp.sum(lines, axis=0, keepdims=True))
            top = functools.reduce(jnp.maximum, levels)
            shares = [jnp.exp(level - top) for level in levels]
            total = functools.reduce(jnp.add, shares)
            spread = jnp.concatenate([eye * (share / total) for share in shares], axis=1)
            at = base + slot * SEG
            stacked = jnp.concatenate([part[at : at + SEG, :] for part in parts], axis=0)
            mixed = jnp.dot(spread.astype(jnp.bfloat16), stacked, preferred_element_type=jnp.float32)
            rows = slice(slot * SEG, (slot + 1) * SEG)
            out_ref[rows, head * HEAD_DIM : (head + 1) * HEAD_DIM] = mixed.astype(jnp.bfloat16)


def outward_kernel(first_row, begun, info, first_ref, second_ref, w_ref, *refs):
    out_ref, zl = refs[-1], info[0]
    total = refs[0][...] if begun else 0.0
    for a, block in enumerate((first_ref, second_ref)):
        rows = pl.ds(pl.multiple_of((zl ^ a) * 384 + first_row, HEAD_DIM), block.shape[1])
        total += jnp.dot(block[...], w_ref[rows, :], preferred_element_type=jnp.float32)
    out_ref[...] = total.astype(out_ref.dtype)


def outward(other_half, first_row, dtype, info, blocks, w_out, begun=(), after=()):
    depth, width = w_out.shape[0], w_out.shape[1] // 2
    whole = lambda n, info_ref: (0, 0)
    grid_spec = pltpu.PrefetchScalarGridSpec(
        num_scalar_prefetch=1,
        grid=(1,),
        in_specs=[pl.BlockSpec(block.shape, whole) for block in blocks]
        + [pl.BlockSpec((depth, width), lambda n, info_ref: (0, info_ref[3] ^ other_half))]
        + [pl.BlockSpec((256, width), whole)] * len(begun)
        + [pl.BlockSpec(memory_space=pl.ANY)] * len(after),
        out_specs=pl.BlockSpec((256, width), whole),
    )
    return pl.pallas_call(
        functools.partial(outward_kernel, first_row, len(begun)),
        grid_spec=grid_spec,
        out_shape=jax.ShapeDtypeStruct((256, width), dtype),
        compiler_params=pltpu.CompilerParams(vmem_limit_bytes=40 << 20),
        cost_estimate=pl.CostEstimate(
            flops=4 * 256 * blocks[0].shape[1] * width, bytes_accessed=2 * depth * width, transcendentals=0
        ),
    )(info, *blocks, w_out, *begun, *after)


def spread_pairs(a):
    pairs = []
    for z in range(4):
        for x in range(4):
            for c in range(2):
                target = 2 * c + ((z % 2) ^ a)
                pairs.append(((z * 4 + x) * 2 + c, (target * 4 + x) * 2 + ((z // 2) ^ (x % 2))))
    return pairs


def turn(step):
    return [(n, (n + step) % 4) for n in range(4)]


def body(tokens, clip_id, w_qkv, w_out):
    z, y, x, c = [lax.axis_index(name) for name in ("z", "y", "x", "core")]
    zl, zh = z % 2, z // 2
    swap = [(0, 1), (1, 0)]
    info = jnp.stack([zl, y, x, c, zh]).astype(jnp.int32)

    halves = clip_id.reshape(2, SEG)
    counts = jnp.stack([jnp.sum(halves < 1, axis=1), jnp.sum(halves < 2, axis=1)], axis=1)
    header = jnp.pad(counts.astype(jnp.bfloat16), ((0, 14), (0, HEAD_DIM - 2)))

    other = lax.ppermute(tokens, "core", swap)
    both = jnp.where(c == 0, jnp.concatenate([tokens, other], 1), jnp.concatenate([other, tokens], 1))
    own_kv = jnp.einsum("td,sdc->stc", both, w_qkv[1:], preferred_element_type=jnp.float32)
    own_q = jnp.einsum("td,sdc->stc", both, w_qkv[:1], preferred_element_type=jnp.float32)
    own_q = own_q * (1.0 / math.sqrt(HEAD_DIM))

    def to_group(parts, own, after):
        kernel = functools.partial(send_kernel, parts)
        blocks = small_call(kernel, parts * 256 + (16 if parts == 1 else 32), 384, [own.astype(jnp.bfloat16), header], after, info, 2)
        moved = [lax.ppermute(block, ("z", "x", "core"), spread_pairs(a)) for a, block in enumerate(blocks)]
        return blocks, moved

    leaving, q_in = to_group(1, own_q, ())
    leaving, kv_in = to_group(2, own_kv, leaving[:1])
    [mine] = small_call(queries_kernel, 528, 384, q_in, leaving[:1])
    queries = [mine] + [lax.ppermute(mine, "x", turn(step)) for step in (1, 3)]
    def key_blocks(head, after=()):
        [own] = small_call(functools.partial(pairs_kernel, head), 1056, HEAD_DIM, kv_in, after)
        return [own] + [lax.ppermute(own, "y", turn(step)) for step in (1, 2, 3)]

    def merged(blocks, after=()):
        [near] = small_call(merge_kernel, KEYS + 128, HEAD_DIM, blocks, after, info)
        return near, lax.ppermute(near, "core", swap)

    kv = key_blocks(0, queries[:1])
    held = small_call(pass_kernel, 272, 384, q_in, (*queries[1:], kv[0]), outs=2)
    queries = queries + [lax.ppermute(block, "x", turn(2)) for block in held]
    kv_next = key_blocks(1, queries[1:])
    part = attend(0, info, queries, *merged(kv, (*queries[1:], kv_next[0])))
    kv_last = key_blocks(2, (*kv_next[1:], part[0]))
    part = attend(1, info, queries, *merged(kv_next, part[:1]), part)
    last = attend(2, info, queries, *merged(kv_last, part[:1]))

    def gather_results(blocks):
        return [blocks[0]] + [lax.ppermute(blocks[step], "x", turn(step)) for step in (1, 2, 3)]

    def go_back(heads, blocks, after=()):
        kernel = functools.partial(combine_kernel, heads)
        [mixed] = small_call(kernel, 512, heads * HEAD_DIM, gather_results(blocks), after)
        back = []
        for a in range(2):
            returns = [(target, source) for source, target in spread_pairs(a)]
            back.append(lax.ppermute(mixed[256 * a : 256 * (a + 1)], ("z", "x", "core"), returns))
        return mixed, back

    mixed, early = go_back(2, part, last[:1])
    _, late = go_back(1, last, (mixed,))
    there = outward(1, 0, jnp.float32, info, early, w_out)
    here = outward(0, 0, jnp.float32, info, early, w_out)
    there = outward(1, 256, jnp.bfloat16, info, late, w_out, (there,), (here,))
    received = lax.ppermute(there, "core", swap)
    here = outward(0, 256, jnp.float32, info, late, w_out, (here,), (there,))
    return (here + received.astype(jnp.float32)).astype(jnp.bfloat16)


def solution(mesh):
    fine = Mesh(mesh.devices.reshape(4, 4, 4, 2), ("z", "y", "x", "core"))
    seq = ("z", "y", "x")
    in_specs = (P(seq, "core"), P(seq), P(None, None, "core"), P("core", None))
    return jax.shard_map(body, mesh=fine, in_specs=in_specs, out_specs=P(seq, "core"), check_vma=False)
```
